32 devices in a mesh: frames: 2 (over y), slab: 16 (over z, x, core).
Axes of the slice: x: 2, y: 2, z: 4, core: 2. Of those that a mesh axis runs over, the one named last changes fastest.
Arguments:
- raw_movie: bfloat16 [4, 1024, 128], P('frames', 'slab'), may hold values from -18 to 18
- shifts: int32 [2, 4, 32, 1], P(None, 'frames', 'slab'), may hold values from -3 to 3
- footprints: bfloat16 [512, 16, 16], P('slab'), may hold values from 0.049804688 to 1
- anchors: int32 [512, 2], P('slab'), may hold values from 0 to 1008, as said below
- block_of: int32 [512], P('slab'), may hold values from 0 to 3, as said below
- init_traces: float32 [512, 4], P('slab', 'frames'), may hold values from -6 to 6
Outputs:
- traces_z: float32 [512, 4], P('slab', 'frames')
- residual: float32 [4, 1024, 128], P('frames', 'slab')
The draws below stay inside these ranges and needn't reach their ends.
Inputs may be any that keep to these rules, and one draw needn't show every extreme that they name: `anchors`: the tile of a source owned by slab s (sources s * 32 to s * 32 + 31) has its top row in s * 64 - 16 // 2 to s * 64 + 64 - 16 // 2 - 1, moved into the grid where it would leave it; its left column lies in 0 to 112. `block_of`: among the 32 sources of one slab, each block number is held by at most 16 sources, and some block number by exactly 16.
All inputs are finite; a program needn't handle non-finite values.
Results may differ from the reference program's by a relative error of at most 0.003.
Values may be sent and summed in bfloat16 or wider, within the bound.
No kernel may reach another device: no remote copies, remote signals or barrier semaphores. Data moves between devices by JAX's collectives and lax.ppermute only.
A program may use at most 64 MiB of HBM per device.

```python
import jax
import jax.numpy as jnp
from jax import lax

ROWS = 64
COLS = 128
K_DEV = 32
TILE = 16
SHIFT = 3
PATCH_R = 32
PATCH_C = 128
BLOCKS = 4
SWEEPS = 3
FRAMES = 4
NROWS = 1024
SOURCES = 512
NPR = 32
NPC = 1
BMAX = 16


def draw_raw_movie(key, part):
    frame_ramp = 1.0 + 2.0 * jnp.arange(FRAMES, dtype=jnp.float32) / max(FRAMES - 1, 1)
    pattern = jnp.clip(jax.random.normal(key, (FRAMES, NROWS, COLS), jnp.float32), -6.0, 6.0)
    return (pattern * frame_ramp[:, None, None]).astype(jnp.bfloat16)


def draw_anchors(key, part):
    subkeys = jax.random.split(key, 2)
    owner_slab = jnp.arange(SOURCES, dtype=jnp.int32) // K_DEV
    row_anchor = owner_slab * ROWS - TILE // 2 + jax.random.randint(subkeys[0], (SOURCES,), 0, ROWS, dtype=jnp.int32)
    row_anchor = jnp.clip(row_anchor, 0, NROWS - TILE)
    col_anchor = jax.random.randint(subkeys[1], (SOURCES,), 0, COLS - TILE + 1, dtype=jnp.int32)
    return jnp.stack([row_anchor, col_anchor], axis=1).astype(jnp.int32)


def draw_block_of(key, part):
    subkeys = jax.random.split(key, 3)
    slab_total = SOURCES // K_DEV
    heavy = jax.random.randint(subkeys[0], (slab_total, 1), 0, BLOCKS, dtype=jnp.int32)
    orders = jax.vmap(lambda single_key: jax.random.permutation(single_key, K_DEV))(jax.random.split(subkeys[1], slab_total))
    others = (heavy + 1 + jax.random.randint(subkeys[2], (slab_total, K_DEV), 0, BLOCKS - 1, dtype=jnp.int32)) % BLOCKS
    forced = orders < BMAX
    return jnp.where(forced, heavy, others).reshape(SOURCES).astype(jnp.int32)


def with_ends(entries, rng, least, high):
    shape = entries.shape
    spot = [jax.random.randint(jax.random.fold_in(rng, axis), (), 0, shape[axis]) for axis in range(len(shape))]
    entries = entries.at[tuple(spot)].set(least)
    longest = shape.index(max(shape))
    spot[longest] = (spot[longest] + 1) % shape[longest]
    return entries.at[tuple(spot)].set(high)


def block_scale(rng, dims, shards, least, high):
    gain = 1.0
    for dim, parts in shards:
        draws = jax.random.uniform(jax.random.fold_in(jax.random.fold_in(rng, 6), dim), (parts,), jnp.float32, least / len(shards), high / len(shards))
        gain = gain * jnp.repeat(jnp.exp(draws), dims[dim] // parts).reshape((-1,) + (1,) * (len(dims) - 1 - dim))
    return gain


def normal_values(stream_key, dims, deviation, most, shards=(), kind=jnp.bfloat16):
    gain = block_scale(stream_key, dims, shards, -0.22, 0.18) if shards else 1.0
    entries = jax.random.normal(stream_key, dims, jnp.float32) * deviation * gain
    return jnp.minimum(jnp.maximum(entries, -most), most).astype(kind)


def setup_inputs(seed: int = 0) -> dict:
    key_list = jax.random.split(jax.random.key(seed), 7)
    raw_movie = draw_raw_movie(jax.random.fold_in(key_list[6], 71), 0)
    shifts = with_ends(jax.random.randint(key_list[1], (2, FRAMES, NPR, NPC), -SHIFT, SHIFT + 1), jax.random.fold_in(key_list[1], 1), -SHIFT, SHIFT).astype(jnp.int32)
    footprints = jnp.clip(0.049804688 + 0.9501953 * jax.random.uniform(key_list[2], (SOURCES, TILE, TILE), jnp.float32) ** block_scale(key_list[2], (SOURCES, TILE, TILE), ((0, 16),), -0.2, 0.2), 0.049804688, 1.0).astype(jnp.bfloat16)
    anchors = draw_anchors(jax.random.fold_in(key_list[6], 71), 0)
    block_of = draw_block_of(jax.random.fold_in(key_list[6], 71), 0)
    init_traces = normal_values(key_list[5], (SOURCES, FRAMES), 1.0, 6.0, ((0, 16), (1, 2)), jnp.float32)
    return {"raw_movie": raw_movie, "shifts": shifts, "footprints": footprints, "anchors": anchors, "block_of": block_of, "init_traces": init_traces}


WEIGHT_NEAR = 0.75
WEIGHT_FAR = 0.25
EPSILON = 1e-05

def warp_frame(padded, rows_shift, cols_shift):
    count_r, count_c = rows_shift.shape

    def one_patch(patch_row, patch_col, row_shift, col_shift):
        window = lax.dynamic_slice(padded, (SHIFT + 1 + patch_row * PATCH_R + row_shift, SHIFT + patch_col * PATCH_C + col_shift), (PATCH_R + 1, PATCH_C)).astype(jnp.float32)
        return WEIGHT_NEAR * window[:-1] + WEIGHT_FAR * window[1:]
    across = jax.vmap(one_patch, in_axes=(None, 0, 0, 0))
    layout = jax.vmap(across, in_axes=(0, None, 0, 0))(jnp.arange(count_r, dtype=jnp.int32), jnp.arange(count_c, dtype=jnp.int32), rows_shift, cols_shift)
    return layout.transpose(0, 2, 1, 3).reshape(count_r * PATCH_R, count_c * PATCH_C)

def reference(raw_movie, shifts, footprints, anchors, block_of, init_traces):
    padded = jnp.pad(raw_movie, ((0, 0), (SHIFT + 1, SHIFT + 1), (SHIFT, SHIFT)))
    corrected = jax.vmap(warp_frame)(padded, shifts[0], shifts[1]).astype(jnp.bfloat16)
    offsets = jnp.arange(TILE, dtype=jnp.int32)
    tile_rows = anchors[:, 0][:, None, None] + offsets[None, :, None]
    tile_cols = anchors[:, 1][:, None, None] + offsets[None, None, :]
    weights = footprints.astype(jnp.float32)
    norm_sq = lax.optimization_barrier(jnp.sum(weights * weights, axis=(1, 2)))
    block_masks = [block_of == block_idx for block_idx in range(BLOCKS)]

    def render(values):
        canvas = jnp.zeros((NROWS, COLS), jnp.float32)
        return canvas.at[tile_rows, tile_cols].add(weights * values[:, None, None])

    def solve_frame(inputs):
        frame_image, first_traces = inputs
        residual = frame_image.astype(jnp.float32) - render(first_traces)
        traces = first_traces
        for sweep_idx in range(SWEEPS):
            for block_idx in range(BLOCKS):
                projected = lax.optimization_barrier(jnp.sum(residual[tile_rows, tile_cols] * weights, axis=(1, 2)))
                change = jnp.where(block_masks[block_idx], projected / norm_sq, jnp.zeros_like(projected))
                traces = traces + change
                residual = residual - render(change)
        return (traces, residual)
    traces, residual = lax.map(solve_frame, (corrected, init_traces.T))
    traces = traces.T
    trace_mean = lax.optimization_barrier(jnp.mean(traces, axis=1, keepdims=True))
    square_mean = lax.optimization_barrier(jnp.mean(traces * traces, axis=1, keepdims=True))
    spread = square_mean - trace_mean * trace_mean
    traces_z = (traces - trace_mean) / jnp.sqrt(spread + EPSILON)
    return (traces_z, residual)
```

```python
import functools

import jax
import jax.numpy as jnp
from jax import lax
from jax.experimental import pallas as pl
from jax.experimental.pallas import tpu as pltpu
from jax.sharding import PartitionSpec as P

SHIFT = 3
PATCH_R = 32
BLOCKS = 4
SWEEPS = 3
TILE = 16
RIM = 8
LANES = 128
K = 32
GROUPS = LANES // K
WEIGHT_NEAR = 0.75
WEIGHT_FAR = 0.25
EPSILON = 1e-05
F32 = jnp.float32
BF16 = jnp.bfloat16

PK_RAW_LAST = 64
PK_RAW_FIRST = 96
PK_COL = 128
PK_ROW = 160
PK_ALL = 176


def iota(shape, axis):
    return lax.broadcasted_iota(jnp.int32, shape, axis)


def lane_pick(values, index):
    return jnp.take_along_axis(values, index, axis=1, mode="promise_in_bounds")


def placed_tiles(pack):
    col = pack[PK_COL : PK_COL + K, 0:1].astype(F32).astype(jnp.int32)
    offset = iota((K, LANES), 1) - col
    inside = (offset >= 0) & (offset < TILE)
    base = jnp.clip(offset, 0, TILE - 1)
    out = []
    for i in range(TILE):
        half, part = divmod(i, 8)
        tile = pack[half * K : (half + 1) * K].astype(F32)
        out.append(jnp.where(inside, lane_pick(tile, base + part * TILE), 0.0))
    return jnp.concatenate(out, axis=0).astype(BF16)


def dot_nt(a, b):
    return lax.dot_general(a, b, (((1,), (1,)), ((), ())), preferred_element_type=F32)


def fold_lanes(x):
    x = x + pltpu.roll(x, 64, 1)
    return x + pltpu.roll(x, 32, 1)


def gram(tiles_a, tiles_b, row_a, row_b):
    full = dot_nt(tiles_a, tiles_b)
    diff = row_a - row_b - (iota((K, LANES), 1) // K).astype(F32)
    total = jnp.zeros((K, LANES), F32)
    for q in range(-(TILE - 1), TILE):
        part = None
        for m in range(4):
            i = 4 * m - q
            if 0 <= i < TILE:
                block = full[i * K : (i + 1) * K, m * LANES : (m + 1) * LANES]
                part = block if part is None else part + block
        if part is not None:
            total = total + jnp.where(diff == float(q), part, 0.0)
    return fold_lanes(total)


def pack_blocks(mat):
    group = iota((8, LANES), 1) // K
    out = mat[0:8]
    for q in range(1, GROUPS):
        out = jnp.where(group == q, mat[8 * q : 8 * q + 8], out)
    return out


def project(corr, tiles, rel):
    part = dot_nt(corr, tiles)
    total = jnp.zeros(rel.shape, F32)
    for m in range(4):
        total = total + jnp.where(rel == float(4 * m), part[:, m * LANES : (m + 1) * LANES], 0.0)
    return fold_lanes(jnp.sum(total, axis=0, keepdims=True))


def prepare_kernel(shifts, up_shift, flags, own, up, raw, misc, out, t_own, t_up, corr_out, ext, corr):
    frames = raw.shape[0]
    rows = raw.shape[1]
    patches = rows // PATCH_R
    lane = iota((1, LANES), 1)
    zeros16 = jnp.zeros((16, LANES), F32)
    for t in range(frames):
        ext[t, 0:16] = up[PK_RAW_LAST + 16 * t : PK_RAW_LAST + 16 * t + 16].astype(F32)
        ext[t, 16 : 16 + rows] = raw[t].astype(F32)
        ext[t, 16 + rows : 32 + rows] = zeros16

    def warped(t, first, count, a, c):
        near = ext[t, pl.ds(16 + first + a, count)]
        far = ext[t, pl.ds(17 + first + a, count)]
        both = WEIGHT_NEAR * near + WEIGHT_FAR * far
        moved = pltpu.roll(both, lax.rem(LANES - c, LANES), 1)
        ok = (lane + c >= 0) & (lane + c < LANES)
        return jnp.where(ok, moved, 0.0)

    for t in range(frames):
        corr[t, 0:RIM] = warped(t, -RIM, RIM, up_shift[t], up_shift[frames + t])
        for p in range(patches):
            corr[t, RIM + p * PATCH_R : RIM + (p + 1) * PATCH_R] = warped(
                t, p * PATCH_R, PATCH_R, shifts[0, t, p], shifts[1, t, p]
            )
        corr_out[t] = corr[t, RIM : RIM + rows].astype(BF16)

    tiles_own = placed_tiles(own[...])
    tiles_up = placed_tiles(up[...])
    t_own[...] = tiles_own
    t_up[...] = tiles_up
    row_own = own[PK_ROW : PK_ROW + 1].astype(F32)
    row_up = up[PK_ROW : PK_ROW + 1].astype(F32) - float(rows)
    row_own_col = own[PK_COL : PK_COL + K, 1:2].astype(F32)
    row_up_col = up[PK_COL : PK_COL + K, 1:2].astype(F32) - float(rows)
    out[0:8] = pack_blocks(gram(tiles_own, tiles_own, row_own_col, row_own))
    out[8:16] = pack_blocks(gram(tiles_up, tiles_own, row_up_col, row_own))
    out[16:24] = pack_blocks(gram(tiles_own, tiles_up, row_own_col, row_up))

    ext_rows = rows + RIM
    y = iota((ext_rows, LANES), 0)
    group = (iota((ext_rows, LANES), 1) // K).astype(F32)
    keep = jnp.where((y < rows) | (flags[1] == 1), 1.0, 0.0)
    rel_own = y.astype(F32) - row_own - group
    rel_up = (y.astype(F32) - row_up - group)[0 : 2 * RIM]
    sub = iota((8, LANES), 0)
    group8 = iota((8, LANES), 1) // K
    rest = misc[...]
    for t in range(frames):
        image = corr[t]
        p_own = project((image * keep).astype(BF16), tiles_own, rel_own)
        p_up = project(image[0 : 2 * RIM].astype(BF16), tiles_up, rel_up)
        rest = jnp.where((sub == t) & (group8 == 0), p_own, rest)
        rest = jnp.where((sub == t) & (group8 == 1), p_up, rest)
    out[24:32] = rest


def regroup(arrays, group):
    a0, a1, a2, a3 = arrays
    odd = (group % 2) == 1

    def pair(x, y):
        return (
            jnp.where(odd, pltpu.roll(y, K, 1), x),
            jnp.where(odd, y, pltpu.roll(x, LANES - K, 1)),
        )

    b0, b1 = pair(a0, a1)
    b2, b3 = pair(a2, a3)
    high = group >= 2

    def pair2(x, y):
        return (
            jnp.where(high, pltpu.roll(y, 2 * K, 1), x),
            jnp.where(high, y, pltpu.roll(x, 2 * K, 1)),
        )

    c0, c2 = pair2(b0, b2)
    c1, c3 = pair2(b1, b3)
    return c0, c1, c2, c3


def sweep_kernel(frames, flags, gathered, out, g_ref, state_ref, traces_ref):
    slabs = gathered.shape[0]
    lines = slabs // GROUPS
    rows = frames * lines
    group8 = iota((8, LANES), 1) // K
    lane = iota((rows, LANES), 1)
    for line in range(lines):
        for kind in range(4):
            blocks = regroup(
                [gathered[GROUPS * line + g, 8 * kind : 8 * kind + 8] for g in range(GROUPS)], group8
            )
            for q in range(GROUPS):
                if kind < 3:
                    for t in range(frames):
                        first = (kind * K + 8 * q) * rows + t * lines + line
                        g_ref[pl.ds(first, 8, stride=rows), :] = blocks[q]
                else:
                    for t in range(frames):
                        state_ref[q, pl.ds(t * lines + line, 1), :] = blocks[q][t : t + 1]

    def from_next(x):
        turned = pltpu.roll(x, LANES - K, 1)
        return jnp.where(lane >= LANES - K, pltpu.roll(turned, rows - 1, 0), turned)

    def from_last(x):
        turned = pltpu.roll(x, K, 1)
        return jnp.where(lane < K, pltpu.roll(turned, 1, 0), turned)

    line_id = lax.rem(iota((rows, LANES), 0), lines)
    end = (line_id == lines - 1) & (lane >= LANES - K)
    for j in range(K):
        at = pl.ds((2 * K + j) * rows, rows)
        g_ref[at, :] = jnp.where(end, 0.0, from_next(g_ref[at, :]))

    start = (lane // K) * K
    norm = jnp.zeros((rows, LANES), F32)
    for j in range(K):
        norm = norm + jnp.where(lane - start == j, g_ref[pl.ds(j * rows, rows), :], 0.0)
    p = state_ref[0] + jnp.where(end, 0.0, from_next(state_ref[1]))
    traces = state_ref[2]
    block_of = state_ref[3]

    def coupled(change):
        sources = (change, from_last(change), from_next(change))
        totals = [jnp.zeros((rows, LANES), F32) for _ in range(6)]
        for j in range(K):
            index = start + j
            for kind in range(3):
                slot = kind * 2 + j % 2
                totals[slot] = totals[slot] + g_ref[pl.ds((kind * K + j) * rows, rows), :] * lane_pick(
                    sources[kind], index
                )
        return (totals[0] + totals[1]) + (totals[2] + totals[3]) + (totals[4] + totals[5])

    p = p - coupled(traces)

    def step(n, carry):
        p, traces = carry
        block = lax.rem(n, BLOCKS).astype(F32)
        change = jnp.where(block_of == block, p / norm, 0.0)
        return p - coupled(change), traces + change

    p, traces = lax.fori_loop(0, SWEEPS * BLOCKS, step, (p, traces))
    traces_ref[...] = traces
    slab = flags[0]
    out[...] = jnp.zeros((8, LANES), F32)
    for place, other in enumerate((slab, jnp.maximum(slab - 1, 0), jnp.minimum(slab + 1, slabs - 1))):
        for t in range(frames):
            row = traces_ref[pl.ds(t * lines + other // GROUPS, 1), :]
            row = pltpu.roll(row, lax.rem(LANES - K * lax.rem(other, GROUPS), LANES), 1)
            row = jnp.where(iota((1, LANES), 1) < K, row, 0.0)
            out[place * frames + t : place * frames + t + 1] = fold_lanes(row)


def render(rel, values, tiles):
    parts = []
    for m in range(4):
        parts.append(jnp.where(rel == float(4 * m), values, 0.0))
    mixed = jnp.concatenate(parts, axis=1)
    high = mixed.astype(BF16)
    low = (mixed - high.astype(F32)).astype(BF16)
    return jnp.dot(high, tiles, preferred_element_type=F32) + jnp.dot(
        low, tiles, preferred_element_type=F32
    )


def finish_kernel(shifts, own, up, low, raw, corr_in, t_own, t_up, values, out, ext):
    frames = raw.shape[0]
    rows = raw.shape[1]
    lane = iota((1, LANES), 1)
    tiles_low = placed_tiles(low[...])
    row_own = own[PK_ROW : PK_ROW + 1].astype(F32)
    row_up = up[PK_ROW : PK_ROW + 1].astype(F32) - float(rows)
    row_low = low[PK_ROW : PK_ROW + 1].astype(F32) + float(rows)
    y = (iota((rows, LANES), 0) + RIM).astype(F32)
    group = (iota((rows, LANES), 1) // K).astype(F32)
    last = rows // PATCH_R - 1
    for t in range(frames):
        ext[0:16] = raw[t, rows - 16 : rows].astype(F32)
        ext[16:32] = low[PK_RAW_FIRST + 16 * t : PK_RAW_FIRST + 16 * t + 16].astype(F32)
        a = shifts[0, t, last]
        c = shifts[1, t, last]
        both = WEIGHT_NEAR * ext[pl.ds(8 + a, 8)] + WEIGHT_FAR * ext[pl.ds(9 + a, 8)]
        moved = pltpu.roll(both, lax.rem(LANES - c, LANES), 1)
        ok = (lane + c >= 0) & (lane + c < LANES)
        tail = jnp.where(ok, moved, 0.0).astype(BF16).astype(F32)
        image = render(y - row_own - group, values[t : t + 1], t_own[...])
        rel_up = (y - row_up - group)[0:RIM]
        rel_low = (y - row_low - group)[rows - RIM : rows]
        top = render(rel_up, values[frames + t : frames + t + 1], t_up[...])
        bottom = render(rel_low, values[2 * frames + t : 2 * frames + t + 1], tiles_low)
        out[t, 0:RIM] = corr_in[t, 0:RIM].astype(F32) - image[0:RIM] - top
        out[t, RIM : rows - RIM] = corr_in[t, RIM : rows - RIM].astype(F32) - image[RIM : rows - RIM]
        out[t, rows - RIM : rows] = tail - image[rows - RIM : rows] - bottom


def shards(raw_movie, shifts, footprints, anchors, block_of, init_traces):
    frames, rows, cols = raw_movie.shape
    slab = lax.axis_index("slab")
    slabs = lax.axis_size("slab")
    frame_parts = lax.axis_size("frames")
    vmem = pl.BlockSpec(memory_space=pltpu.VMEM)
    smem = pl.BlockSpec(memory_space=pltpu.SMEM)

    row_rel = (anchors[:, 0] - (slab * rows - RIM)).astype(BF16)
    col = anchors[:, 1].astype(BF16)
    shifts3 = shifts[:, :, :, 0]
    columns = jnp.pad(jnp.stack([col, row_rel], axis=1), ((0, 0), (0, LANES - 2)))
    line0 = jnp.tile(row_rel, GROUPS)[None]
    line1 = jnp.pad(shifts3[:, :, -1].reshape(1, 2 * frames).astype(BF16), ((0, 0), (0, LANES - 2 * frames)))
    pack = jnp.concatenate(
        [
            footprints.reshape(K, 2, LANES).transpose(1, 0, 2).reshape(2 * K, LANES),
            raw_movie[:, rows - 16 :].reshape(frames * 16, cols),
            raw_movie[:, :16].reshape(frames * 16, cols),
            columns,
            line0,
            line1,
            jnp.zeros((14, LANES), BF16),
        ],
        axis=0,
    )
    up = lax.ppermute(pack, "slab", [(i, i + 1) for i in range(slabs - 1)])
    low = lax.ppermute(pack, "slab", [(i + 1, i) for i in range(slabs - 1)])

    up_shift = up[PK_ROW + 1, : 2 * frames].astype(jnp.int32)
    flags = jnp.stack([slab, (slab == slabs - 1).astype(jnp.int32)]).astype(jnp.int32)
    misc = jnp.concatenate(
        [
            jnp.zeros((frames, 2 * K), F32),
            init_traces.T,
            jnp.broadcast_to(block_of.astype(F32)[None], (frames, K)),
        ],
        axis=1,
    )
    misc = jnp.pad(misc, ((0, 8 - frames), (0, 0)))

    payload, t_own, t_up, corr = pl.pallas_call(
        prepare_kernel,
        out_shape=(
            jax.ShapeDtypeStruct((32, LANES), F32),
            jax.ShapeDtypeStruct((TILE * K, LANES), BF16),
            jax.ShapeDtypeStruct((TILE * K, LANES), BF16),
            jax.ShapeDtypeStruct((frames, rows, LANES), BF16),
        ),
        in_specs=[smem, smem, smem, vmem, vmem, vmem, vmem],
        out_specs=(vmem, vmem, vmem, vmem),
        scratch_shapes=[
            pltpu.VMEM((frames, rows + 32, LANES), F32),
            pltpu.VMEM((frames, rows + RIM, LANES), F32),
        ],
    )(shifts3, up_shift, flags, pack, up, raw_movie, misc)

    gathered = lax.all_to_all(jnp.broadcast_to(payload[None], (slabs, 32, LANES)), "slab", 0, 0)

    lines = slabs // GROUPS
    values = pl.pallas_call(
        functools.partial(sweep_kernel, frames),
        out_shape=jax.ShapeDtypeStruct((8, LANES), F32),
        in_specs=[smem, vmem],
        out_specs=vmem,
        scratch_shapes=[
            pltpu.VMEM((3 * K * frames * lines, LANES), F32),
            pltpu.VMEM((4, frames * lines, LANES), F32),
            pltpu.VMEM((frames * lines, LANES), F32),
        ],
    )(flags, gathered)

    traces = values[:frames, :K]
    total = jnp.sum(traces, axis=0)
    total_sq = jnp.sum(traces * traces, axis=0)
    sums = jnp.stack([total, total_sq])
    moments = sums
    for hop in range(1, frame_parts):
        moments = moments + lax.ppermute(
            sums, "frames", [(i, (i + hop) % frame_parts) for i in range(frame_parts)]
        )

    residual = pl.pallas_call(
        finish_kernel,
        out_shape=jax.ShapeDtypeStruct((frames, rows, LANES), F32),
        in_specs=[smem] + [vmem] * 8,
        out_specs=vmem,
        scratch_shapes=[pltpu.VMEM((32, LANES), F32)],
    )(shifts3, pack, up, low, raw_movie, corr, t_own, t_up, values)

    frame_total = frames * frame_parts
    trace_mean = moments[0] / frame_total
    spread = moments[1] / frame_total - trace_mean * trace_mean
    traces_z = (traces - trace_mean) / jnp.sqrt(spread + EPSILON)
    return traces_z.T, residual


def solution(mesh):
    in_specs = (
        P("frames", "slab", None),
        P(None, "frames", "slab", None),
        P("slab", None, None),
        P("slab", None),
        P("slab"),
        P("slab", "frames"),
    )
    out_specs = (P("slab", "frames"), P("frames", "slab", None))
    return jax.shard_map(shards, mesh=mesh, in_specs=in_specs, out_specs=out_specs, check_vma=False)
```

```python
import functools

import jax
import jax.numpy as jnp
from jax import lax
from jax.experimental import pallas as pl
from jax.experimental.pallas import tpu as pltpu
from jax.sharding import PartitionSpec as P

SHIFT = 3
PATCH_R = 32
BLOCKS = 4
SWEEPS = 3
TILE = 16
RIM = 8
LANES = 128
K = 32
GROUPS = LANES // K
WEIGHT_NEAR = 0.75
WEIGHT_FAR = 0.25
EPSILON = 1e-05
F32 = jnp.float32
BF16 = jnp.bfloat16

PK_RAW_LAST = 64
PK_RAW_FIRST = 96
PK_META = 128
PK_ALL = 144
META_ROW = 0
META_COL = 1
META_SHIFT = 2


def iota(shape, axis):
    return lax.broadcasted_iota(jnp.int32, shape, axis)


def lane_pick(values, index):
    return jnp.take_along_axis(values, index, axis=1, mode="promise_in_bounds")


def as_column(line):
    own = iota((K, LANES), 0) == iota((K, LANES), 1)
    return jnp.sum(jnp.where(own, line, 0.0), axis=1, keepdims=True)


def placed_tiles(tiles, col_line):
    col = as_column(col_line).astype(jnp.int32)
    offset = iota((K, LANES), 1) - col
    inside = (offset >= 0) & (offset < TILE)
    base = jnp.clip(offset, 0, TILE - 1)
    out = []
    for i in range(TILE):
        half, part = divmod(i, 8)
        tile = tiles[half * K : (half + 1) * K].astype(F32)
        out.append(jnp.where(inside, lane_pick(tile, base + part * TILE), 0.0))
    return jnp.concatenate(out, axis=0).astype(BF16)


def dot_nt(a, b):
    return lax.dot_general(a, b, (((1,), (1,)), ((), ())), preferred_element_type=F32)


def fold_lanes(x):
    x = x + pltpu.roll(x, 64, 1)
    return x + pltpu.roll(x, 32, 1)


def gram(tiles_a, tiles_b, row_a, row_b):
    full = dot_nt(tiles_a, tiles_b)
    diff = row_a - row_b - (iota((K, LANES), 1) // K).astype(F32)
    total = jnp.zeros((K, LANES), F32)
    for q in range(-(TILE - 1), TILE):
        part = None
        for m in range(4):
            i = 4 * m - q
            if 0 <= i < TILE:
                block = full[i * K : (i + 1) * K, m * LANES : (m + 1) * LANES]
                part = block if part is None else part + block
        if part is not None:
            total = total + jnp.where(diff == float(q), part, 0.0)
    return fold_lanes(total)


def project(corr, tiles, rel):
    part = dot_nt(corr, tiles)
    total = jnp.zeros(rel.shape, F32)
    for m in range(4):
        total = total + jnp.where(rel == float(4 * m), part[:, m * LANES : (m + 1) * LANES], 0.0)
    return fold_lanes(jnp.sum(total, axis=0, keepdims=True))


def pack_kernel(shifts, raw, tiles, anchors, out):
    frames, rows, _ = raw.shape
    last = rows // PATCH_R - 1
    base = lax.axis_index("slab") * rows - RIM
    for half in range(2):
        part = tiles[8 * half : 8 * half + 8].astype(F32).reshape(LANES, K)
        out[K * half : K * half + K] = part.T.astype(BF16)
    for t in range(frames):
        out[PK_RAW_LAST + 16 * t : PK_RAW_LAST + 16 * t + 16] = raw[t, rows - 16 : rows]
        out[PK_RAW_FIRST + 16 * t : PK_RAW_FIRST + 16 * t + 16] = raw[t, 0:16]
    places = anchors[...].astype(F32)
    places = jnp.concatenate([places] * GROUPS, axis=1)
    sub = iota((16, LANES), 0)
    meta = jnp.where(sub == META_COL, places[1:2], 0.0)
    meta = jnp.where(sub == META_ROW, places[0:1] - base.astype(F32), meta)
    for t in range(frames):
        for axis in range(2):
            value = shifts[axis, t, 0, last].astype(F32)
            meta = jnp.where(sub == META_SHIFT + axis * frames + t, value, meta)
    out[PK_META:PK_ALL] = meta.astype(BF16)


def write_tile(out, first, mat, rows):
    lane = iota((K, LANES), 1)
    own = lane // 8 == iota((K, LANES), 0) % 16
    for lq in range(4):
        part = jnp.where(own, lane_pick(mat, 8 * lq + lane % 8), 0.0)
        for jh in range(2):
            if 2 * lq + jh in rows:
                out[first + 2 * lq + jh : first + 2 * lq + jh + 1] = jnp.sum(
                    part[16 * jh : 16 * jh + 16], axis=0, keepdims=True
                )


def prepare_kernel(shifts, own, up, raw, init, block_of, out, t_own, t_up, corr_out, ext, corr, tile):
    frames, rows, _ = raw.shape
    patches = rows // PATCH_R
    is_last = lax.axis_index("slab") == lax.axis_size("slab") - 1
    lane = iota((1, LANES), 1)
    for t in range(frames):
        ext[t, 0:16] = up[PK_RAW_LAST + 16 * t : PK_RAW_LAST + 16 * t + 16].astype(F32)
        ext[t, 16 : 16 + rows] = raw[t].astype(F32)
        ext[t, 16 + rows : 32 + rows] = jnp.zeros((16, LANES), F32)
    meta_own = own[PK_META:PK_ALL].astype(F32)
    meta_up = up[PK_META:PK_ALL].astype(F32)

    for t in range(frames):
        a_up = meta_up[META_SHIFT + t : META_SHIFT + t + 1]
        c_up = meta_up[META_SHIFT + frames + t : META_SHIFT + frames + t + 1].astype(jnp.int32)
        both = jnp.zeros((RIM, LANES), F32)
        for a in range(-SHIFT, SHIFT + 1):
            near = ext[t, 8 + a : 16 + a]
            far = ext[t, 9 + a : 17 + a]
            both = jnp.where(a_up == float(a), WEIGHT_NEAR * near + WEIGHT_FAR * far, both)
        from_lane = iota((RIM, LANES), 1) + c_up
        moved = lane_pick(both, jnp.clip(from_lane, 0, LANES - 1))
        corr[t, 0:RIM] = jnp.where((from_lane >= 0) & (from_lane < LANES), moved, 0.0)
        for p in range(patches):
            a = shifts[0, t, 0, p]
            c = shifts[1, t, 0, p]
            near = ext[t, pl.ds(16 + p * PATCH_R + a, PATCH_R)]
            far = ext[t, pl.ds(17 + p * PATCH_R + a, PATCH_R)]
            both = WEIGHT_NEAR * near + WEIGHT_FAR * far
            moved = pltpu.roll(both, lax.rem(LANES - c, LANES), 1)
            ok = (lane + c >= 0) & (lane + c < LANES)
            corr[t, RIM + p * PATCH_R : RIM + (p + 1) * PATCH_R] = jnp.where(ok, moved, 0.0)
        corr_out[t] = corr[t, RIM : RIM + rows].astype(BF16)

    row_own = meta_own[META_ROW : META_ROW + 1]
    row_up = meta_up[META_ROW : META_ROW + 1] - float(rows)
    tiles_own = placed_tiles(own[0 : 2 * K], meta_own[META_COL : META_COL + 1])
    tiles_up = placed_tiles(up[0 : 2 * K], meta_up[META_COL : META_COL + 1])
    t_own[...] = tiles_own
    t_up[...] = tiles_up
    write_tile(tile, 0, gram(tiles_own, tiles_own, as_column(row_own), row_own), (0, 2, 4, 5, 6, 7))
    write_tile(tile, 8, gram(tiles_up, tiles_own, as_column(row_up), row_own), range(8))

    ext_rows = rows + RIM
    y = iota((ext_rows, LANES), 0)
    group = (iota((ext_rows, LANES), 1) // K).astype(F32)
    keep = jnp.where((y < rows) | is_last, 1.0, 0.0)
    rel_own = y.astype(F32) - row_own - group
    rel_up = (y.astype(F32) - row_up - group)[0 : 2 * RIM]
    place = iota((8, LANES), 1)
    source = 8 * ((place // 16) % 4) + place % 8
    frame = (place // 8) % 2
    first_kind = place < LANES // 2
    line1 = jnp.zeros((8, LANES), F32)
    line3 = jnp.zeros((8, LANES), F32)
    inits = jnp.concatenate([init[...]] * GROUPS, axis=1)
    blocks = jnp.concatenate([block_of[...].astype(F32)] * GROUPS, axis=1)

    def spread_out(line):
        return lane_pick(jnp.broadcast_to(line, (8, LANES)), source)

    for t in range(frames):
        image = corr[t]
        p_own = project((image * keep).astype(BF16), tiles_own, rel_own)
        p_up = project(image[0 : 2 * RIM].astype(BF16), tiles_up, rel_up)
        line1 = jnp.where(frame == t, jnp.where(first_kind, spread_out(p_own), spread_out(p_up)), line1)
        line3 = jnp.where(
            frame == t, jnp.where(first_kind, spread_out(inits[t : t + 1]), spread_out(blocks)), line3
        )
    tile[1:2] = line1[0:1]
    tile[3:4] = line3[0:1]
    whole = tile[...]
    for s in range(out.shape[0] // 16):
        out[16 * s : 16 * s + 16] = whole


def sweep_kernel(frames, slabs, gathered, out, turned, g_ref):
    per = K // slabs
    lane = iota((8, LANES), 1)
    sub = iota((8, LANES), 0)
    quarter = lane // K
    slab = lane % slabs
    frame = (lane % K) // slabs

    def turn(tile):
        arrays = []
        for n in range(2 // per):
            lines = []
            for lq in range(4):
                for h in range(per):
                    jh = n * per + h
                    lines.append(gathered[pl.ds(8 * tile + 2 * lq + jh, slabs, stride=16), :])
            at = (2 * tile + n) * LANES
            turned[at : at + LANES] = jnp.concatenate(lines, axis=0).T
            arrays.append(at)
        return (arrays * 2)[:2] if per == 2 else arrays

    def half_lane(jh):
        return jh * slabs if per == 2 else 0

    base_g = turn(0)
    base_x = turn(1)

    for jh in range(2):
        index = quarter * K + half_lane(jh) + slab
        for j in range(16):
            n = 16 * jh + j
            rows = turned[base_x[jh] + 8 * j : base_x[jh] + 8 * j + 8]
            g_ref[8 * (K + n) : 8 * (K + n) + 8] = lane_pick(rows, index)
            rows = turned[base_g[jh] + 8 * j : base_g[jh] + 8 * j + 8]
            g_ref[8 * n : 8 * n + 8] = lane_pick(rows, index)
    for r in range(8):
        parts = [turned[pl.ds(base_g[0] + 64 * v + r, 8, stride=8), :] for v in range(2)]
        for oq in (2, 3):
            n = 8 * oq + r
            index = oq * K + half_lane(0) + slab
            corner = jnp.where(quarter == 0, lane_pick(parts[0], index), lane_pick(parts[1], index))
            at = pl.ds(8 * n, 8)
            g_ref[at, :] = jnp.where(quarter < 2, corner, g_ref[at, :])
    later = jnp.minimum(slab + 1, slabs - 1)
    inner = slab < slabs - 1
    for r in range(8):
        parts = [
            [turned[pl.ds(base_x[uh] + 64 * v + r, 8, stride=8), :] for v in range(2)]
            for uh in range(3 - per)
        ]
        for oq in range(4):
            if per == 2:
                index = oq * K + (quarter // 2) * slabs + later
                value = jnp.where(
                    quarter % 2 == 0, lane_pick(parts[0][0], index), lane_pick(parts[0][1], index)
                )
            else:
                index = oq * K + later
                value = lane_pick(parts[0][0], index)
                for uq in range(1, 4):
                    value = jnp.where(quarter == uq, lane_pick(parts[uq // 2][uq % 2], index), value)
            n = 2 * K + 8 * oq + r
            g_ref[8 * n : 8 * n + 8] = jnp.where(inner, value, 0.0)

    lanes_of = half_lane(1)
    states = []
    for nv in range(frames // per):
        found = []
        for line, kind, shifted in ((0, 0, False), (0, 1, True), (1, 0, False), (1, 1, False)):
            index = line * K + lanes_of + (later if shifted else slab)
            value = jnp.zeros((8, LANES), F32)
            for lq in range(4):
                for h in range(per):
                    n = 8 * kind + 2 * lq + nv * per + h
                    rows = turned[base_g[1] + 8 * n : base_g[1] + 8 * n + 8]
                    value = jnp.where((quarter == lq) & (frame == h), lane_pick(rows, index), value)
            found.append(jnp.where(inner, value, 0.0) if shifted else value)
        states.append(found)
    norm = jnp.zeros((8, LANES), F32)
    for n in range(K):
        mine = (sub == n % 8) & (quarter == n // 8)
        norm = jnp.where(mine, g_ref[8 * n : 8 * n + 8], norm)
    inverse = 1.0 / norm
    block_of = states[0][3]
    inverses = [jnp.where(block_of == float(b), inverse, 0.0) for b in range(BLOCKS)]

    local = lane % K
    before = jnp.where(slab == 0, local, local - 1)
    after = jnp.where(inner, local + 1, local)

    def coupled(change):
        totals = [None] * 6
        for kind, place in enumerate((local, before, after)):
            for q in range(4):
                picked = lane_pick(change, q * K + place)
                for r in range(8):
                    n = kind * K + 8 * q + r
                    term = g_ref[8 * n : 8 * n + 8] * jnp.broadcast_to(picked[r : r + 1], (8, LANES))
                    slot = 2 * kind + r % 2
                    totals[slot] = term if totals[slot] is None else totals[slot] + term
        return (totals[0] + totals[1]) + ((totals[2] + totals[3]) + (totals[4] + totals[5]))

    p = [s[0] + s[1] - coupled(s[2]) for s in states]
    traces = [s[2] for s in states]

    def sweep(_, carry):
        p, traces = carry
        for b in range(BLOCKS):
            change = [x * inverses[b] for x in p]
            traces = [x + c for x, c in zip(traces, change)]
            p = [x - coupled(c) for x, c in zip(p, change)]
        return p, traces

    p, traces = lax.fori_loop(0, SWEEPS, sweep, (p, traces))

    me = lax.axis_index("slab")
    mine = sub == lane % 8
    lines = []
    for other in (me, jnp.maximum(me - 1, 0), jnp.minimum(me + 1, slabs - 1)):
        for t in range(frames):
            index = ((lane % K) // 8) * K + (t % per) * slabs + other
            value = jnp.where(mine, lane_pick(traces[t // per], index), 0.0)
            lines.append(jnp.sum(value, axis=0, keepdims=True))
    own = lines[:frames]
    lines.append(functools.reduce(jnp.add, own))
    lines.append(functools.reduce(jnp.add, [x * x for x in own]))
    for n, line in enumerate(lines):
        out[n : n + 1] = line


def render(rel, values, tiles):
    parts = []
    for m in range(4):
        parts.append(jnp.where(rel == float(4 * m), values, 0.0))
    mixed = jnp.concatenate(parts, axis=1)
    high = mixed.astype(BF16)
    low = (mixed - high.astype(F32)).astype(BF16)
    return jnp.dot(high, tiles, preferred_element_type=F32) + jnp.dot(
        low, tiles, preferred_element_type=F32
    )


def finish_kernel(shifts, own, up, low, raw, corr_in, t_own, t_up, values, out, ext):
    frames, rows, _ = raw.shape
    lane = iota((1, LANES), 1)
    meta_low = low[PK_META:PK_ALL].astype(F32)
    tiles_low = placed_tiles(low[0 : 2 * K], meta_low[META_COL : META_COL + 1])
    row_own = own[PK_META:PK_ALL].astype(F32)[META_ROW : META_ROW + 1]
    row_up = up[PK_META:PK_ALL].astype(F32)[META_ROW : META_ROW + 1] - float(rows)
    row_low = meta_low[META_ROW : META_ROW + 1] + float(rows)
    y = (iota((rows, LANES), 0) + RIM).astype(F32)
    group = (iota((rows, LANES), 1) // K).astype(F32)
    last = rows // PATCH_R - 1
    for t in range(frames):
        ext[0:16] = raw[t, rows - 16 : rows].astype(F32)
        ext[16:32] = low[PK_RAW_FIRST + 16 * t : PK_RAW_FIRST + 16 * t + 16].astype(F32)
        a = shifts[0, t, 0, last]
        c = shifts[1, t, 0, last]
        both = WEIGHT_NEAR * ext[pl.ds(8 + a, 8)] + WEIGHT_FAR * ext[pl.ds(9 + a, 8)]
        moved = pltpu.roll(both, lax.rem(LANES - c, LANES), 1)
        ok = (lane + c >= 0) & (lane + c < LANES)
        tail = jnp.where(ok, moved, 0.0).astype(BF16).astype(F32)
        image = render(y - row_own - group, values[t : t + 1], t_own[...])
        rel_up = (y - row_up - group)[0:RIM]
        rel_low = (y - row_low - group)[rows - RIM : rows]
        top = render(rel_up, values[frames + t : frames + t + 1], t_up[...])
        bottom = render(rel_low, values[2 * frames + t : 2 * frames + t + 1], tiles_low)
        out[t, 0:RIM] = corr_in[t, 0:RIM].astype(F32) - image[0:RIM] - top
        out[t, RIM : rows - RIM] = corr_in[t, RIM : rows - RIM].astype(F32) - image[RIM : rows - RIM]
        out[t, rows - RIM : rows] = tail - image[rows - RIM : rows] - bottom


def shards(raw_movie, shifts, footprints, anchors, block_of, init_traces):
    frames, rows, cols = raw_movie.shape
    slabs = lax.axis_size("slab")
    frame_parts = lax.axis_size("frames")
    vmem = pl.BlockSpec(memory_space=pltpu.VMEM)
    smem = pl.BlockSpec(memory_space=pltpu.SMEM)
    shifts = shifts.transpose(0, 1, 3, 2)

    pack = pl.pallas_call(
        pack_kernel,
        out_shape=jax.ShapeDtypeStruct((PK_ALL, LANES), BF16),
        in_specs=[smem, vmem, vmem, vmem],
        out_specs=vmem,
    )(shifts, raw_movie, footprints.transpose(1, 2, 0), anchors.T)
    up = lax.ppermute(pack, "slab", [(i, i + 1) for i in range(slabs - 1)])
    low = lax.ppermute(pack, "slab", [(i + 1, i) for i in range(slabs - 1)])

    payload, t_own, t_up, corr = pl.pallas_call(
        prepare_kernel,
        out_shape=(
            jax.ShapeDtypeStruct((slabs * 16, LANES), F32),
            jax.ShapeDtypeStruct((TILE * K, LANES), BF16),
            jax.ShapeDtypeStruct((TILE * K, LANES), BF16),
            jax.ShapeDtypeStruct((frames, rows, LANES), BF16),
        ),
        in_specs=[smem, vmem, vmem, vmem, vmem, vmem],
        out_specs=(vmem, vmem, vmem, vmem),
        scratch_shapes=[
            pltpu.VMEM((frames, rows + 32, LANES), F32),
            pltpu.VMEM((frames, rows + RIM, LANES), F32),
            pltpu.VMEM((16, LANES), F32),
        ],
    )(shifts, pack, up, raw_movie, init_traces.T, block_of[None])

    gathered = lax.all_to_all(payload.reshape(slabs, 16, LANES), "slab", 0, 0).reshape(slabs * 16, LANES)

    values = pl.pallas_call(
        functools.partial(sweep_kernel, frames, slabs),
        out_shape=jax.ShapeDtypeStruct((8, LANES), F32),
        in_specs=[vmem],
        out_specs=vmem,
        scratch_shapes=[pltpu.VMEM((4 * LANES, LANES), F32), pltpu.VMEM((8 * 3 * K, LANES), F32)],
    )(gathered)

    moments = values[3 * frames : 3 * frames + 2, :K]
    for hop in range(1, frame_parts):
        other = lax.ppermute(
            values, "frames", [(i, (i + hop) % frame_parts) for i in range(frame_parts)]
        )
        moments = moments + other[3 * frames : 3 * frames + 2, :K]

    residual = pl.pallas_call(
        finish_kernel,
        out_shape=jax.ShapeDtypeStruct((frames, rows, LANES), F32),
        in_specs=[smem] + [vmem] * 8,
        out_specs=vmem,
        scratch_shapes=[pltpu.VMEM((32, LANES), F32)],
    )(shifts, pack, up, low, raw_movie, corr, t_own, t_up, values)

    frame_total = frames * frame_parts
    trace_mean = moments[0] / frame_total
    spread = moments[1] / frame_total - trace_mean * trace_mean
    traces_z = (values[:frames, :K] - trace_mean) / jnp.sqrt(spread + EPSILON)
    return traces_z.T, residual


def solution(mesh):
    in_specs = (
        P("frames", "slab", None),
        P(None, "frames", "slab", None),
        P("slab", None, None),
        P("slab", None),
        P("slab"),
        P("slab", "frames"),
    )
    out_specs = (P("slab", "frames"), P("frames", "slab", None))
    return jax.shard_map(shards, mesh=mesh, in_specs=in_specs, out_specs=out_specs, check_vma=False)
```

```python
import functools

import jax
import jax.numpy as jnp
from jax import lax
from jax.experimental import pallas as pl
from jax.experimental.pallas import tpu as pltpu
from jax.sharding import PartitionSpec as P

SHIFT = 3
PATCH_R = 32
BLOCKS = 4
SWEEPS = 3
TILE = 16
RIM = 8
LANES = 128
K = 32
GROUPS = LANES // K
WEIGHT_NEAR = 0.75
WEIGHT_FAR = 0.25
EPSILON = 1e-05
F32 = jnp.float32
BF16 = jnp.bfloat16

PK_RAW_LAST = 64
PK_RAW_FIRST = 96
PK_META = 128
PK_ALL = 144
META_ROW = 0
META_COL = 1
META_SHIFT = 2
META_FIRST = 6
VMEM_BYTES = 8 << 20
VMEM_SPEC = pl.BlockSpec(memory_space=pltpu.VMEM)
SMEM_SPEC = pl.BlockSpec(memory_space=pltpu.SMEM)


def iota(shape, axis):
    return lax.broadcasted_iota(jnp.int32, shape, axis)


def lane_pick(values, index):
    return jnp.take_along_axis(values, index, axis=1, mode="promise_in_bounds")


def as_column(line):
    own = iota((K, LANES), 0) == iota((K, LANES), 1)
    return jnp.sum(jnp.where(own, line, 0.0), axis=1, keepdims=True)


def placed_tiles(tiles, col_line):
    col = as_column(col_line).astype(jnp.int32)
    offset = iota((K, LANES), 1) - col
    inside = (offset >= 0) & (offset < TILE)
    base = jnp.clip(offset, 0, TILE - 1)
    out = []
    for i in range(TILE):
        half, part = divmod(i, 8)
        tile = tiles[half * K : (half + 1) * K].astype(F32)
        out.append(jnp.where(inside, lane_pick(tile, base + part * TILE), 0.0))
    return jnp.concatenate(out, axis=0).astype(BF16)


def dot_nt(a, b):
    return lax.dot_general(a, b, (((1,), (1,)), ((), ())), preferred_element_type=F32)


def fold_lanes(x):
    x = x + pltpu.roll(x, 64, 1)
    return x + pltpu.roll(x, 32, 1)


def gram(tiles_a, tiles_b, row_a, row_b):
    full = dot_nt(tiles_a, tiles_b)
    diff = row_a - row_b - (iota((K, LANES), 1) // K).astype(F32)
    total = jnp.zeros((K, LANES), F32)
    for q in range(-(TILE - 1), TILE):
        part = None
        for m in range(4):
            i = 4 * m - q
            if 0 <= i < TILE:
                block = full[i * K : (i + 1) * K, m * LANES : (m + 1) * LANES]
                part = block if part is None else part + block
        if part is not None:
            total = total + jnp.where(diff == float(q), part, 0.0)
    return fold_lanes(total)


def project(corr, tiles, rel):
    part = dot_nt(corr, tiles)
    total = jnp.zeros(rel.shape, F32)
    for m in range(4):
        total = total + jnp.where(rel == float(4 * m), part[:, m * LANES : (m + 1) * LANES], 0.0)
    return fold_lanes(jnp.sum(total, axis=0, keepdims=True))


def neighbour_routes(slabs):
    pairs = [(i, i ^ 1) for i in range(slabs)]
    ends = [(0, 1), (1, 2), (2, 0), (slabs - 3, slabs - 2), (slabs - 2, slabs - 1), (slabs - 1, slabs - 3)]
    middle = [p for i in range(3, slabs - 4, 2) for p in ((i, i + 1), (i + 1, i))]
    crossed = [(i, i ^ 3) for i in range(slabs)]
    return pairs, ends + middle, crossed


def from_above(slab, by_pair, by_middle):
    found = jnp.where(slab % 2 == 1, by_pair.astype(F32), by_middle.astype(F32))
    return jnp.where(slab == 0, 0.0, found)


def from_below(slab, slabs, by_pair, by_middle, by_cross):
    odd = jnp.where((slab == 1) | (slab == slabs - 3), by_cross.astype(F32), by_middle.astype(F32))
    found = jnp.where(slab % 2 == 0, by_pair.astype(F32), odd)
    return jnp.where(slab == slabs - 1, 0.0, found)


def gather_masks(slabs):
    bits = slabs.bit_length() - 1
    return [(1 << (bits - 1 - r)) | 1 for r in range(bits - 1)] + [1]


def gather_place(diff, slabs):
    bits = slabs.bit_length() - 1
    odd = diff & 1
    place = jnp.zeros_like(diff)
    for r in range(bits - 1):
        bit = (diff >> (bits - 1 - r)) & 1
        place = place + bit * (1 << r)
        odd = odd ^ bit
    return place + odd * (1 << (bits - 1))


def pack_kernel(shifts, raw, tiles, anchors, out):
    frames, rows, _ = raw.shape
    last = rows // PATCH_R - 1
    base = lax.axis_index("slab") * rows - RIM
    for half in range(2):
        part = tiles[8 * half : 8 * half + 8].astype(F32).reshape(LANES, K)
        out[K * half : K * half + K] = part.T.astype(BF16)
    for t in range(frames):
        out[PK_RAW_LAST + 16 * t : PK_RAW_LAST + 16 * t + 16] = raw[t, rows - 16 : rows]
        out[PK_RAW_FIRST + 16 * t : PK_RAW_FIRST + 16 * t + 16] = raw[t, 0:16]
    places = anchors[...].astype(F32)
    places = jnp.concatenate([places] * GROUPS, axis=1)
    sub = iota((16, LANES), 0)
    meta = jnp.where(sub == META_COL, places[1:2], 0.0)
    meta = jnp.where(sub == META_ROW, places[0:1] - base.astype(F32), meta)
    for t in range(frames):
        for axis in range(2):
            for place, patch in ((META_SHIFT, last), (META_FIRST, 0)):
                value = shifts[axis, t, 0, patch].astype(F32)
                meta = jnp.where(sub == place + axis * frames + t, value, meta)
    out[PK_META:PK_ALL] = meta.astype(BF16)


def write_tile(out, first, mat, rows):
    lane = iota((K, LANES), 1)
    own = lane // 8 == iota((K, LANES), 0) % 16
    for lq in range(4):
        part = jnp.where(own, lane_pick(mat, 8 * lq + lane % 8), 0.0)
        for jh in range(2):
            if 2 * lq + jh in rows:
                out[first + 2 * lq + jh : first + 2 * lq + jh + 1] = jnp.sum(
                    part[16 * jh : 16 * jh + 16], axis=0, keepdims=True
                )


def warp(near_far, c):
    near, far = near_far
    both = WEIGHT_NEAR * near + WEIGHT_FAR * far
    moved = pltpu.roll(both, lax.rem(LANES - c, LANES), 1)
    place = iota((1, LANES), 1) + c
    return jnp.where((place >= 0) & (place < LANES), moved, 0.0)


def warp_by_lines(slices, a_line, c_line):
    both = jnp.zeros((RIM, LANES), F32)
    for a in range(-SHIFT, SHIFT + 1):
        near, far = slices(a)
        both = jnp.where(a_line == float(a), WEIGHT_NEAR * near + WEIGHT_FAR * far, both)
    place = iota((RIM, LANES), 1) + c_line.astype(jnp.int32)
    moved = lane_pick(both, jnp.clip(place, 0, LANES - 1))
    return jnp.where((place >= 0) & (place < LANES), moved, 0.0)


def own_kernel(shifts, own, raw, tile, part, t_own, corr, ext):
    frames, rows, _ = raw.shape
    slab = lax.axis_index("slab")
    is_last = slab == lax.axis_size("slab") - 1
    meta = own[PK_META:PK_ALL].astype(F32)
    row = meta[META_ROW : META_ROW + 1]
    tiles = placed_tiles(own[0 : 2 * K], meta[META_COL : META_COL + 1])
    t_own[...] = tiles
    tile[...] = jnp.zeros((8, LANES), F32)
    part[...] = jnp.zeros((8, LANES), F32)
    write_tile(tile, 0, gram(tiles, tiles, as_column(row), row), (0, 2, 4, 5, 6, 7))
    y = iota((rows, LANES), 0)
    keep = (y >= RIM) & ((y < rows - RIM) | is_last)
    rel = (y + RIM).astype(F32) - row - (iota((rows, LANES), 1) // K).astype(F32)
    for t in range(frames):
        ext[0:16] = jnp.zeros((16, LANES), F32)
        ext[16 : 16 + rows] = raw[t].astype(F32)
        ext[16 + rows : 32 + rows] = jnp.zeros((16, LANES), F32)
        parts = []
        for p in range(rows // PATCH_R):
            first = 16 + p * PATCH_R + shifts[0, t, 0, p]
            pair = ext[pl.ds(first, PATCH_R)], ext[pl.ds(first + 1, PATCH_R)]
            parts.append(warp(pair, shifts[1, t, 0, p]))
        image = jnp.concatenate(parts, axis=0)
        corr[t] = image.astype(BF16)
        part[t : t + 1] = project(jnp.where(keep, image, 0.0).astype(BF16), tiles, rel)


def edge_kernel(own, by_pair, by_middle, raw, init, block_of, t_own, tile, part, out, t_up, top):
    frames, rows, _ = raw.shape
    up = from_above(lax.axis_index("slab"), by_pair[...], by_middle[...])
    meta_own = own[PK_META:PK_ALL].astype(F32)
    meta_up = up[PK_META:PK_ALL]
    row_own = meta_own[META_ROW : META_ROW + 1]
    row_up = meta_up[META_ROW : META_ROW + 1] - float(rows)
    tiles_own = t_own[...]
    tiles_up = placed_tiles(up[0 : 2 * K], meta_up[META_COL : META_COL + 1])
    t_up[...] = tiles_up
    out[0:8] = tile[...]
    write_tile(out, 8, gram(tiles_up, tiles_own, as_column(row_up), row_own), range(8))

    place = iota((8, LANES), 1)
    source = 8 * ((place // 16) % 4) + place % 8
    frame = (place // 8) % 2
    first_kind = place < LANES // 2
    line1 = jnp.zeros((8, LANES), F32)
    line3 = jnp.zeros((8, LANES), F32)
    inits = jnp.concatenate([init[...]] * GROUPS, axis=1)
    blocks = jnp.concatenate([block_of[...].astype(F32)] * GROUPS, axis=1)

    def spread_out(line):
        return lane_pick(jnp.broadcast_to(line, (8, LANES)), source)

    shape = (2 * RIM, LANES)
    rel_own = iota(shape, 0).astype(F32) - row_own - (iota(shape, 1) // K).astype(F32)
    rel_up = iota(shape, 0).astype(F32) - row_up - (iota(shape, 1) // K).astype(F32)
    for t in range(frames):
        at = PK_RAW_LAST + 16 * t
        rows_near = jnp.concatenate([up[at : at + 16], raw[t, 0:16].astype(F32)], axis=0)

        def slices(first):
            return lambda a: (rows_near[first + a : first + a + RIM], rows_near[first + a + 1 : first + a + 1 + RIM])

        zone = []
        for first, meta, row in ((8, meta_up, META_SHIFT), (16, meta_own, META_FIRST)):
            a_line = meta[row + t : row + t + 1]
            c_line = meta[row + frames + t : row + frames + t + 1]
            zone.append(warp_by_lines(slices(first), a_line, c_line))
        image = jnp.concatenate(zone, axis=0).astype(BF16)
        top[t] = zone[1]
        p_own = project(image, tiles_own, rel_own) + part[t : t + 1]
        p_up = project(image, tiles_up, rel_up)
        line1 = jnp.where(frame == t, jnp.where(first_kind, spread_out(p_own), spread_out(p_up)), line1)
        line3 = jnp.where(
            frame == t, jnp.where(first_kind, spread_out(inits[t : t + 1]), spread_out(blocks)), line3
        )
    out[1:2] = line1[0:1]
    out[3:4] = line3[0:1]


def sweep_kernel(frames, slabs, gathered, out, turned, g_ref):
    per = K // slabs
    lane = iota((8, LANES), 1)
    sub = iota((8, LANES), 0)
    quarter = lane // K
    slab = lane % slabs
    frame = (lane % K) // slabs
    me = lax.axis_index("slab")
    later = jnp.minimum(slab + 1, slabs - 1)
    here = gather_place(slab ^ me, slabs)
    there = gather_place(later ^ me, slabs)

    def turn(tile):
        arrays = []
        for n in range(2 // per):
            lines = []
            for lq in range(4):
                for h in range(per):
                    jh = n * per + h
                    lines.append(gathered[pl.ds(8 * tile + 2 * lq + jh, slabs, stride=16), :])
            at = (2 * tile + n) * LANES
            turned[at : at + LANES] = jnp.concatenate(lines, axis=0).T
            arrays.append(at)
        return (arrays * 2)[:2] if per == 2 else arrays

    def half_lane(jh):
        return jh * slabs if per == 2 else 0

    base_g = turn(0)
    base_x = turn(1)

    for jh in range(2):
        index = quarter * K + half_lane(jh) + here
        for j in range(16):
            n = 16 * jh + j
            rows = turned[base_x[jh] + 8 * j : base_x[jh] + 8 * j + 8]
            g_ref[8 * (K + n) : 8 * (K + n) + 8] = lane_pick(rows, index)
            rows = turned[base_g[jh] + 8 * j : base_g[jh] + 8 * j + 8]
            g_ref[8 * n : 8 * n + 8] = lane_pick(rows, index)
    for r in range(8):
        parts = [turned[pl.ds(base_g[0] + 64 * v + r, 8, stride=8), :] for v in range(2)]
        for oq in (2, 3):
            n = 8 * oq + r
            index = oq * K + half_lane(0) + here
            corner = jnp.where(quarter == 0, lane_pick(parts[0], index), lane_pick(parts[1], index))
            at = pl.ds(8 * n, 8)
            g_ref[at, :] = jnp.where(quarter < 2, corner, g_ref[at, :])
    inner = slab < slabs - 1
    for r in range(8):
        parts = [
            [turned[pl.ds(base_x[uh] + 64 * v + r, 8, stride=8), :] for v in range(2)]
            for uh in range(3 - per)
        ]
        for oq in range(4):
            if per == 2:
                index = oq * K + (quarter // 2) * slabs + there
                value = jnp.where(
                    quarter % 2 == 0, lane_pick(parts[0][0], index), lane_pick(parts[0][1], index)
                )
            else:
                index = oq * K + there
                value = lane_pick(parts[0][0], index)
                for uq in range(1, 4):
                    value = jnp.where(quarter == uq, lane_pick(parts[uq // 2][uq % 2], index), value)
            n = 2 * K + 8 * oq + r
            g_ref[8 * n : 8 * n + 8] = jnp.where(inner, value, 0.0)

    lanes_of = half_lane(1)
    states = []
    for nv in range(frames // per):
        found = []
        for line, kind, shifted in ((0, 0, False), (0, 1, True), (1, 0, False), (1, 1, False)):
            index = line * K + lanes_of + (there if shifted else here)
            value = jnp.zeros((8, LANES), F32)
            for lq in range(4):
                for h in range(per):
                    n = 8 * kind + 2 * lq + nv * per + h
                    rows = turned[base_g[1] + 8 * n : base_g[1] + 8 * n + 8]
                    value = jnp.where((quarter == lq) & (frame == h), lane_pick(rows, index), value)
            found.append(jnp.where(inner, value, 0.0) if shifted else value)
        states.append(found)
    norm = jnp.zeros((8, LANES), F32)
    for n in range(K):
        mine = (sub == n % 8) & (quarter == n // 8)
        norm = jnp.where(mine, g_ref[8 * n : 8 * n + 8], norm)
    inverse = 1.0 / norm
    block_of = states[0][3]
    inverses = [jnp.where(block_of == float(b), inverse, 0.0) for b in range(BLOCKS)]

    local = lane % K
    before = jnp.where(slab == 0, local, local - 1)
    after = jnp.where(inner, local + 1, local)

    def coupled(change):
        totals = [None] * 6
        for kind, place in enumerate((local, before, after)):
            for q in range(4):
                picked = lane_pick(change, q * K + place)
                for r in range(8):
                    n = kind * K + 8 * q + r
                    term = g_ref[8 * n : 8 * n + 8] * jnp.broadcast_to(picked[r : r + 1], (8, LANES))
                    slot = 2 * kind + r % 2
                    totals[slot] = term if totals[slot] is None else totals[slot] + term
        return (totals[0] + totals[1]) + ((totals[2] + totals[3]) + (totals[4] + totals[5]))

    p = [s[0] + s[1] - coupled(s[2]) for s in states]
    traces = [s[2] for s in states]

    def sweep(_, carry):
        p, traces = carry
        for b in range(BLOCKS):
            change = [x * inverses[b] for x in p]
            traces = [x + c for x, c in zip(traces, change)]
            p = [x - coupled(c) for x, c in zip(p, change)]
        return p, traces

    p, traces = lax.fori_loop(0, SWEEPS, sweep, (p, traces))

    mine = sub == lane % 8
    lines = []
    for other in (me, jnp.maximum(me - 1, 0), jnp.minimum(me + 1, slabs - 1)):
        for t in range(frames):
            index = ((lane % K) // 8) * K + (t % per) * slabs + other
            value = jnp.where(mine, lane_pick(traces[t // per], index), 0.0)
            lines.append(jnp.sum(value, axis=0, keepdims=True))
    own = lines[:frames]
    lines.append(functools.reduce(jnp.add, own))
    lines.append(functools.reduce(jnp.add, [x * x for x in own]))
    for n, line in enumerate(lines):
        out[n : n + 1] = line


def render(rel, values, tiles):
    parts = []
    for m in range(4):
        parts.append(jnp.where(rel == float(4 * m), values, 0.0))
    mixed = jnp.concatenate(parts, axis=1)
    high = mixed.astype(BF16)
    low = (mixed - high.astype(F32)).astype(BF16)
    return jnp.dot(high, tiles, preferred_element_type=F32) + jnp.dot(
        low, tiles, preferred_element_type=F32
    )


def finish_kernel(shifts, own, by_pair, by_middle, by_cross, raw, corr, top, t_own, t_up, values, out, ext):
    frames, rows, _ = raw.shape
    slab = lax.axis_index("slab")
    low = from_below(slab, lax.axis_size("slab"), by_pair[...], by_middle[...], by_cross[...])
    meta_low = low[PK_META:PK_ALL]
    tiles_low = placed_tiles(low[0 : 2 * K], meta_low[META_COL : META_COL + 1])
    meta_up = from_above(slab, by_pair[PK_META:PK_ALL], by_middle[PK_META:PK_ALL])
    row_own = own[PK_META:PK_ALL].astype(F32)[META_ROW : META_ROW + 1]
    row_up = meta_up[META_ROW : META_ROW + 1] - float(rows)
    row_low = meta_low[META_ROW : META_ROW + 1] + float(rows)
    y = (iota((rows, LANES), 0) + RIM).astype(F32)
    group = (iota((rows, LANES), 1) // K).astype(F32)
    last = rows // PATCH_R - 1
    for t in range(frames):
        ext[0:16] = raw[t, rows - 16 : rows].astype(F32)
        ext[16:32] = low[PK_RAW_FIRST + 16 * t : PK_RAW_FIRST + 16 * t + 16]
        a = shifts[0, t, 0, last]
        tail = warp((ext[pl.ds(8 + a, RIM)], ext[pl.ds(9 + a, RIM)]), shifts[1, t, 0, last])
        image = render(y - row_own - group, values[t : t + 1], t_own[...])
        rel_up = (y - row_up - group)[0:RIM]
        rel_low = (y - row_low - group)[rows - RIM : rows]
        above = render(rel_up, values[frames + t : frames + t + 1], t_up[...])
        below = render(rel_low, values[2 * frames + t : 2 * frames + t + 1], tiles_low)
        out[t, 0:RIM] = top[t].astype(BF16).astype(F32) - image[0:RIM] - above
        out[t, RIM : rows - RIM] = corr[t, RIM : rows - RIM].astype(F32) - image[RIM : rows - RIM]
        out[t, rows - RIM : rows] = tail.astype(BF16).astype(F32) - image[rows - RIM : rows] - below


def local_call(kernel, out_shape, in_specs, scratch_shapes, flops, *args):
    def held(x, spec):
        return pltpu.with_memory_space_constraint(x, pltpu.VMEM) if spec is VMEM_SPEC else x

    return pl.pallas_call(
        kernel,
        out_shape=out_shape,
        in_specs=in_specs,
        out_specs=jax.tree.map(lambda _: VMEM_SPEC, out_shape),
        scratch_shapes=scratch_shapes,
        compiler_params=pltpu.CompilerParams(vmem_limit_bytes=VMEM_BYTES),
        cost_estimate=pl.CostEstimate(flops=flops, bytes_accessed=1 << 18, transcendentals=0),
    )(*[held(x, spec) for x, spec in zip(args, in_specs)])


def shards(raw_movie, shifts, footprints, anchors, block_of, init_traces):
    frames, rows, cols = raw_movie.shape
    slabs = lax.axis_size("slab")
    frame_parts = lax.axis_size("frames")
    vmem, smem = VMEM_SPEC, SMEM_SPEC
    shifts = shifts.transpose(0, 1, 3, 2)
    tiles_shape = pltpu.VMEM((TILE * K, LANES), BF16)
    frame_shape = pltpu.VMEM((frames, rows, LANES), BF16)
    small_shape = pltpu.VMEM((8, LANES), F32)

    pack = local_call(
        pack_kernel,
        pltpu.VMEM((PK_ALL, LANES), BF16),
        [smem, vmem, vmem, vmem],
        [],
        10**8,
        shifts,
        raw_movie,
        footprints.transpose(1, 2, 0),
        anchors.T,
    )
    by_pair, by_middle, by_cross = [lax.ppermute(pack, "slab", route) for route in neighbour_routes(slabs)]

    tile, part, t_own, corr = local_call(
        own_kernel,
        (small_shape, small_shape, tiles_shape, frame_shape),
        [smem, vmem, vmem],
        [pltpu.VMEM((rows + 32, LANES), F32)],
        10**9,
        shifts,
        pack,
        raw_movie,
    )
    gathered, t_up, top = local_call(
        edge_kernel,
        (pltpu.VMEM((16, LANES), F32), tiles_shape, pltpu.VMEM((frames, RIM, LANES), F32)),
        [vmem] * 9,
        [],
        10**9,
        pack,
        by_pair,
        by_middle,
        raw_movie,
        init_traces.T,
        block_of[None],
        t_own,
        tile,
        part,
    )
    for mask in gather_masks(slabs):
        other = lax.ppermute(gathered, "slab", [(i, i ^ mask) for i in range(slabs)])
        gathered = jnp.concatenate([gathered, other], axis=0)

    values = local_call(
        functools.partial(sweep_kernel, frames, slabs),
        small_shape,
        [vmem],
        [pltpu.VMEM((4 * LANES, LANES), F32), pltpu.VMEM((8 * 3 * K, LANES), F32)],
        10**9,
        gathered,
    )

    moments = values[3 * frames : 3 * frames + 2, :K]
    for hop in range(1, frame_parts):
        other = lax.ppermute(
            values, "frames", [(i, (i + hop) % frame_parts) for i in range(frame_parts)]
        )
        moments = moments + other[3 * frames : 3 * frames + 2, :K]

    residual = local_call(
        finish_kernel,
        jax.ShapeDtypeStruct((frames, rows, LANES), F32),
        [smem] + [vmem] * 10,
        [pltpu.VMEM((32, LANES), F32)],
        10**9,
        shifts,
        pack,
        by_pair,
        by_middle,
        by_cross,
        raw_movie,
        corr,
        top,
        t_own,
        t_up,
        values,
    )

    frame_total = frames * frame_parts
    trace_mean = moments[0] / frame_total
    spread = moments[1] / frame_total - trace_mean * trace_mean
    traces_z = (values[:frames, :K] - trace_mean) / jnp.sqrt(spread + EPSILON)
    return traces_z.T, residual


def solution(mesh):
    in_specs = (
        P("frames", "slab", None),
        P(None, "frames", "slab", None),
        P("slab", None, None),
        P("slab", None),
        P("slab"),
        P("slab", "frames"),
    )
    out_specs = (P("slab", "frames"), P("frames", "slab", None))
    return jax.shard_map(shards, mesh=mesh, in_specs=in_specs, out_specs=out_specs, check_vma=False)
```

```python
import functools

import jax
import jax.numpy as jnp
from jax import lax
from jax.experimental import pallas as pl
from jax.experimental.pallas import tpu as pltpu
from jax.sharding import PartitionSpec as P

SHIFT = 3
PATCH_R = 32
BLOCKS = 4
SWEEPS = 3
TILE = 16
RIM = 8
LANES = 128
K = 32
GROUPS = LANES // K
WEIGHT_NEAR = 0.75
WEIGHT_FAR = 0.25
EPSILON = 1e-05
F32 = jnp.float32
BF16 = jnp.bfloat16

PK_RAW_LAST = 64
PK_RAW_FIRST = 96
PK_META = 128
PK_ALL = 144
META_ROW = 0
META_COL = 1
META_SHIFT = 2
META_FIRST = 6
VMEM_BYTES = 8 << 20
VMEM_SPEC = pl.BlockSpec(memory_space=pltpu.VMEM)


def iota(shape, axis):
    return lax.broadcasted_iota(jnp.int32, shape, axis)


def lane_pick(values, index):
    return jnp.take_along_axis(values, index, axis=1, mode="promise_in_bounds")


def as_column(line):
    own = iota((K, LANES), 0) == iota((K, LANES), 1)
    return jnp.sum(jnp.where(own, line, 0.0), axis=1, keepdims=True)


def placed_tiles(tiles, col_line):
    col = as_column(col_line).astype(jnp.int32)
    offset = iota((K, LANES), 1) - col
    inside = (offset >= 0) & (offset < TILE)
    base = jnp.clip(offset, 0, TILE - 1)
    out = []
    for i in range(tiles.shape[0] // K * 8):
        half, part = divmod(i, 8)
        tile = tiles[half * K : (half + 1) * K].astype(F32)
        out.append(jnp.where(inside, lane_pick(tile, base + part * TILE), 0.0))
    return jnp.concatenate(out, axis=0).astype(BF16)


def dot_nt(a, b):
    return lax.dot_general(a, b, (((1,), (1,)), ((), ())), preferred_element_type=F32)


def fold_lanes(x):
    x = x + pltpu.roll(x, 64, 1)
    return x + pltpu.roll(x, 32, 1)


def gram(tiles_a, tiles_b, row_a, row_b):
    full = dot_nt(tiles_a, tiles_b)
    diff = row_a - row_b - (iota((K, LANES), 1) // K).astype(F32)
    total = jnp.zeros((K, LANES), F32)
    for q in range(-(TILE - 1), TILE):
        part = None
        for m in range(4):
            i = 4 * m - q
            if 0 <= i < TILE:
                block = full[i * K : (i + 1) * K, m * LANES : (m + 1) * LANES]
                part = block if part is None else part + block
        if part is not None:
            total = total + jnp.where(diff == float(q), part, 0.0)
    return fold_lanes(total)


def project(corr, tiles, rel):
    part = dot_nt(corr, tiles)
    total = jnp.zeros(rel.shape, F32)
    for m in range(4):
        total = total + jnp.where(rel == float(4 * m), part[:, m * LANES : (m + 1) * LANES], 0.0)
    return fold_lanes(jnp.sum(total, axis=0, keepdims=True))


def neighbour_routes(slabs):
    pairs = [(i, i ^ 1) for i in range(slabs)]
    ends = [(0, 1), (1, 2), (2, 0), (slabs - 3, slabs - 2), (slabs - 2, slabs - 1), (slabs - 1, slabs - 3)]
    middle = [p for i in range(3, slabs - 4, 2) for p in ((i, i + 1), (i + 1, i))]
    return pairs, ends + middle


def from_above(slab, by_pair, by_middle):
    found = jnp.where(slab % 2 == 1, by_pair.astype(F32), by_middle.astype(F32))
    return jnp.where(slab == 0, 0.0, found)


def below_part(pack, frames):
    firsts = [pack[PK_RAW_FIRST + 16 * t : PK_RAW_FIRST + 16 * t + 16].astype(F32)[0:8] for t in range(frames)]
    parts = [pack[0:K].astype(F32)] + firsts + [pack[PK_META:PK_ALL].astype(F32)]
    return jnp.concatenate(parts, axis=0)


def from_below(slab, slabs, by_pair, by_middle, by_cross):
    odd = jnp.where((slab == 1) | (slab == slabs - 3), by_cross, by_middle)
    found = jnp.where(slab % 2 == 0, by_pair, odd)
    return jnp.where(slab == slabs - 1, 0.0, found)


def gather_masks(slabs):
    bits = slabs.bit_length() - 1
    return [(1 << (bits - 1 - r)) | 1 for r in range(bits - 1)] + [1]


def gather_place(diff, slabs):
    bits = slabs.bit_length() - 1
    odd = diff & 1
    place = jnp.zeros_like(diff)
    for r in range(bits - 1):
        bit = (diff >> (bits - 1 - r)) & 1
        place = place + bit * (1 << r)
        odd = odd ^ bit
    return place + odd * (1 << (bits - 1))


def gather_source():
    place = iota((8, LANES), 1)
    return 8 * ((place // 16) % 4) + place % 8, (place // 8) % 2, place < LANES // 2


def pack_kernel(shifts, raw, tiles, anchors, init, block_of, out, raw_out, line):
    frames, rows, _ = raw.shape
    last = rows // PATCH_R - 1
    base = lax.axis_index("slab") * rows - RIM
    for half in range(2):
        part = tiles[8 * half : 8 * half + 8].astype(F32).reshape(LANES, K)
        out[K * half : K * half + K] = part.T.astype(BF16)
    for t in range(frames):
        out[PK_RAW_LAST + 16 * t : PK_RAW_LAST + 16 * t + 16] = raw[t, rows - 16 : rows]
        out[PK_RAW_FIRST + 16 * t : PK_RAW_FIRST + 16 * t + 16] = raw[t, 0:16]
    raw_out[...] = raw[...]
    places = jnp.concatenate([anchors[...].astype(F32)] * GROUPS, axis=1)
    sub = iota((16, LANES), 0)
    meta = jnp.where(sub == META_COL, places[1:2], 0.0)
    meta = jnp.where(sub == META_ROW, places[0:1] - base.astype(F32), meta)
    for t in range(frames):
        for axis in range(2):
            pair = shifts[axis, t].astype(F32)
            for place, patch in ((META_SHIFT, last), (META_FIRST, 0)):
                meta = jnp.where(sub == place + axis * frames + t, pair[:, patch : patch + 1], meta)
    out[PK_META:PK_ALL] = meta.astype(BF16)
    source, frame, first_kind = gather_source()
    inits = jnp.concatenate([init[...]] * GROUPS, axis=1)
    blocks = jnp.concatenate([block_of[...].astype(F32)] * GROUPS, axis=1)
    found = jnp.zeros((8, LANES), F32)
    for t in range(frames):
        both = [lane_pick(jnp.broadcast_to(x, (8, LANES)), source) for x in (inits[t : t + 1], blocks)]
        found = jnp.where(frame == t, jnp.where(first_kind, both[0], both[1]), found)
    line[...] = found


def write_tile(out, first, mat, rows):
    lane = iota((K, LANES), 1)
    own = lane // 8 == iota((K, LANES), 0) % 16
    for lq in range(4):
        part = jnp.where(own, lane_pick(mat, 8 * lq + lane % 8), 0.0)
        for jh in range(2):
            if 2 * lq + jh in rows:
                out[first + 2 * lq + jh : first + 2 * lq + jh + 1] = jnp.sum(
                    part[16 * jh : 16 * jh + 16], axis=0, keepdims=True
                )


def warp(rows_at, count, a_line, c_line):
    both = jnp.zeros((count, LANES), F32)
    for a in range(-SHIFT, SHIFT + 1):
        window = rows_at(a)
        blend = WEIGHT_NEAR * window[0:count] + WEIGHT_FAR * window[1 : count + 1]
        both = jnp.where(a_line == float(a), blend, both)
    place = iota((count, LANES), 1) + c_line.astype(jnp.int32)
    moved = lane_pick(both, jnp.clip(place, 0, LANES - 1))
    return jnp.where((place >= 0) & (place < LANES), moved, 0.0)


def shift_lines(meta, row, frames, t):
    return meta[row + t : row + t + 1], meta[row + frames + t : row + frames + t + 1]


def own_kernel(own, raw, tile, part, t_own, corr, extra, ext):
    frames, rows, _ = raw.shape
    slab = lax.axis_index("slab")
    is_last = slab == lax.axis_size("slab") - 1
    extra[...] = below_part(own[...], frames)
    meta = own[PK_META:PK_ALL].astype(F32)
    row = meta[META_ROW : META_ROW + 1]
    tiles = placed_tiles(own[0 : 2 * K], meta[META_COL : META_COL + 1])
    t_own[...] = tiles
    tile[...] = jnp.zeros((8, LANES), F32)
    part[...] = jnp.zeros((8, LANES), F32)
    write_tile(tile, 0, gram(tiles, tiles, as_column(row), row), (0, 2, 4, 5, 6, 7))
    y = iota((rows, LANES), 0)
    keep = (y >= RIM) & ((y < rows - RIM) | is_last)
    rel = (y + RIM).astype(F32) - row - (iota((rows, LANES), 1) // K).astype(F32)
    for t in range(frames):
        ext[0:16] = jnp.zeros((16, LANES), F32)
        ext[16 : 16 + rows] = raw[t].astype(F32)
        ext[16 + rows : 32 + rows] = jnp.zeros((16, LANES), F32)
        parts = []
        for p, row_of in ((0, META_FIRST), (1, META_SHIFT)):

            def rows_at(a, first=16 + p * PATCH_R):
                return ext[first + a : first + a + PATCH_R + 1]

            parts.append(warp(rows_at, PATCH_R, *shift_lines(meta, row_of, frames, t)))
        image = jnp.concatenate(parts, axis=0)
        corr[t] = image.astype(BF16)
        part[t : t + 1] = project(jnp.where(keep, image, 0.0).astype(BF16), tiles, rel)


def low_kernel(own, by_pair, by_middle, by_cross, tiles, tail, lines, ext):
    frames = tail.shape[0]
    low = from_below(
        lax.axis_index("slab"),
        lax.axis_size("slab"),
        below_part(by_pair[...], frames),
        below_part(by_middle[...], frames),
        by_cross[...],
    )
    meta = own[PK_META:PK_ALL].astype(F32)
    meta_low = low[K + 8 * frames :]
    tiles[...] = placed_tiles(low[0:K], meta_low[META_COL : META_COL + 1])
    lines[...] = jnp.broadcast_to(meta_low[META_ROW : META_ROW + 1], (8, LANES))
    for t in range(frames):
        ext[0:16] = own[PK_RAW_LAST + 16 * t : PK_RAW_LAST + 16 * t + 16].astype(F32)
        ext[16:24] = low[K + 8 * t : K + 8 * t + 8]

        def rows_at(a):
            return ext[8 + a : 17 + a]

        tail[t] = warp(rows_at, RIM, *shift_lines(meta, META_SHIFT, frames, t))


def edge_kernel(rows, own, by_pair, by_middle, line, t_own, tile, part, out, t_up, top):
    frames = top.shape[0]
    up = from_above(lax.axis_index("slab"), by_pair[...], by_middle[...])
    meta_own = own[PK_META:PK_ALL].astype(F32)
    meta_up = up[PK_META:PK_ALL]
    row_own = meta_own[META_ROW : META_ROW + 1]
    row_up = meta_up[META_ROW : META_ROW + 1] - float(rows)
    tiles_own = t_own[...]
    tiles_up = placed_tiles(up[0 : 2 * K], meta_up[META_COL : META_COL + 1])
    t_up[...] = tiles_up
    out[0:8] = tile[...]
    write_tile(out, 8, gram(tiles_up, tiles_own, as_column(row_up), row_own), range(8))

    source, frame, first_kind = gather_source()
    found = jnp.zeros((8, LANES), F32)
    shape = (2 * RIM, LANES)
    rel_own = iota(shape, 0).astype(F32) - row_own - (iota(shape, 1) // K).astype(F32)
    rel_up = iota(shape, 0).astype(F32) - row_up - (iota(shape, 1) // K).astype(F32)
    for t in range(frames):
        at = PK_RAW_LAST + 16 * t
        first = PK_RAW_FIRST + 16 * t
        near = jnp.concatenate([up[at : at + 16], own[first : first + 16].astype(F32)], axis=0)
        zone = []
        for start, meta, row in ((8, meta_up, META_SHIFT), (16, meta_own, META_FIRST)):

            def rows_at(a, start=start):
                return near[start + a : start + a + RIM + 1]

            zone.append(warp(rows_at, RIM, *shift_lines(meta, row, frames, t)))
        image = jnp.concatenate(zone, axis=0).astype(BF16)
        top[t] = zone[1]
        sums = (project(image, tiles_own, rel_own) + part[t : t + 1], project(image, tiles_up, rel_up))
        both = [lane_pick(jnp.broadcast_to(x, (8, LANES)), source) for x in sums]
        found = jnp.where(frame == t, jnp.where(first_kind, both[0], both[1]), found)
    out[1:2] = found[0:1]
    out[3:4] = line[0:1]


def sweep_kernel(frames, slabs, gathered, out, turned, g_ref):
    per = K // slabs
    lane = iota((8, LANES), 1)
    sub = iota((8, LANES), 0)
    quarter = lane // K
    slab = lane % slabs
    frame = (lane % K) // slabs
    me = lax.axis_index("slab")
    later = jnp.minimum(slab + 1, slabs - 1)
    here = gather_place(slab ^ me, slabs)
    there = gather_place(later ^ me, slabs)

    def turn(tile):
        arrays = []
        for n in range(2 // per):
            lines = []
            for lq in range(4):
                for h in range(per):
                    jh = n * per + h
                    lines.append(gathered[pl.ds(8 * tile + 2 * lq + jh, slabs, stride=16), :])
            at = (2 * tile + n) * LANES
            turned[at : at + LANES] = jnp.concatenate(lines, axis=0).T
            arrays.append(at)
        return (arrays * 2)[:2] if per == 2 else arrays

    def half_lane(jh):
        return jh * slabs if per == 2 else 0

    base_g = turn(0)
    base_x = turn(1)

    for jh in range(2):
        index = quarter * K + half_lane(jh) + here
        for j in range(16):
            n = 16 * jh + j
            rows = turned[base_x[jh] + 8 * j : base_x[jh] + 8 * j + 8]
            g_ref[8 * (K + n) : 8 * (K + n) + 8] = lane_pick(rows, index)
            rows = turned[base_g[jh] + 8 * j : base_g[jh] + 8 * j + 8]
            g_ref[8 * n : 8 * n + 8] = lane_pick(rows, index)
    for r in range(8):
        parts = [turned[pl.ds(base_g[0] + 64 * v + r, 8, stride=8), :] for v in range(2)]
        for oq in (2, 3):
            n = 8 * oq + r
            index = oq * K + half_lane(0) + here
            corner = jnp.where(quarter == 0, lane_pick(parts[0], index), lane_pick(parts[1], index))
            at = pl.ds(8 * n, 8)
            g_ref[at, :] = jnp.where(quarter < 2, corner, g_ref[at, :])
    inner = slab < slabs - 1
    for r in range(8):
        parts = [
            [turned[pl.ds(base_x[uh] + 64 * v + r, 8, stride=8), :] for v in range(2)]
            for uh in range(3 - per)
        ]
        for oq in range(4):
            if per == 2:
                index = oq * K + (quarter // 2) * slabs + there
                value = jnp.where(
                    quarter % 2 == 0, lane_pick(parts[0][0], index), lane_pick(parts[0][1], index)
                )
            else:
                index = oq * K + there
                value = lane_pick(parts[0][0], index)
                for uq in range(1, 4):
                    value = jnp.where(quarter == uq, lane_pick(parts[uq // 2][uq % 2], index), value)
            n = 2 * K + 8 * oq + r
            g_ref[8 * n : 8 * n + 8] = jnp.where(inner, value, 0.0)

    lanes_of = half_lane(1)
    states = []
    for nv in range(frames // per):
        found = []
        for line, kind, shifted in ((0, 0, False), (0, 1, True), (1, 0, False), (1, 1, False)):
            index = line * K + lanes_of + (there if shifted else here)
            value = jnp.zeros((8, LANES), F32)
            for lq in range(4):
                for h in range(per):
                    n = 8 * kind + 2 * lq + nv * per + h
                    rows = turned[base_g[1] + 8 * n : base_g[1] + 8 * n + 8]
                    value = jnp.where((quarter == lq) & (frame == h), lane_pick(rows, index), value)
            found.append(jnp.where(inner, value, 0.0) if shifted else value)
        states.append(found)
    norm = jnp.zeros((8, LANES), F32)
    for n in range(K):
        mine = (sub == n % 8) & (quarter == n // 8)
        norm = jnp.where(mine, g_ref[8 * n : 8 * n + 8], norm)
    inverse = 1.0 / norm
    block_of = states[0][3]
    inverses = [jnp.where(block_of == float(b), inverse, 0.0) for b in range(BLOCKS)]

    local = lane % K
    before = jnp.where(slab == 0, local, local - 1)
    after = jnp.where(inner, local + 1, local)

    def coupled(change):
        totals = [None] * 6
        for kind, place in enumerate((local, before, after)):
            for q in range(4):
                picked = lane_pick(change, q * K + place)
                for r in range(8):
                    n = kind * K + 8 * q + r
                    term = g_ref[8 * n : 8 * n + 8] * jnp.broadcast_to(picked[r : r + 1], (8, LANES))
                    slot = 2 * kind + r % 2
                    totals[slot] = term if totals[slot] is None else totals[slot] + term
        return (totals[0] + totals[1]) + ((totals[2] + totals[3]) + (totals[4] + totals[5]))

    p = [s[0] + s[1] - coupled(s[2]) for s in states]
    traces = [s[2] for s in states]

    def sweep(_, carry):
        p, traces = carry
        for b in range(BLOCKS):
            change = [x * inverses[b] for x in p]
            traces = [x + c for x, c in zip(traces, change)]
            p = [x - coupled(c) for x, c in zip(p, change)]
        return p, traces

    p, traces = lax.fori_loop(0, SWEEPS, sweep, (p, traces))

    mine = sub == lane % 8
    lines = []
    for other in (me, jnp.maximum(me - 1, 0), jnp.minimum(me + 1, slabs - 1)):
        for t in range(frames):
            index = ((lane % K) // 8) * K + (t % per) * slabs + other
            value = jnp.where(mine, lane_pick(traces[t // per], index), 0.0)
            lines.append(jnp.sum(value, axis=0, keepdims=True))
    own = lines[:frames]
    lines.append(functools.reduce(jnp.add, own))
    lines.append(functools.reduce(jnp.add, [x * x for x in own]))
    for n, line in enumerate(lines):
        out[n : n + 1] = line


def render(rel, values, tiles, groups=range(4)):
    mixed = jnp.concatenate([jnp.where(rel == float(4 * m), values, 0.0) for m in groups], axis=1)
    high = mixed.astype(BF16)
    low = (mixed - high.astype(F32)).astype(BF16)
    return jnp.dot(high, tiles, preferred_element_type=F32) + jnp.dot(
        low, tiles, preferred_element_type=F32
    )


def finish_kernel(own, by_pair, by_middle, corr, top, tail, lines, t_own, t_up, t_low, values, out):
    frames, rows, _ = corr.shape
    slab = lax.axis_index("slab")
    meta_up = from_above(slab, by_pair[PK_META:PK_ALL], by_middle[PK_META:PK_ALL])
    row_own = own[PK_META:PK_ALL].astype(F32)[META_ROW : META_ROW + 1]
    row_up = meta_up[META_ROW : META_ROW + 1] - float(rows)
    row_low = lines[0:1] + float(rows)
    y = (iota((rows, LANES), 0) + RIM).astype(F32)
    group = (iota((rows, LANES), 1) // K).astype(F32)
    rel_own = y - row_own - group
    rel_up = (y - row_up - group)[0:RIM]
    rel_low = (y - row_low - group)[rows - RIM : rows]
    half = t_low.shape[0]
    for t in range(frames):
        image = render(rel_own, values[t : t + 1], t_own[...])
        above = render(rel_up, values[frames + t : frames + t + 1], t_up[half:], (2, 3))
        below = render(rel_low, values[2 * frames + t : 2 * frames + t + 1], t_low[...], (0, 1))
        out[t, 0:RIM] = top[t].astype(BF16).astype(F32) - image[0:RIM] - above
        out[t, RIM : rows - RIM] = corr[t, RIM : rows - RIM].astype(F32) - image[RIM : rows - RIM]
        out[t, rows - RIM : rows] = tail[t].astype(BF16).astype(F32) - image[rows - RIM : rows] - below


def local_call(kernel, out_shape, scratch_shapes, flops, args, hold=True):
    if hold:
        args = [pltpu.with_memory_space_constraint(x, pltpu.VMEM) for x in args]
    return pl.pallas_call(
        kernel,
        out_shape=out_shape,
        in_specs=[VMEM_SPEC] * len(args),
        out_specs=jax.tree.map(lambda _: VMEM_SPEC, out_shape),
        scratch_shapes=scratch_shapes,
        compiler_params=pltpu.CompilerParams(vmem_limit_bytes=VMEM_BYTES),
        cost_estimate=pl.CostEstimate(flops=flops, bytes_accessed=1 << 18, transcendentals=0),
    )(*args)


def shards(raw_movie, shifts, footprints, anchors, block_of, init_traces):
    frames, rows, cols = raw_movie.shape
    slabs = lax.axis_size("slab")
    frame_parts = lax.axis_size("frames")
    small = pltpu.VMEM((8, LANES), F32)
    tiles = pltpu.VMEM((TILE * K, LANES), BF16)
    half_tiles = pltpu.VMEM((TILE * K // 2, LANES), BF16)
    image = pltpu.VMEM((frames, rows, LANES), BF16)
    rim = pltpu.VMEM((frames, RIM, LANES), F32)
    extra_rows = K + 8 * frames + 16

    pack, raw, line = local_call(
        pack_kernel,
        (pltpu.VMEM((PK_ALL, LANES), BF16), image, small),
        [],
        10**8,
        (shifts.transpose(0, 1, 3, 2), raw_movie, footprints.transpose(1, 2, 0), anchors.T, init_traces.T, block_of[None]),
        hold=False,
    )
    by_pair, by_middle = [lax.ppermute(pack, "slab", route) for route in neighbour_routes(slabs)]

    tile, part, t_own, corr, extra = local_call(
        own_kernel,
        (small, small, tiles, image, pltpu.VMEM((extra_rows, LANES), F32)),
        [pltpu.VMEM((rows + 32, LANES), F32)],
        10**9,
        (pack, raw),
    )
    gathered, t_up, top = local_call(
        functools.partial(edge_kernel, rows),
        (pltpu.VMEM((16, LANES), F32), tiles, rim),
        [],
        10**9,
        (pack, by_pair, by_middle, line, t_own, tile, part),
    )
    for mask in gather_masks(slabs):
        route = [(i, i ^ mask) for i in range(slabs)]
        if mask == 3:
            other = lax.ppermute(jnp.concatenate([extra, gathered], axis=0), "slab", route)
            by_cross, other = other[:extra_rows], other[extra_rows:]
        else:
            other = lax.ppermute(gathered, "slab", route)
        gathered = jnp.concatenate([gathered, other], axis=0)

    t_low, tail, lines = local_call(
        low_kernel,
        (half_tiles, rim, small),
        [pltpu.VMEM((24, LANES), F32)],
        10**9,
        (pack, by_pair, by_middle, by_cross),
    )
    values = local_call(
        functools.partial(sweep_kernel, frames, slabs),
        small,
        [pltpu.VMEM((4 * LANES, LANES), F32), pltpu.VMEM((8 * 3 * K, LANES), F32)],
        10**9,
        (gathered,),
    )

    moments = values[3 * frames : 3 * frames + 2, :K]
    for hop in range(1, frame_parts):
        other = lax.ppermute(
            values, "frames", [(i, (i + hop) % frame_parts) for i in range(frame_parts)]
        )
        moments = moments + other[3 * frames : 3 * frames + 2, :K]

    residual = local_call(
        finish_kernel,
        jax.ShapeDtypeStruct((frames, rows, LANES), F32),
        [],
        10**9,
        (pack, by_pair, by_middle, corr, top, tail, lines, t_own, t_up, t_low, values),
    )

    frame_total = frames * frame_parts
    trace_mean = moments[0] / frame_total
    spread = moments[1] / frame_total - trace_mean * trace_mean
    traces_z = (values[:frames, :K] - trace_mean) / jnp.sqrt(spread + EPSILON)
    return traces_z.T, residual


def solution(mesh):
    in_specs = (
        P("frames", "slab", None),
        P(None, "frames", "slab", None),
        P("slab", None, None),
        P("slab", None),
        P("slab"),
        P("slab", "frames"),
    )
    out_specs = (P("slab", "frames"), P("frames", "slab", None))
    return jax.shard_map(shards, mesh=mesh, in_specs=in_specs, out_specs=out_specs, check_vma=False)
```

```python
import functools

import jax
import jax.numpy as jnp
from jax import lax
from jax.experimental import pallas as pl
from jax.experimental.pallas import tpu as pltpu
from jax.sharding import PartitionSpec as P

SHIFT = 3
PATCH_R = 32
BLOCKS = 4
SWEEPS = 3
TILE = 16
RIM = 8
LANES = 128
K = 32
GROUPS = LANES // K
WEIGHT_NEAR = 0.75
WEIGHT_FAR = 0.25
EPSILON = 1e-05
F32 = jnp.float32
BF16 = jnp.bfloat16

PK_RAW_LAST = 64
PK_RAW_FIRST = 96
PK_META = 128
PK_ALL = 144
META_ROW = 0
META_COL = 1
META_SHIFT = 2
META_FIRST = 6
VMEM_BYTES = 8 << 20
VMEM_SPEC = pl.BlockSpec(memory_space=pltpu.VMEM)


def iota(shape, axis):
    return lax.broadcasted_iota(jnp.int32, shape, axis)


def lane_pick(values, index):
    return jnp.take_along_axis(values, index, axis=1, mode="promise_in_bounds")


def as_column(line):
    own = iota((K, LANES), 0) == iota((K, LANES), 1)
    return jnp.sum(jnp.where(own, line, 0.0), axis=1, keepdims=True)


def placed_tiles(tiles, col_line):
    col = as_column(col_line).astype(jnp.int32)
    offset = iota((K, LANES), 1) - col
    inside = (offset >= 0) & (offset < TILE)
    base = jnp.clip(offset, 0, TILE - 1)
    out = []
    for i in range(tiles.shape[0] // K * 8):
        half, part = divmod(i, 8)
        tile = tiles[half * K : (half + 1) * K].astype(F32)
        out.append(jnp.where(inside, lane_pick(tile, base + part * TILE), 0.0))
    return jnp.concatenate(out, axis=0).astype(BF16)


def dot_nt(a, b):
    return lax.dot_general(a, b, (((1,), (1,)), ((), ())), preferred_element_type=F32)


def fold_lanes(x):
    x = x + pltpu.roll(x, 64, 1)
    return x + pltpu.roll(x, 32, 1)


def gram(tiles_a, tiles_b, row_a, row_b):
    full = dot_nt(tiles_a, tiles_b)
    diff = row_a - row_b - (iota((K, LANES), 1) // K).astype(F32)
    total = jnp.zeros((K, LANES), F32)
    for q in range(-(TILE - 1), TILE):
        part = None
        for m in range(4):
            i = 4 * m - q
            if 0 <= i < TILE:
                block = full[i * K : (i + 1) * K, m * LANES : (m + 1) * LANES]
                part = block if part is None else part + block
        if part is not None:
            total = total + jnp.where(diff == float(q), part, 0.0)
    return fold_lanes(total)


def project(corr, tiles, rel):
    part = dot_nt(corr, tiles)
    total = jnp.zeros(rel.shape, F32)
    for m in range(4):
        total = total + jnp.where(rel == float(4 * m), part[:, m * LANES : (m + 1) * LANES], 0.0)
    return fold_lanes(jnp.sum(total, axis=0, keepdims=True))


def neighbour_routes(slabs):
    pairs = [(i, i ^ 1) for i in range(slabs)]
    ends = [(0, 1), (1, 2), (2, 0), (slabs - 3, slabs - 2), (slabs - 2, slabs - 1), (slabs - 1, slabs - 3)]
    middle = [p for i in range(3, slabs - 4, 2) for p in ((i, i + 1), (i + 1, i))]
    return pairs, ends + middle


def from_above(slab, by_pair, by_middle):
    found = jnp.where(slab % 2 == 1, by_pair.astype(F32), by_middle.astype(F32))
    return jnp.where(slab == 0, 0.0, found)


def below_part(pack, frames):
    firsts = [pack[PK_RAW_FIRST + 16 * t : PK_RAW_FIRST + 16 * t + 16].astype(F32)[0:8] for t in range(frames)]
    parts = [pack[0:K].astype(F32)] + firsts + [pack[PK_META:PK_ALL].astype(F32)]
    return jnp.concatenate(parts, axis=0)


def from_below(slab, slabs, by_pair, by_middle, by_cross):
    odd = jnp.where((slab == 1) | (slab == slabs - 3), by_cross, by_middle)
    found = jnp.where(slab % 2 == 0, by_pair, odd)
    return jnp.where(slab == slabs - 1, 0.0, found)


def gather_masks(slabs):
    bits = slabs.bit_length() - 1
    return [(2 << r) | 1 for r in range(bits - 1)] + [1]


def gather_place(diff, slabs):
    bits = slabs.bit_length() - 1
    odd = diff & 1
    place = jnp.zeros_like(diff)
    for r in range(bits - 1):
        bit = (diff >> (r + 1)) & 1
        place = place + bit * (1 << r)
        odd = odd ^ bit
    return place + odd * (1 << (bits - 1))


def gather_source():
    place = iota((8, LANES), 1)
    return 8 * ((place // 16) % 4) + place % 8, (place // 8) % 2, place < LANES // 2


def pack_kernel(*refs):
    count = 6
    given, (out, raw, line) = refs[:count], refs[count : count + 3]
    held = refs[count + 3 : 2 * count + 2]
    sems = refs[-1]
    shifts, tiles, anchors, init, block_of = held
    copies = [
        pltpu.make_async_copy(source, target, sems.at[n])
        for n, (source, target) in enumerate(zip(given, (raw, *held)))
    ]
    for copy in copies:
        copy.start()
    for copy in copies:
        copy.wait()
    frames, rows, _ = raw.shape
    last = rows // PATCH_R - 1
    base = lax.axis_index("slab") * rows - RIM
    for half in range(2):
        part = tiles[8 * half : 8 * half + 8].astype(F32).reshape(LANES, K)
        out[K * half : K * half + K] = part.T.astype(BF16)
    for t in range(frames):
        out[PK_RAW_LAST + 16 * t : PK_RAW_LAST + 16 * t + 16] = raw[t, rows - 16 : rows]
        out[PK_RAW_FIRST + 16 * t : PK_RAW_FIRST + 16 * t + 16] = raw[t, 0:16]
    places = jnp.concatenate([anchors[...].astype(F32)] * GROUPS, axis=1)
    sub = iota((16, LANES), 0)
    meta = jnp.where(sub == META_COL, places[1:2], 0.0)
    meta = jnp.where(sub == META_ROW, places[0:1] - base.astype(F32), meta)
    for t in range(frames):
        for axis in range(2):
            pair = shifts[axis, t].astype(F32)
            for place, patch in ((META_SHIFT, last), (META_FIRST, 0)):
                meta = jnp.where(sub == place + axis * frames + t, pair[:, patch : patch + 1], meta)
    out[PK_META:PK_ALL] = meta.astype(BF16)
    source, frame, first_kind = gather_source()
    inits = jnp.concatenate([init[...]] * GROUPS, axis=1)
    blocks = jnp.concatenate([block_of[...].astype(F32)] * GROUPS, axis=1)
    found = jnp.zeros((8, LANES), F32)
    for t in range(frames):
        both = [lane_pick(jnp.broadcast_to(x, (8, LANES)), source) for x in (inits[t : t + 1], blocks)]
        found = jnp.where(frame == t, jnp.where(first_kind, both[0], both[1]), found)
    line[...] = found


def write_tile(out, first, mat, rows):
    lane = iota((K, LANES), 1)
    own = lane // 8 == iota((K, LANES), 0) % 16
    for lq in range(4):
        part = jnp.where(own, lane_pick(mat, 8 * lq + lane % 8), 0.0)
        for jh in range(2):
            if 2 * lq + jh in rows:
                out[first + 2 * lq + jh : first + 2 * lq + jh + 1] = jnp.sum(
                    part[16 * jh : 16 * jh + 16], axis=0, keepdims=True
                )


def warp(rows_at, count, a_line, c_line):
    both = jnp.zeros((count, LANES), F32)
    for a in range(-SHIFT, SHIFT + 1):
        window = rows_at(a)
        blend = WEIGHT_NEAR * window[0:count] + WEIGHT_FAR * window[1 : count + 1]
        both = jnp.where(a_line == float(a), blend, both)
    place = iota((count, LANES), 1) + c_line.astype(jnp.int32)
    moved = lane_pick(both, jnp.clip(place, 0, LANES - 1))
    return jnp.where((place >= 0) & (place < LANES), moved, 0.0)


def shift_lines(meta, row, frames, t):
    return meta[row + t : row + t + 1], meta[row + frames + t : row + frames + t + 1]


def own_kernel(own, raw, tile, part, t_own, corr, extra, ext):
    frames, rows, _ = raw.shape
    slab = lax.axis_index("slab")
    is_last = slab == lax.axis_size("slab") - 1
    extra[...] = below_part(own[...], frames)
    meta = own[PK_META:PK_ALL].astype(F32)
    row = meta[META_ROW : META_ROW + 1]
    tiles = placed_tiles(own[0 : 2 * K], meta[META_COL : META_COL + 1])
    t_own[...] = tiles
    tile[...] = jnp.zeros((8, LANES), F32)
    part[...] = jnp.zeros((8, LANES), F32)
    write_tile(tile, 0, gram(tiles, tiles, as_column(row), row), (0, 2, 4, 5, 6, 7))
    y = iota((rows, LANES), 0)
    keep = (y >= RIM) & ((y < rows - RIM) | is_last)
    rel = (y + RIM).astype(F32) - row - (iota((rows, LANES), 1) // K).astype(F32)
    for t in range(frames):
        ext[0:16] = jnp.zeros((16, LANES), F32)
        ext[16 : 16 + rows] = raw[t].astype(F32)
        ext[16 + rows : 32 + rows] = jnp.zeros((16, LANES), F32)
        parts = []
        for p, row_of in ((0, META_FIRST), (1, META_SHIFT)):

            def rows_at(a, first=16 + p * PATCH_R):
                return ext[first + a : first + a + PATCH_R + 1]

            parts.append(warp(rows_at, PATCH_R, *shift_lines(meta, row_of, frames, t)))
        image = jnp.concatenate(parts, axis=0)
        corr[t] = image.astype(BF16)
        part[t : t + 1] = project(jnp.where(keep, image, 0.0).astype(BF16), tiles, rel)


def low_kernel(own, by_pair, by_middle, by_cross, tiles, tail, lines, ext):
    frames = tail.shape[0]
    low = from_below(
        lax.axis_index("slab"),
        lax.axis_size("slab"),
        below_part(by_pair[...], frames),
        below_part(by_middle[...], frames),
        by_cross[...],
    )
    meta = own[PK_META:PK_ALL].astype(F32)
    meta_low = low[K + 8 * frames :]
    tiles[...] = placed_tiles(low[0:K], meta_low[META_COL : META_COL + 1])
    lines[...] = jnp.broadcast_to(meta_low[META_ROW : META_ROW + 1], (8, LANES))
    for t in range(frames):
        ext[0:16] = own[PK_RAW_LAST + 16 * t : PK_RAW_LAST + 16 * t + 16].astype(F32)
        ext[16:24] = low[K + 8 * t : K + 8 * t + 8]

        def rows_at(a):
            return ext[8 + a : 17 + a]

        tail[t] = warp(rows_at, RIM, *shift_lines(meta, META_SHIFT, frames, t))


def edge_kernel(rows, own, by_pair, by_middle, line, t_own, tile, part, out, t_up, top):
    frames = top.shape[0]
    up = from_above(lax.axis_index("slab"), by_pair[...], by_middle[...])
    meta_own = own[PK_META:PK_ALL].astype(F32)
    meta_up = up[PK_META:PK_ALL]
    row_own = meta_own[META_ROW : META_ROW + 1]
    row_up = meta_up[META_ROW : META_ROW + 1] - float(rows)
    tiles_own = t_own[...]
    tiles_up = placed_tiles(up[0 : 2 * K], meta_up[META_COL : META_COL + 1])
    t_up[...] = tiles_up
    out[0:8] = tile[...]
    write_tile(out, 8, gram(tiles_up, tiles_own, as_column(row_up), row_own), range(8))

    source, frame, first_kind = gather_source()
    found = jnp.zeros((8, LANES), F32)
    shape = (2 * RIM, LANES)
    rel_own = iota(shape, 0).astype(F32) - row_own - (iota(shape, 1) // K).astype(F32)
    rel_up = iota(shape, 0).astype(F32) - row_up - (iota(shape, 1) // K).astype(F32)
    for t in range(frames):
        at = PK_RAW_LAST + 16 * t
        first = PK_RAW_FIRST + 16 * t
        near = jnp.concatenate([up[at : at + 16], own[first : first + 16].astype(F32)], axis=0)
        zone = []
        for start, meta, row in ((8, meta_up, META_SHIFT), (16, meta_own, META_FIRST)):

            def rows_at(a, start=start):
                return near[start + a : start + a + RIM + 1]

            zone.append(warp(rows_at, RIM, *shift_lines(meta, row, frames, t)))
        image = jnp.concatenate(zone, axis=0).astype(BF16)
        top[t] = zone[1]
        sums = (project(image, tiles_own, rel_own) + part[t : t + 1], project(image, tiles_up, rel_up))
        both = [lane_pick(jnp.broadcast_to(x, (8, LANES)), source) for x in sums]
        found = jnp.where(frame == t, jnp.where(first_kind, both[0], both[1]), found)
    out[1:2] = found[0:1]
    out[3:4] = line[0:1]


def sweep_kernel(frames, slabs, gathered, out, sent, turned, g_ref):
    per = K // slabs
    lane = iota((8, LANES), 1)
    sub = iota((8, LANES), 0)
    quarter = lane // K
    slab = lane % slabs
    frame = (lane % K) // slabs
    me = lax.axis_index("slab")
    later = jnp.minimum(slab + 1, slabs - 1)
    here = gather_place(slab ^ me, slabs)
    there = gather_place(later ^ me, slabs)

    def turn(tile):
        arrays = []
        for n in range(2 // per):
            lines = []
            for lq in range(4):
                for h in range(per):
                    jh = n * per + h
                    lines.append(gathered[pl.ds(8 * tile + 2 * lq + jh, slabs, stride=16), :])
            at = (2 * tile + n) * LANES
            turned[at : at + LANES] = jnp.concatenate(lines, axis=0).T
            arrays.append(at)
        return (arrays * 2)[:2] if per == 2 else arrays

    def half_lane(jh):
        return jh * slabs if per == 2 else 0

    base_g = turn(0)
    base_x = turn(1)

    for jh in range(2):
        index = quarter * K + half_lane(jh) + here
        for j in range(16):
            n = 16 * jh + j
            rows = turned[base_x[jh] + 8 * j : base_x[jh] + 8 * j + 8]
            g_ref[8 * (K + n) : 8 * (K + n) + 8] = lane_pick(rows, index)
            rows = turned[base_g[jh] + 8 * j : base_g[jh] + 8 * j + 8]
            g_ref[8 * n : 8 * n + 8] = lane_pick(rows, index)
    for r in range(8):
        parts = [turned[pl.ds(base_g[0] + 64 * v + r, 8, stride=8), :] for v in range(2)]
        for oq in (2, 3):
            n = 8 * oq + r
            index = oq * K + half_lane(0) + here
            corner = jnp.where(quarter == 0, lane_pick(parts[0], index), lane_pick(parts[1], index))
            at = pl.ds(8 * n, 8)
            g_ref[at, :] = jnp.where(quarter < 2, corner, g_ref[at, :])
    inner = slab < slabs - 1
    for r in range(8):
        parts = [
            [turned[pl.ds(base_x[uh] + 64 * v + r, 8, stride=8), :] for v in range(2)]
            for uh in range(3 - per)
        ]
        for oq in range(4):
            if per == 2:
                index = oq * K + (quarter // 2) * slabs + there
                value = jnp.where(
                    quarter % 2 == 0, lane_pick(parts[0][0], index), lane_pick(parts[0][1], index)
                )
            else:
                index = oq * K + there
                value = lane_pick(parts[0][0], index)
                for uq in range(1, 4):
                    value = jnp.where(quarter == uq, lane_pick(parts[uq // 2][uq % 2], index), value)
            n = 2 * K + 8 * oq + r
            g_ref[8 * n : 8 * n + 8] = jnp.where(inner, value, 0.0)

    lanes_of = half_lane(1)
    states = []
    for nv in range(frames // per):
        found = []
        for line, kind, shifted in ((0, 0, False), (0, 1, True), (1, 0, False), (1, 1, False)):
            index = line * K + lanes_of + (there if shifted else here)
            value = jnp.zeros((8, LANES), F32)
            for lq in range(4):
                for h in range(per):
                    n = 8 * kind + 2 * lq + nv * per + h
                    rows = turned[base_g[1] + 8 * n : base_g[1] + 8 * n + 8]
                    value = jnp.where((quarter == lq) & (frame == h), lane_pick(rows, index), value)
            found.append(jnp.where(inner, value, 0.0) if shifted else value)
        states.append(found)
    norm = jnp.zeros((8, LANES), F32)
    for n in range(K):
        mine = (sub == n % 8) & (quarter == n // 8)
        norm = jnp.where(mine, g_ref[8 * n : 8 * n + 8], norm)
    inverse = 1.0 / norm
    block_of = states[0][3]
    inverses = [jnp.where(block_of == float(b), inverse, 0.0) for b in range(BLOCKS)]

    local = lane % K
    before = jnp.where(slab == 0, local, local - 1)
    after = jnp.where(inner, local + 1, local)

    def coupled(change):
        totals = [None] * 6
        for kind, place in enumerate((local, before, after)):
            for q in range(4):
                picked = lane_pick(change, q * K + place)
                for r in range(8):
                    n = kind * K + 8 * q + r
                    term = g_ref[8 * n : 8 * n + 8] * jnp.broadcast_to(picked[r : r + 1], (8, LANES))
                    slot = 2 * kind + r % 2
                    totals[slot] = term if totals[slot] is None else totals[slot] + term
        return (totals[0] + totals[1]) + ((totals[2] + totals[3]) + (totals[4] + totals[5]))

    p = [s[0] + s[1] - coupled(s[2]) for s in states]
    traces = [s[2] for s in states]

    def sweep(_, carry):
        p, traces = carry
        for b in range(BLOCKS):
            change = [x * inverses[b] for x in p]
            traces = [x + c for x, c in zip(traces, change)]
            p = [x - coupled(c) for x, c in zip(p, change)]
        return p, traces

    p, traces = lax.fori_loop(0, SWEEPS, sweep, (p, traces))

    mine = sub == lane % 8

    def lines_of(other):
        lines = []
        for t in range(frames):
            index = ((lane % K) // 8) * K + (t % per) * slabs + other
            value = jnp.where(mine, lane_pick(traces[t // per], index), 0.0)
            lines.append(jnp.sum(value, axis=0, keepdims=True))
        return lines

    def sums_of(lines):
        return [functools.reduce(jnp.add, lines), functools.reduce(jnp.add, [x * x for x in lines])]

    own = lines_of(me)
    lines = own + lines_of(jnp.maximum(me - 1, 0)) + lines_of(jnp.minimum(me + 1, slabs - 1))
    for n, line in enumerate(lines + sums_of(own)):
        out[n : n + 1] = line
    for n, line in enumerate(sums_of(lines_of(me ^ 1))):
        sent[n : n + 1] = line


def render(rel, values, tiles, groups=range(4)):
    mixed = jnp.concatenate([jnp.where(rel == float(4 * m), values, 0.0) for m in groups], axis=1)
    high = mixed.astype(BF16)
    low = (mixed - high.astype(F32)).astype(BF16)
    return jnp.dot(high, tiles, preferred_element_type=F32) + jnp.dot(
        low, tiles, preferred_element_type=F32
    )


def finish_kernel(own, by_pair, by_middle, corr, top, tail, lines, t_own, t_up, t_low, values, out):
    frames, rows, _ = corr.shape
    slab = lax.axis_index("slab")
    meta_up = from_above(slab, by_pair[PK_META:PK_ALL], by_middle[PK_META:PK_ALL])
    row_own = own[PK_META:PK_ALL].astype(F32)[META_ROW : META_ROW + 1]
    row_up = meta_up[META_ROW : META_ROW + 1] - float(rows)
    row_low = lines[0:1] + float(rows)
    y = (iota((rows, LANES), 0) + RIM).astype(F32)
    group = (iota((rows, LANES), 1) // K).astype(F32)
    rel_own = y - row_own - group
    rel_up = (y - row_up - group)[0:RIM]
    rel_low = (y - row_low - group)[rows - RIM : rows]
    half = t_low.shape[0]
    for t in range(frames):
        image = render(rel_own, values[t : t + 1], t_own[...])
        above = render(rel_up, values[frames + t : frames + t + 1], t_up[half:], (2, 3))
        below = render(rel_low, values[2 * frames + t : 2 * frames + t + 1], t_low[...], (0, 1))
        out[t, 0:RIM] = top[t].astype(BF16).astype(F32) - image[0:RIM] - above
        out[t, RIM : rows - RIM] = corr[t, RIM : rows - RIM].astype(F32) - image[RIM : rows - RIM]
        out[t, rows - RIM : rows] = tail[t].astype(BF16).astype(F32) - image[rows - RIM : rows] - below


def local_call(kernel, out_shape, scratch_shapes, flops, args, space=pltpu.VMEM):
    args = [pltpu.with_memory_space_constraint(x, space) for x in args]
    return pl.pallas_call(
        kernel,
        out_shape=out_shape,
        in_specs=[pl.BlockSpec(memory_space=space)] * len(args),
        out_specs=jax.tree.map(lambda _: VMEM_SPEC, out_shape),
        scratch_shapes=scratch_shapes,
        compiler_params=pltpu.CompilerParams(vmem_limit_bytes=VMEM_BYTES),
        cost_estimate=pl.CostEstimate(flops=flops, bytes_accessed=1 << 18, transcendentals=0),
    )(*args)


def shards(raw_movie, shifts, footprints, anchors, block_of, init_traces):
    frames, rows, cols = raw_movie.shape
    slabs = lax.axis_size("slab")
    frame_parts = lax.axis_size("frames")
    small = pltpu.VMEM((8, LANES), F32)
    tiles = pltpu.VMEM((TILE * K, LANES), BF16)
    half_tiles = pltpu.VMEM((TILE * K // 2, LANES), BF16)
    image = pltpu.VMEM((frames, rows, LANES), BF16)
    rim = pltpu.VMEM((frames, RIM, LANES), F32)
    extra_rows = K + 8 * frames + 16

    given = (
        raw_movie,
        shifts.transpose(0, 1, 3, 2),
        footprints.transpose(1, 2, 0),
        anchors.T,
        init_traces.T,
        block_of[None],
    )
    pack, raw, line = local_call(
        pack_kernel,
        (pltpu.VMEM((PK_ALL, LANES), BF16), image, small),
        [pltpu.VMEM(x.shape, x.dtype) for x in given[1:]] + [pltpu.SemaphoreType.DMA((len(given),))],
        10**8,
        given,
        space=pltpu.HBM,
    )
    by_pair, by_middle = [lax.ppermute(pack, "slab", route) for route in neighbour_routes(slabs)]

    tile, part, t_own, corr, extra = local_call(
        own_kernel,
        (small, small, tiles, image, pltpu.VMEM((extra_rows, LANES), F32)),
        [pltpu.VMEM((rows + 32, LANES), F32)],
        10**9,
        (pack, raw),
    )
    gathered, t_up, top = local_call(
        functools.partial(edge_kernel, rows),
        (pltpu.VMEM((16, LANES), F32), tiles, rim),
        [],
        10**9,
        (pack, by_pair, by_middle, line, t_own, tile, part),
    )
    for mask in gather_masks(slabs):
        route = [(i, i ^ mask) for i in range(slabs)]
        if mask == 3:
            other = lax.ppermute(jnp.concatenate([extra, gathered], axis=0), "slab", route)
            by_cross, other = other[:extra_rows], other[extra_rows:]
        else:
            other = lax.ppermute(gathered, "slab", route)
        gathered = jnp.concatenate([gathered, other], axis=0)

    t_low, tail, lines = local_call(
        low_kernel,
        (half_tiles, rim, small),
        [pltpu.VMEM((24, LANES), F32)],
        10**9,
        (pack, by_pair, by_middle, by_cross),
    )
    values, sent = local_call(
        functools.partial(sweep_kernel, frames, slabs),
        (small, small),
        [pltpu.VMEM((4 * LANES, LANES), F32), pltpu.VMEM((8 * 3 * K, LANES), F32)],
        10**9,
        (gathered,),
    )

    moments = values[3 * frames : 3 * frames + 2, :K]
    for hop in range(1, frame_parts):
        route = [
            (f * slabs + s, ((f + hop) % frame_parts) * slabs + (s ^ 1))
            for f in range(frame_parts)
            for s in range(slabs)
        ]
        moments = moments + lax.ppermute(sent, ("frames", "slab"), route)[:2, :K]

    residual = local_call(
        finish_kernel,
        jax.ShapeDtypeStruct((frames, rows, LANES), F32),
        [],
        10**9,
        (pack, by_pair, by_middle, corr, top, tail, lines, t_own, t_up, t_low, values),
    )

    frame_total = frames * frame_parts
    trace_mean = moments[0] / frame_total
    spread = moments[1] / frame_total - trace_mean * trace_mean
    traces_z = (values[:frames, :K] - trace_mean) / jnp.sqrt(spread + EPSILON)
    return traces_z.T, residual


def solution(mesh):
    in_specs = (
        P("frames", "slab", None),
        P(None, "frames", "slab", None),
        P("slab", None, None),
        P("slab", None),
        P("slab"),
        P("slab", "frames"),
    )
    out_specs = (P("slab", "frames"), P("frames", "slab", None))
    return jax.shard_map(shards, mesh=mesh, in_specs=in_specs, out_specs=out_specs, check_vma=False)
```

```python
import functools

import jax
import jax.numpy as jnp
from jax import lax
from jax.experimental import pallas as pl
from jax.experimental.pallas import tpu as pltpu
from jax.sharding import PartitionSpec as P

SHIFT = 3
PATCH_R = 32
BLOCKS = 4
SWEEPS = 3
TILE = 16
RIM = 8
LANES = 128
K = 32
GROUPS = LANES // K
WEIGHT_NEAR = 0.75
WEIGHT_FAR = 0.25
EPSILON = 1e-05
F32 = jnp.float32
BF16 = jnp.bfloat16

PK_RAW = 64
PK_META = 96
PK_ALL = 112
META_ROW = 0
META_COL = 1
META_SHIFT = 2
META_FIRST = 6
VMEM_BYTES = 8 << 20
VMEM_SPEC = pl.BlockSpec(memory_space=pltpu.VMEM)


def iota(shape, axis):
    return lax.broadcasted_iota(jnp.int32, shape, axis)


def lane_pick(values, index):
    return jnp.take_along_axis(values, index, axis=1, mode="promise_in_bounds")


def as_column(line):
    own = iota((K, LANES), 0) == iota((K, LANES), 1)
    return jnp.sum(jnp.where(own, line, 0.0), axis=1, keepdims=True)


def placed_tiles(tiles, col_line):
    col = as_column(col_line).astype(jnp.int32)
    offset = iota((K, LANES), 1) - col
    inside = (offset >= 0) & (offset < TILE)
    base = jnp.clip(offset, 0, TILE - 1)
    out = []
    for i in range(tiles.shape[0] // K * 8):
        half, part = divmod(i, 8)
        tile = tiles[half * K : (half + 1) * K].astype(F32)
        out.append(jnp.where(inside, lane_pick(tile, base + part * TILE), 0.0))
    return jnp.concatenate(out, axis=0).astype(BF16)


def dot_nt(a, b):
    return lax.dot_general(a, b, (((1,), (1,)), ((), ())), preferred_element_type=F32)


def fold_lanes(x):
    return (x + pltpu.roll(x, K, 1)) + (pltpu.roll(x, 2 * K, 1) + pltpu.roll(x, 3 * K, 1))


def gram(tiles_a, tiles_b, row_a, row_b):
    full = dot_nt(tiles_a, tiles_b)
    diff = row_a - row_b - (iota((K, LANES), 1) // K).astype(F32)
    total = jnp.zeros((K, LANES), F32)
    for q in range(-(TILE - 1), TILE):
        part = None
        for m in range(4):
            i = 4 * m - q
            if 0 <= i < TILE:
                block = full[i * K : (i + 1) * K, m * LANES : (m + 1) * LANES]
                part = block if part is None else part + block
        if part is not None:
            total = total + jnp.where(diff == float(q), part, 0.0)
    return fold_lanes(total)


def project(corr, tiles, rel):
    part = dot_nt(corr, tiles)
    total = jnp.zeros(rel.shape, F32)
    for m in range(4):
        total = total + jnp.where(rel == float(4 * m), part[:, m * LANES : (m + 1) * LANES], 0.0)
    return fold_lanes(jnp.sum(total, axis=0, keepdims=True))


def neighbour_routes(slabs):
    pairs = [(i, i ^ 1) for i in range(slabs)]
    ends = [(0, 1), (1, 2), (2, 0), (slabs - 3, slabs - 2), (slabs - 2, slabs - 1), (slabs - 1, slabs - 3)]
    middle = [p for i in range(3, slabs - 4, 2) for p in ((i, i + 1), (i + 1, i))]
    return pairs, ends + middle


def from_above(slab, by_pair, by_middle):
    found = jnp.where(slab % 2 == 1, by_pair.astype(F32), by_middle.astype(F32))
    return jnp.where(slab == 0, 0.0, found)


def below_part(pack, firsts):
    return jnp.concatenate([pack[0:K].astype(F32), *firsts, pack[PK_META:PK_ALL].astype(F32)], axis=0)


def received_below(pack, frames):
    firsts = [pack[PK_RAW + 16 * t : PK_RAW + 16 * t + 16].astype(F32)[0:8] for t in range(frames)]
    return below_part(pack, firsts)


def write_edge_rows(out, raw, to_below):
    frames, rows, _ = raw.shape
    for t in range(frames):
        last, first = raw[t, rows - 16 : rows].astype(F32), raw[t, 0:16].astype(F32)
        out[PK_RAW + 16 * t : PK_RAW + 16 * t + 16] = jnp.where(to_below, last, first).astype(BF16)


def from_below(slab, slabs, by_pair, by_middle, by_cross):
    odd = jnp.where((slab == 1) | (slab == slabs - 3), by_cross, by_middle)
    found = jnp.where(slab % 2 == 0, by_pair, odd)
    return jnp.where(slab == slabs - 1, 0.0, found)


def gather_masks(slabs):
    bits = slabs.bit_length() - 1
    return [(1 << b) | 1 for b in range(bits - 1, 0, -1)] + [1]


def gather_place(diff, slabs):
    bits = slabs.bit_length() - 1
    odd = diff & 1
    place = jnp.zeros_like(diff)
    for r in range(bits - 1):
        bit = (diff >> (bits - 1 - r)) & 1
        place = place + bit * (1 << r)
        odd = odd ^ bit
    return place + odd * (1 << (bits - 1))


def gather_source():
    place = iota((8, LANES), 1)
    return 8 * ((place // 16) % 4) + place % 8, (place // 8) % 2, place < LANES // 2


def pack_kernel(*refs):
    count = 6
    given, (out, raw, line) = refs[:count], refs[count : count + 3]
    held = refs[count + 3 : 2 * count + 2]
    sems = refs[-1]
    shifts, tiles, anchors, init, block_of = held
    copies = [
        pltpu.make_async_copy(source, target, sems.at[n])
        for n, (source, target) in enumerate(zip(given, (raw, *held)))
    ]
    for copy in copies:
        copy.start()
    for copy in copies:
        copy.wait()
    frames, rows, _ = raw.shape
    last = rows // PATCH_R - 1
    slab = lax.axis_index("slab")
    base = slab * rows - RIM
    for half in range(2):
        part = tiles[8 * half : 8 * half + 8].astype(F32).reshape(LANES, K)
        out[K * half : K * half + K] = part.T.astype(BF16)
    write_edge_rows(out, raw, slab % 2 == 1)
    places = jnp.concatenate([anchors[...].astype(F32)] * GROUPS, axis=1)
    sub = iota((16, LANES), 0)
    meta = jnp.where(sub == META_COL, places[1:2], 0.0)
    meta = jnp.where(sub == META_ROW, places[0:1] - base.astype(F32), meta)
    for t in range(frames):
        for axis in range(2):
            pair = shifts[axis, t].astype(F32)
            for place, patch in ((META_SHIFT, last), (META_FIRST, 0)):
                meta = jnp.where(sub == place + axis * frames + t, pair[:, patch : patch + 1], meta)
    out[PK_META:PK_ALL] = meta.astype(BF16)
    source, frame, first_kind = gather_source()
    inits = jnp.concatenate([init[...]] * GROUPS, axis=1)
    blocks = jnp.concatenate([block_of[...].astype(F32)] * GROUPS, axis=1)
    found = jnp.zeros((8, LANES), F32)
    for t in range(frames):
        both = [lane_pick(jnp.broadcast_to(x, (8, LANES)), source) for x in (inits[t : t + 1], blocks)]
        found = jnp.where(frame == t, jnp.where(first_kind, both[0], both[1]), found)
    line[...] = found


def write_tile(out, first, mat, rows):
    lane = iota((K, LANES), 1)
    own = lane // 8 == iota((K, LANES), 0) % 16
    for lq in range(4):
        part = jnp.where(own, lane_pick(mat, 8 * lq + lane % 8), 0.0)
        for jh in range(2):
            if 2 * lq + jh in rows:
                out[first + 2 * lq + jh : first + 2 * lq + jh + 1] = jnp.sum(
                    part[16 * jh : 16 * jh + 16], axis=0, keepdims=True
                )


def warp(rows_at, count, a_line, c_line):
    both = jnp.zeros((count, LANES), F32)
    for a in range(-SHIFT, SHIFT + 1):
        window = rows_at(a)
        blend = WEIGHT_NEAR * window[0:count] + WEIGHT_FAR * window[1 : count + 1]
        both = jnp.where(a_line == float(a), blend, both)
    place = iota((count, LANES), 1) + c_line.astype(jnp.int32)
    moved = lane_pick(both, jnp.clip(place, 0, LANES - 1))
    return jnp.where((place >= 0) & (place < LANES), moved, 0.0)


def shift_lines(meta, row, frames, t):
    return meta[row + t : row + t + 1], meta[row + frames + t : row + frames + t + 1]


def own_kernel(own, raw, pair, tile, part, t_own, corr, extra, ext):
    frames, rows, _ = raw.shape
    slab = lax.axis_index("slab")
    is_last = slab == lax.axis_size("slab") - 1
    pair[0:PK_RAW] = own[0:PK_RAW]
    pair[PK_META:PK_ALL] = own[PK_META:PK_ALL]
    write_edge_rows(pair, raw, slab % 2 == 0)
    extra[...] = below_part(own[...], [raw[t, 0:16].astype(F32)[0:8] for t in range(frames)])
    meta = own[PK_META:PK_ALL].astype(F32)
    row = meta[META_ROW : META_ROW + 1]
    tiles = placed_tiles(own[0 : 2 * K], meta[META_COL : META_COL + 1])
    t_own[...] = tiles
    tile[...] = jnp.zeros((8, LANES), F32)
    part[...] = jnp.zeros((8, LANES), F32)
    write_tile(tile, 0, gram(tiles, tiles, as_column(row), row), (0, 2, 4, 5, 6, 7))
    y = iota((rows, LANES), 0)
    keep = (y >= RIM) & ((y < rows - RIM) | is_last)
    rel = (y + RIM).astype(F32) - row - (iota((rows, LANES), 1) // K).astype(F32)
    for t in range(frames):
        ext[0:16] = jnp.zeros((16, LANES), F32)
        ext[16 : 16 + rows] = raw[t].astype(F32)
        ext[16 + rows : 32 + rows] = jnp.zeros((16, LANES), F32)
        parts = []
        for p, row_of in ((0, META_FIRST), (1, META_SHIFT)):

            def rows_at(a, first=16 + p * PATCH_R):
                return ext[first + a : first + a + PATCH_R + 1]

            parts.append(warp(rows_at, PATCH_R, *shift_lines(meta, row_of, frames, t)))
        image = jnp.concatenate(parts, axis=0)
        corr[t] = image.astype(BF16)
        part[t : t + 1] = project(jnp.where(keep, image, 0.0).astype(BF16), tiles, rel)


def low_kernel(own, raw, by_pair, by_middle, by_cross, tiles, tail, lines, ext):
    frames, rows, _ = raw.shape
    low = from_below(
        lax.axis_index("slab"),
        lax.axis_size("slab"),
        received_below(by_pair[...], frames),
        received_below(by_middle[...], frames),
        by_cross[...],
    )
    meta = own[PK_META:PK_ALL].astype(F32)
    meta_low = low[K + 8 * frames :]
    tiles[...] = placed_tiles(low[0:K], meta_low[META_COL : META_COL + 1])
    lines[...] = jnp.broadcast_to(meta_low[META_ROW : META_ROW + 1], (8, LANES))
    for t in range(frames):
        ext[0:16] = raw[t, rows - 16 : rows].astype(F32)
        ext[16:24] = low[K + 8 * t : K + 8 * t + 8]

        def rows_at(a):
            return ext[8 + a : 17 + a]

        tail[t] = warp(rows_at, RIM, *shift_lines(meta, META_SHIFT, frames, t))


def edge_kernel(own, raw, by_pair, by_middle, line, t_own, tile, part, out, t_up, top):
    frames, rows, _ = raw.shape
    up = from_above(lax.axis_index("slab"), by_pair[...], by_middle[...])
    meta_own = own[PK_META:PK_ALL].astype(F32)
    meta_up = up[PK_META:PK_ALL]
    row_own = meta_own[META_ROW : META_ROW + 1]
    row_up = meta_up[META_ROW : META_ROW + 1] - float(rows)
    tiles_own = t_own[...]
    tiles_up = placed_tiles(up[0 : 2 * K], meta_up[META_COL : META_COL + 1])
    t_up[...] = tiles_up
    out[0:8] = tile[...]
    write_tile(out, 8, gram(tiles_up, tiles_own, as_column(row_up), row_own), range(8))

    source, frame, first_kind = gather_source()
    found = jnp.zeros((8, LANES), F32)
    shape = (2 * RIM, LANES)
    rel_own = iota(shape, 0).astype(F32) - row_own - (iota(shape, 1) // K).astype(F32)
    rel_up = iota(shape, 0).astype(F32) - row_up - (iota(shape, 1) // K).astype(F32)
    for t in range(frames):
        at = PK_RAW + 16 * t
        near = jnp.concatenate([up[at : at + 16], raw[t, 0:16].astype(F32)], axis=0)
        zone = []
        for start, meta, row in ((8, meta_up, META_SHIFT), (16, meta_own, META_FIRST)):

            def rows_at(a, start=start):
                return near[start + a : start + a + RIM + 1]

            zone.append(warp(rows_at, RIM, *shift_lines(meta, row, frames, t)))
        image = jnp.concatenate(zone, axis=0).astype(BF16)
        top[t] = zone[1]
        sums = (project(image, tiles_own, rel_own) + part[t : t + 1], project(image, tiles_up, rel_up))
        both = [lane_pick(jnp.broadcast_to(x, (8, LANES)), source) for x in sums]
        found = jnp.where(frame == t, jnp.where(first_kind, both[0], both[1]), found)
    out[1:2] = found[0:1]
    out[3:4] = line[0:1]


def sweep_kernel(frames, slabs, gathered, out, sent, turned, g_ref):
    per = K // slabs
    lane = iota((8, LANES), 1)
    sub = iota((8, LANES), 0)
    quarter = lane // K
    slab = lane % slabs
    frame = (lane % K) // slabs
    me = lax.axis_index("slab")
    later = jnp.minimum(slab + 1, slabs - 1)
    here = gather_place(slab ^ me, slabs)
    there = gather_place(later ^ me, slabs)

    def turn(tile):
        arrays = []
        for n in range(2 // per):
            lines = []
            for lq in range(4):
                for h in range(per):
                    jh = n * per + h
                    lines.append(gathered[pl.ds(8 * tile + 2 * lq + jh, slabs, stride=16), :])
            at = (2 * tile + n) * LANES
            turned[at : at + LANES] = jnp.concatenate(lines, axis=0).T
            arrays.append(at)
        return (arrays * 2)[:2] if per == 2 else arrays

    def half_lane(jh):
        return jh * slabs if per == 2 else 0

    base_g = turn(0)
    base_x = turn(1)

    for jh in range(2):
        index = quarter * K + half_lane(jh) + here
        for j in range(16):
            n = 16 * jh + j
            rows = turned[base_x[jh] + 8 * j : base_x[jh] + 8 * j + 8]
            g_ref[8 * (K + n) : 8 * (K + n) + 8] = lane_pick(rows, index)
            rows = turned[base_g[jh] + 8 * j : base_g[jh] + 8 * j + 8]
            g_ref[8 * n : 8 * n + 8] = lane_pick(rows, index)
    for r in range(8):
        parts = [turned[pl.ds(base_g[0] + 64 * v + r, 8, stride=8), :] for v in range(2)]
        for oq in (2, 3):
            n = 8 * oq + r
            index = oq * K + half_lane(0) + here
            corner = jnp.where(quarter == 0, lane_pick(parts[0], index), lane_pick(parts[1], index))
            at = pl.ds(8 * n, 8)
            g_ref[at, :] = jnp.where(quarter < 2, corner, g_ref[at, :])
    inner = slab < slabs - 1
    for r in range(8):
        parts = [
            [turned[pl.ds(base_x[uh] + 64 * v + r, 8, stride=8), :] for v in range(2)]
            for uh in range(3 - per)
        ]
        for oq in range(4):
            if per == 2:
                index = oq * K + (quarter // 2) * slabs + there
                value = jnp.where(
                    quarter % 2 == 0, lane_pick(parts[0][0], index), lane_pick(parts[0][1], index)
                )
            else:
                index = oq * K + there
                value = lane_pick(parts[0][0], index)
                for uq in range(1, 4):
                    value = jnp.where(quarter == uq, lane_pick(parts[uq // 2][uq % 2], index), value)
            n = 2 * K + 8 * oq + r
            g_ref[8 * n : 8 * n + 8] = jnp.where(inner, value, 0.0)

    lanes_of = half_lane(1)
    states = []
    for nv in range(frames // per):
        found = []
        for line, kind, shifted in ((0, 0, False), (0, 1, True), (1, 0, False), (1, 1, False)):
            index = line * K + lanes_of + (there if shifted else here)
            value = jnp.zeros((8, LANES), F32)
            for lq in range(4):
                for h in range(per):
                    n = 8 * kind + 2 * lq + nv * per + h
                    rows = turned[base_g[1] + 8 * n : base_g[1] + 8 * n + 8]
                    value = jnp.where((quarter == lq) & (frame == h), lane_pick(rows, index), value)
            found.append(jnp.where(inner, value, 0.0) if shifted else value)
        states.append(found)
    norm = jnp.zeros((8, LANES), F32)
    for n in range(K):
        mine = (sub == n % 8) & (quarter == n // 8)
        norm = jnp.where(mine, g_ref[8 * n : 8 * n + 8], norm)
    inverse = 1.0 / norm
    block_of = states[0][3]
    inverses = [jnp.where(block_of == float(b), inverse, 0.0) for b in range(BLOCKS)]

    local = lane % K
    before = jnp.where(slab == 0, local, local - 1)
    after = jnp.where(inner, local + 1, local)

    def coupled(change):
        totals = [None] * 6
        for kind, place in enumerate((local, before, after)):
            for q in range(4):
                picked = lane_pick(change, q * K + place)
                for r in range(8):
                    n = kind * K + 8 * q + r
                    term = g_ref[8 * n : 8 * n + 8] * jnp.broadcast_to(picked[r : r + 1], (8, LANES))
                    slot = 2 * kind + r % 2
                    totals[slot] = term if totals[slot] is None else totals[slot] + term
        return (totals[0] + totals[1]) + ((totals[2] + totals[3]) + (totals[4] + totals[5]))

    p = [s[0] + s[1] - coupled(s[2]) for s in states]
    traces = [s[2] for s in states]

    def sweep(_, carry):
        p, traces = carry
        for b in range(BLOCKS):
            change = [x * inverses[b] for x in p]
            traces = [x + c for x, c in zip(traces, change)]
            p = [x - coupled(c) for x, c in zip(p, change)]
        return p, traces

    p, traces = lax.fori_loop(0, SWEEPS, sweep, (p, traces))

    mine = sub == lane % 8

    def lines_of(other):
        lines = []
        for t in range(frames):
            index = ((lane % K) // 8) * K + (t % per) * slabs + other
            value = jnp.where(mine, lane_pick(traces[t // per], index), 0.0)
            lines.append(jnp.sum(value, axis=0, keepdims=True))
        return lines

    def sums_of(lines):
        return [functools.reduce(jnp.add, lines), functools.reduce(jnp.add, [x * x for x in lines])]

    own = lines_of(me)
    lines = own + lines_of(jnp.maximum(me - 1, 0)) + lines_of(jnp.minimum(me + 1, slabs - 1))
    for n, line in enumerate(lines + sums_of(own)):
        out[n : n + 1] = line
    for n, line in enumerate(sums_of(lines_of(me ^ 1))):
        sent[n : n + 1] = line


def render(rel, values, tiles, groups=range(4)):
    mixed = jnp.concatenate([jnp.where(rel == float(4 * m), values, 0.0) for m in groups], axis=1)
    high = mixed.astype(BF16)
    low = (mixed - high.astype(F32)).astype(BF16)
    return jnp.dot(high, tiles, preferred_element_type=F32) + jnp.dot(
        low, tiles, preferred_element_type=F32
    )


def finish_kernel(own, by_pair, by_middle, corr, top, tail, lines, t_own, t_up, t_low, values, out):
    frames, rows, _ = corr.shape
    slab = lax.axis_index("slab")
    meta_up = from_above(slab, by_pair[PK_META:PK_ALL], by_middle[PK_META:PK_ALL])
    row_own = own[PK_META:PK_ALL].astype(F32)[META_ROW : META_ROW + 1]
    row_up = meta_up[META_ROW : META_ROW + 1] - float(rows)
    row_low = lines[0:1] + float(rows)
    y = (iota((rows, LANES), 0) + RIM).astype(F32)
    group = (iota((rows, LANES), 1) // K).astype(F32)
    rel_own = y - row_own - group
    rel_up = (y - row_up - group)[0:RIM]
    rel_low = (y - row_low - group)[rows - RIM : rows]
    half = t_low.shape[0]
    for t in range(frames):
        image = render(rel_own, values[t : t + 1], t_own[...])
        above = render(rel_up, values[frames + t : frames + t + 1], t_up[half:], (2, 3))
        below = render(rel_low, values[2 * frames + t : 2 * frames + t + 1], t_low[...], (0, 1))
        out[t, 0:RIM] = top[t].astype(BF16).astype(F32) - image[0:RIM] - above
        out[t, RIM : rows - RIM] = corr[t, RIM : rows - RIM].astype(F32) - image[RIM : rows - RIM]
        out[t, rows - RIM : rows] = tail[t].astype(BF16).astype(F32) - image[rows - RIM : rows] - below


def local_call(kernel, out_shape, scratch_shapes, flops, args, space=pltpu.VMEM):
    args = [pltpu.with_memory_space_constraint(x, space) for x in args]
    return pl.pallas_call(
        kernel,
        out_shape=out_shape,
        in_specs=[pl.BlockSpec(memory_space=space)] * len(args),
        out_specs=jax.tree.map(lambda _: VMEM_SPEC, out_shape),
        scratch_shapes=scratch_shapes,
        compiler_params=pltpu.CompilerParams(vmem_limit_bytes=VMEM_BYTES),
        cost_estimate=pl.CostEstimate(flops=flops, bytes_accessed=1 << 18, transcendentals=0),
    )(*args)


def shards(raw_movie, shifts, footprints, anchors, block_of, init_traces):
    frames, rows, cols = raw_movie.shape
    slabs = lax.axis_size("slab")
    frame_parts = lax.axis_size("frames")
    small = pltpu.VMEM((8, LANES), F32)
    tiles = pltpu.VMEM((TILE * K, LANES), BF16)
    half_tiles = pltpu.VMEM((TILE * K // 2, LANES), BF16)
    image = pltpu.VMEM((frames, rows, LANES), BF16)
    rim = pltpu.VMEM((frames, RIM, LANES), F32)
    extra_rows = K + 8 * frames + 16

    given = (
        raw_movie,
        shifts.transpose(0, 1, 3, 2),
        footprints.transpose(1, 2, 0),
        anchors.T,
        init_traces.T,
        block_of[None],
    )
    pack, raw, line = local_call(
        pack_kernel,
        (pltpu.VMEM((PK_ALL, LANES), BF16), image, small),
        [pltpu.VMEM(x.shape, x.dtype) for x in given[1:]] + [pltpu.SemaphoreType.DMA((len(given),))],
        10**8,
        given,
        space=pltpu.HBM,
    )
    pairs, middle = neighbour_routes(slabs)
    by_middle = lax.ppermute(pack, "slab", middle)

    pair, tile, part, t_own, corr, extra = local_call(
        own_kernel,
        (pltpu.VMEM((PK_ALL, LANES), BF16), small, small, tiles, image, pltpu.VMEM((extra_rows, LANES), F32)),
        [pltpu.VMEM((rows + 32, LANES), F32)],
        10**9,
        (pack, raw),
    )
    by_pair = lax.ppermute(pair, "slab", pairs)
    gathered, t_up, top = local_call(
        edge_kernel,
        (pltpu.VMEM((16, LANES), F32), tiles, rim),
        [],
        10**9,
        (pack, raw, by_pair, by_middle, line, t_own, tile, part),
    )
    for mask in gather_masks(slabs):
        route = [(i, i ^ mask) for i in range(slabs)]
        if mask == 3:
            other = lax.ppermute(jnp.concatenate([extra, gathered], axis=0), "slab", route)
            by_cross, other = other[:extra_rows], other[extra_rows:]
        else:
            other = lax.ppermute(gathered, "slab", route)
        gathered = jnp.concatenate([gathered, other], axis=0)

    t_low, tail, lines = local_call(
        low_kernel,
        (half_tiles, rim, small),
        [pltpu.VMEM((24, LANES), F32)],
        10**9,
        (pack, raw, by_pair, by_middle, by_cross),
    )
    values, sent = local_call(
        functools.partial(sweep_kernel, frames, slabs),
        (small, small),
        [pltpu.VMEM((4 * LANES, LANES), F32), pltpu.VMEM((8 * 3 * K, LANES), F32)],
        10**9,
        (gathered,),
    )

    moments = values[3 * frames : 3 * frames + 2, :K]
    for hop in range(1, frame_parts):
        route = [
            (f * slabs + s, ((f + hop) % frame_parts) * slabs + (s ^ 1))
            for f in range(frame_parts)
            for s in range(slabs)
        ]
        moments = moments + lax.ppermute(sent, ("frames", "slab"), route)[:2, :K]

    residual = local_call(
        finish_kernel,
        jax.ShapeDtypeStruct((frames, rows, LANES), F32),
        [],
        10**9,
        (pack, by_pair, by_middle, corr, top, tail, lines, t_own, t_up, t_low, values),
    )

    frame_total = frames * frame_parts
    trace_mean = moments[0] / frame_total
    spread = moments[1] / frame_total - trace_mean * trace_mean
    traces_z = (values[:frames, :K] - trace_mean) / jnp.sqrt(spread + EPSILON)
    return traces_z.T, residual


def solution(mesh):
    in_specs = (
        P("frames", "slab", None),
        P(None, "frames", "slab", None),
        P("slab", None, None),
        P("slab", None),
        P("slab"),
        P("slab", "frames"),
    )
    out_specs = (P("slab", "frames"), P("frames", "slab", None))
    return jax.shard_map(shards, mesh=mesh, in_specs=in_specs, out_specs=out_specs, check_vma=False)
```

```python
import functools

import jax
import jax.numpy as jnp
from jax import lax
from jax.experimental import pallas as pl
from jax.experimental.pallas import tpu as pltpu
from jax.sharding import PartitionSpec as P

SHIFT = 3
PATCH_R = 32
BLOCKS = 4
SWEEPS = 3
TILE = 16
RIM = 8
LANES = 128
K = 32
GROUPS = LANES // K
WEIGHT_NEAR = 0.75
WEIGHT_FAR = 0.25
EPSILON = 1e-05
F32 = jnp.float32
BF16 = jnp.bfloat16

PK_RAW = 64
PK_META = 96
PK_ALL = 112
META_ROW = 0
META_COL = 1
META_SHIFT = 2
META_FIRST = 6
VMEM_BYTES = 8 << 20
VMEM_SPEC = pl.BlockSpec(memory_space=pltpu.VMEM)


def iota(shape, axis):
    return lax.broadcasted_iota(jnp.int32, shape, axis)


def lane_pick(values, index):
    return jnp.take_along_axis(values, index, axis=1, mode="promise_in_bounds")


def as_column(line):
    own = iota((K, LANES), 0) == iota((K, LANES), 1)
    return jnp.sum(jnp.where(own, line, 0.0), axis=1, keepdims=True)


def placed_tiles(tiles, col_line):
    col = as_column(col_line).astype(jnp.int32)
    offset = iota((K, LANES), 1) - col
    inside = (offset >= 0) & (offset < TILE)
    base = jnp.clip(offset, 0, TILE - 1)
    out = []
    for i in range(tiles.shape[0] // K * 8):
        half, part = divmod(i, 8)
        tile = tiles[half * K : (half + 1) * K].astype(F32)
        out.append(jnp.where(inside, lane_pick(tile, base + part * TILE), 0.0))
    return jnp.concatenate(out, axis=0).astype(BF16)


def dot_nt(a, b):
    return lax.dot_general(a, b, (((1,), (1,)), ((), ())), preferred_element_type=F32)


def fold_lanes(x):
    return (x + pltpu.roll(x, K, 1)) + (pltpu.roll(x, 2 * K, 1) + pltpu.roll(x, 3 * K, 1))


def gram(tiles_a, tiles_b, row_a, row_b):
    full = dot_nt(tiles_a, tiles_b)
    diff = row_a - row_b - (iota((K, LANES), 1) // K).astype(F32)
    total = jnp.zeros((K, LANES), F32)
    for q in range(-(TILE - 1), TILE):
        part = None
        for m in range(4):
            i = 4 * m - q
            if 0 <= i < TILE:
                block = full[i * K : (i + 1) * K, m * LANES : (m + 1) * LANES]
                part = block if part is None else part + block
        if part is not None:
            total = total + jnp.where(diff == float(q), part, 0.0)
    return fold_lanes(total)


def project(corr, tiles, rel):
    part = dot_nt(corr, tiles)
    total = jnp.zeros(rel.shape, F32)
    for m in range(4):
        total = total + jnp.where(rel == float(4 * m), part[:, m * LANES : (m + 1) * LANES], 0.0)
    return fold_lanes(jnp.sum(total, axis=0, keepdims=True))


def neighbour_routes(slabs):
    pairs = [(i, i ^ 1) for i in range(slabs)]
    ends = [(0, 1), (1, 2), (2, 0), (slabs - 3, slabs - 2), (slabs - 2, slabs - 1), (slabs - 1, slabs - 3)]
    middle = [p for i in range(3, slabs - 4, 2) for p in ((i, i + 1), (i + 1, i))]
    return pairs, ends + middle


def from_above(slab, by_pair, by_middle):
    found = jnp.where(slab % 2 == 1, by_pair.astype(F32), by_middle.astype(F32))
    return jnp.where(slab == 0, 0.0, found)


def below_part(pack, firsts):
    return jnp.concatenate([pack[0:K].astype(F32), *firsts, pack[PK_META:PK_ALL].astype(F32)], axis=0)


def received_below(pack, frames):
    firsts = [pack[PK_RAW + 16 * t : PK_RAW + 16 * t + 16].astype(F32)[0:8] for t in range(frames)]
    return below_part(pack, firsts)


def write_edge_rows(out, raw, to_below):
    frames, rows, _ = raw.shape
    for t in range(frames):
        last, first = raw[t, rows - 16 : rows].astype(F32), raw[t, 0:16].astype(F32)
        out[PK_RAW + 16 * t : PK_RAW + 16 * t + 16] = jnp.where(to_below, last, first).astype(BF16)


def from_below(slab, slabs, by_pair, by_middle, by_cross):
    odd = jnp.where((slab == 1) | (slab == slabs - 3), by_cross, by_middle)
    found = jnp.where(slab % 2 == 0, by_pair, odd)
    return jnp.where(slab == slabs - 1, 0.0, found)


def gather_masks(slabs):
    bits = slabs.bit_length() - 1
    return [(1 << b) | 1 for b in range(bits - 1, 0, -1)] + [1]


def gather_place(diff, slabs):
    bits = slabs.bit_length() - 1
    odd = diff & 1
    place = jnp.zeros_like(diff)
    for r in range(bits - 1):
        bit = (diff >> (bits - 1 - r)) & 1
        place = place + bit * (1 << r)
        odd = odd ^ bit
    return place + odd * (1 << (bits - 1))


def gather_source():
    place = iota((8, LANES), 1)
    return 8 * ((place // 16) % 4) + place % 8, (place // 8) % 2, place < LANES // 2


def pack_kernel(*refs):
    count = 6
    given, (out, pair, raw, line) = refs[:count], refs[count : count + 4]
    held = refs[count + 4 : 2 * count + 3]
    sems = refs[-1]
    shifts, tiles, anchors, init, block_of = held
    copies = [
        pltpu.make_async_copy(source, target, sems.at[n])
        for n, (source, target) in enumerate(zip(given, (raw, *held)))
    ]
    for copy in copies:
        copy.start()
    for copy in copies:
        copy.wait()
    frames, rows, _ = raw.shape
    last = rows // PATCH_R - 1
    slab = lax.axis_index("slab")
    base = slab * rows - RIM
    for half in range(2):
        part = tiles[8 * half : 8 * half + 8].astype(F32).reshape(LANES, K)
        out[K * half : K * half + K] = part.T.astype(BF16)
    write_edge_rows(out, raw, slab % 2 == 1)
    places = jnp.concatenate([anchors[...].astype(F32)] * GROUPS, axis=1)
    sub = iota((16, LANES), 0)
    meta = jnp.where(sub == META_COL, places[1:2], 0.0)
    meta = jnp.where(sub == META_ROW, places[0:1] - base.astype(F32), meta)
    for t in range(frames):
        for axis in range(2):
            moves = shifts[axis, t].astype(F32)
            for place, patch in ((META_SHIFT, last), (META_FIRST, 0)):
                meta = jnp.where(sub == place + axis * frames + t, moves[:, patch : patch + 1], meta)
    out[PK_META:PK_ALL] = meta.astype(BF16)
    pair[0:PK_RAW] = out[0:PK_RAW]
    write_edge_rows(pair, raw, slab % 2 == 0)
    pair[PK_META:PK_ALL] = meta.astype(BF16)
    source, frame, first_kind = gather_source()
    inits = jnp.concatenate([init[...]] * GROUPS, axis=1)
    blocks = jnp.concatenate([block_of[...].astype(F32)] * GROUPS, axis=1)
    found = jnp.zeros((8, LANES), F32)
    for t in range(frames):
        both = [lane_pick(jnp.broadcast_to(x, (8, LANES)), source) for x in (inits[t : t + 1], blocks)]
        found = jnp.where(frame == t, jnp.where(first_kind, both[0], both[1]), found)
    line[...] = found


def write_tile(out, first, mat, rows):
    lane = iota((K, LANES), 1)
    own = lane // 8 == iota((K, LANES), 0) % 16
    for lq in range(4):
        part = jnp.where(own, lane_pick(mat, 8 * lq + lane % 8), 0.0)
        for jh in range(2):
            if 2 * lq + jh in rows:
                out[first + 2 * lq + jh : first + 2 * lq + jh + 1] = jnp.sum(
                    part[16 * jh : 16 * jh + 16], axis=0, keepdims=True
                )


def warp(rows_at, count, a_line, c_line):
    both = jnp.zeros((count, LANES), F32)
    for a in range(-SHIFT, SHIFT + 1):
        window = rows_at(a)
        blend = WEIGHT_NEAR * window[0:count] + WEIGHT_FAR * window[1 : count + 1]
        both = jnp.where(a_line == float(a), blend, both)
    place = iota((count, LANES), 1) + c_line.astype(jnp.int32)
    moved = lane_pick(both, jnp.clip(place, 0, LANES - 1))
    return jnp.where((place >= 0) & (place < LANES), moved, 0.0)


def shift_lines(meta, row, frames, t):
    return meta[row + t : row + t + 1], meta[row + frames + t : row + frames + t + 1]


def own_kernel(own, raw, tile, part, t_own, corr, extra, ext):
    frames, rows, _ = raw.shape
    slab = lax.axis_index("slab")
    is_last = slab == lax.axis_size("slab") - 1
    extra[...] = below_part(own[...], [raw[t, 0:16].astype(F32)[0:8] for t in range(frames)]).astype(BF16)
    meta = own[PK_META:PK_ALL].astype(F32)
    row = meta[META_ROW : META_ROW + 1]
    tiles = placed_tiles(own[0 : 2 * K], meta[META_COL : META_COL + 1])
    t_own[...] = tiles
    tile[...] = jnp.zeros((8, LANES), F32)
    part[...] = jnp.zeros((8, LANES), F32)
    write_tile(tile, 0, gram(tiles, tiles, as_column(row), row), (0, 2, 4, 5, 6, 7))
    y = iota((rows, LANES), 0)
    keep = (y >= RIM) & ((y < rows - RIM) | is_last)
    rel = (y + RIM).astype(F32) - row - (iota((rows, LANES), 1) // K).astype(F32)
    for t in range(frames):
        ext[0:16] = jnp.zeros((16, LANES), F32)
        ext[16 : 16 + rows] = raw[t].astype(F32)
        ext[16 + rows : 32 + rows] = jnp.zeros((16, LANES), F32)
        parts = []
        for p, row_of in ((0, META_FIRST), (1, META_SHIFT)):

            def rows_at(a, first=16 + p * PATCH_R):
                return ext[first + a : first + a + PATCH_R + 1]

            parts.append(warp(rows_at, PATCH_R, *shift_lines(meta, row_of, frames, t)))
        image = jnp.concatenate(parts, axis=0)
        corr[t] = image.astype(BF16)
        part[t : t + 1] = project(jnp.where(keep, image, 0.0).astype(BF16), tiles, rel)


def low_kernel(own, raw, by_middle, by_pair, by_cross, tiles, tail, lines, ext):
    frames, rows, _ = raw.shape
    low = from_below(
        lax.axis_index("slab"),
        lax.axis_size("slab"),
        received_below(by_pair[...], frames),
        received_below(by_middle[...], frames),
        by_cross[...].astype(F32),
    )
    meta = own[PK_META:PK_ALL].astype(F32)
    meta_low = low[K + 8 * frames :]
    tiles[...] = placed_tiles(low[0:K], meta_low[META_COL : META_COL + 1])
    lines[...] = jnp.broadcast_to(meta_low[META_ROW : META_ROW + 1], (8, LANES))
    for t in range(frames):
        ext[0:16] = raw[t, rows - 16 : rows].astype(F32)
        ext[16:24] = low[K + 8 * t : K + 8 * t + 8]

        def rows_at(a):
            return ext[8 + a : 17 + a]

        tail[t] = warp(rows_at, RIM, *shift_lines(meta, META_SHIFT, frames, t))


def edge_kernel(own, raw, by_middle, by_pair, line, t_own, tile, part, out, t_up, top):
    frames, rows, _ = raw.shape
    up = from_above(lax.axis_index("slab"), by_pair[...], by_middle[...])
    meta_own = own[PK_META:PK_ALL].astype(F32)
    meta_up = up[PK_META:PK_ALL]
    row_own = meta_own[META_ROW : META_ROW + 1]
    row_up = meta_up[META_ROW : META_ROW + 1] - float(rows)
    tiles_own = t_own[...]
    tiles_up = placed_tiles(up[0 : 2 * K], meta_up[META_COL : META_COL + 1])
    t_up[...] = tiles_up
    out[0:8] = tile[...]
    write_tile(out, 8, gram(tiles_up, tiles_own, as_column(row_up), row_own), range(8))

    source, frame, first_kind = gather_source()
    found = jnp.zeros((8, LANES), F32)
    shape = (2 * RIM, LANES)
    rel_own = iota(shape, 0).astype(F32) - row_own - (iota(shape, 1) // K).astype(F32)
    rel_up = iota(shape, 0).astype(F32) - row_up - (iota(shape, 1) // K).astype(F32)
    for t in range(frames):
        at = PK_RAW + 16 * t
        near = jnp.concatenate([up[at : at + 16], raw[t, 0:16].astype(F32)], axis=0)
        zone = []
        for start, meta, row in ((8, meta_up, META_SHIFT), (16, meta_own, META_FIRST)):

            def rows_at(a, start=start):
                return near[start + a : start + a + RIM + 1]

            zone.append(warp(rows_at, RIM, *shift_lines(meta, row, frames, t)))
        image = jnp.concatenate(zone, axis=0).astype(BF16)
        top[t] = zone[1]
        sums = (project(image, tiles_own, rel_own) + part[t : t + 1], project(image, tiles_up, rel_up))
        both = [lane_pick(jnp.broadcast_to(x, (8, LANES)), source) for x in sums]
        found = jnp.where(frame == t, jnp.where(first_kind, both[0], both[1]), found)
    out[1:2] = found[0:1]
    out[3:4] = line[0:1]


def sweep_kernel(frames, slabs, gathered, out, sent, turned, g_ref):
    per = K // slabs
    lane = iota((8, LANES), 1)
    sub = iota((8, LANES), 0)
    quarter = lane // K
    slab = lane % slabs
    frame = (lane % K) // slabs
    me = lax.axis_index("slab")
    later = jnp.minimum(slab + 1, slabs - 1)
    here = gather_place(slab ^ me, slabs)
    there = gather_place(later ^ me, slabs)

    def turn(tile):
        arrays = []
        for n in range(2 // per):
            lines = []
            for lq in range(4):
                for h in range(per):
                    jh = n * per + h
                    lines.append(gathered[pl.ds(8 * tile + 2 * lq + jh, slabs, stride=16), :])
            at = (2 * tile + n) * LANES
            turned[at : at + LANES] = jnp.concatenate(lines, axis=0).T
            arrays.append(at)
        return (arrays * 2)[:2] if per == 2 else arrays

    def half_lane(jh):
        return jh * slabs if per == 2 else 0

    base_g = turn(0)
    base_x = turn(1)

    for jh in range(2):
        index = quarter * K + half_lane(jh) + here
        for j in range(16):
            n = 16 * jh + j
            rows = turned[base_x[jh] + 8 * j : base_x[jh] + 8 * j + 8]
            g_ref[8 * (K + n) : 8 * (K + n) + 8] = lane_pick(rows, index)
            rows = turned[base_g[jh] + 8 * j : base_g[jh] + 8 * j + 8]
            g_ref[8 * n : 8 * n + 8] = lane_pick(rows, index)
    for r in range(8):
        parts = [turned[pl.ds(base_g[0] + 64 * v + r, 8, stride=8), :] for v in range(2)]
        for oq in (2, 3):
            n = 8 * oq + r
            index = oq * K + half_lane(0) + here
            corner = jnp.where(quarter == 0, lane_pick(parts[0], index), lane_pick(parts[1], index))
            at = pl.ds(8 * n, 8)
            g_ref[at, :] = jnp.where(quarter < 2, corner, g_ref[at, :])
    inner = slab < slabs - 1
    for r in range(8):
        parts = [
            [turned[pl.ds(base_x[uh] + 64 * v + r, 8, stride=8), :] for v in range(2)]
            for uh in range(3 - per)
        ]
        for oq in range(4):
            if per == 2:
                index = oq * K + (quarter // 2) * slabs + there
                value = jnp.where(
                    quarter % 2 == 0, lane_pick(parts[0][0], index), lane_pick(parts[0][1], index)
                )
            else:
                index = oq * K + there
                value = lane_pick(parts[0][0], index)
                for uq in range(1, 4):
                    value = jnp.where(quarter == uq, lane_pick(parts[uq // 2][uq % 2], index), value)
            n = 2 * K + 8 * oq + r
            g_ref[8 * n : 8 * n + 8] = jnp.where(inner, value, 0.0)

    lanes_of = half_lane(1)
    states = []
    for nv in range(frames // per):
        found = []
        for line, kind, shifted in ((0, 0, False), (0, 1, True), (1, 0, False), (1, 1, False)):
            index = line * K + lanes_of + (there if shifted else here)
            value = jnp.zeros((8, LANES), F32)
            for lq in range(4):
                for h in range(per):
                    n = 8 * kind + 2 * lq + nv * per + h
                    rows = turned[base_g[1] + 8 * n : base_g[1] + 8 * n + 8]
                    value = jnp.where((quarter == lq) & (frame == h), lane_pick(rows, index), value)
            found.append(jnp.where(inner, value, 0.0) if shifted else value)
        states.append(found)
    norm = jnp.zeros((8, LANES), F32)
    for n in range(K):
        mine = (sub == n % 8) & (quarter == n // 8)
        norm = jnp.where(mine, g_ref[8 * n : 8 * n + 8], norm)
    inverse = 1.0 / norm
    block_of = states[0][3]
    inverses = [jnp.where(block_of == float(b), inverse, 0.0) for b in range(BLOCKS)]

    local = lane % K
    before = jnp.where(slab == 0, local, local - 1)
    after = jnp.where(inner, local + 1, local)

    def coupled(change):
        totals = [None] * 6
        for kind, place in enumerate((local, before, after)):
            for q in range(4):
                picked = lane_pick(change, q * K + place)
                for r in range(8):
                    n = kind * K + 8 * q + r
                    term = g_ref[8 * n : 8 * n + 8] * jnp.broadcast_to(picked[r : r + 1], (8, LANES))
                    slot = 2 * kind + r % 2
                    totals[slot] = term if totals[slot] is None else totals[slot] + term
        return (totals[0] + totals[1]) + ((totals[2] + totals[3]) + (totals[4] + totals[5]))

    p = [s[0] + s[1] - coupled(s[2]) for s in states]
    traces = [s[2] for s in states]

    def sweep(_, carry):
        p, traces = carry
        for b in range(BLOCKS):
            change = [x * inverses[b] for x in p]
            traces = [x + c for x, c in zip(traces, change)]
            p = [x - coupled(c) for x, c in zip(p, change)]
        return p, traces

    p, traces = lax.fori_loop(0, SWEEPS, sweep, (p, traces))

    mine = sub == lane % 8

    def lines_of(other):
        lines = []
        for t in range(frames):
            index = ((lane % K) // 8) * K + (t % per) * slabs + other
            value = jnp.where(mine, lane_pick(traces[t // per], index), 0.0)
            lines.append(jnp.sum(value, axis=0, keepdims=True))
        return lines

    def sums_of(lines):
        return [functools.reduce(jnp.add, lines), functools.reduce(jnp.add, [x * x for x in lines])]

    own = lines_of(me)
    lines = own + lines_of(jnp.maximum(me - 1, 0)) + lines_of(jnp.minimum(me + 1, slabs - 1))
    for n, line in enumerate(lines + sums_of(own)):
        out[n : n + 1] = line
    for n, line in enumerate(sums_of(lines_of(me ^ 1))):
        sent[n : n + 1] = line


def render(rel, values, tiles, groups=range(4)):
    mixed = jnp.concatenate([jnp.where(rel == float(4 * m), values, 0.0) for m in groups], axis=1)
    high = mixed.astype(BF16)
    low = (mixed - high.astype(F32)).astype(BF16)
    return jnp.dot(high, tiles, preferred_element_type=F32) + jnp.dot(
        low, tiles, preferred_element_type=F32
    )


def finish_kernel(own, by_middle, by_pair, corr, top, tail, lines, t_own, t_up, t_low, values, out):
    frames, rows, _ = corr.shape
    slab = lax.axis_index("slab")
    meta_up = from_above(slab, by_pair[PK_META:PK_ALL], by_middle[PK_META:PK_ALL])
    row_own = own[PK_META:PK_ALL].astype(F32)[META_ROW : META_ROW + 1]
    row_up = meta_up[META_ROW : META_ROW + 1] - float(rows)
    row_low = lines[0:1] + float(rows)
    y = (iota((rows, LANES), 0) + RIM).astype(F32)
    group = (iota((rows, LANES), 1) // K).astype(F32)
    rel_own = y - row_own - group
    rel_up = (y - row_up - group)[0:RIM]
    rel_low = (y - row_low - group)[rows - RIM : rows]
    half = t_low.shape[0]
    for t in range(frames):
        image = render(rel_own, values[t : t + 1], t_own[...])
        above = render(rel_up, values[frames + t : frames + t + 1], t_up[half:], (2, 3))
        below = render(rel_low, values[2 * frames + t : 2 * frames + t + 1], t_low[...], (0, 1))
        out[t, 0:RIM] = top[t].astype(BF16).astype(F32) - image[0:RIM] - above
        out[t, RIM : rows - RIM] = corr[t, RIM : rows - RIM].astype(F32) - image[RIM : rows - RIM]
        out[t, rows - RIM : rows] = tail[t].astype(BF16).astype(F32) - image[rows - RIM : rows] - below


def local_call(kernel, out_shape, scratch_shapes, flops, args, space=pltpu.VMEM):
    args = [pltpu.with_memory_space_constraint(x, space) for x in args]
    return pl.pallas_call(
        kernel,
        out_shape=out_shape,
        in_specs=[pl.BlockSpec(memory_space=space)] * len(args),
        out_specs=jax.tree.map(lambda _: VMEM_SPEC, out_shape),
        scratch_shapes=scratch_shapes,
        compiler_params=pltpu.CompilerParams(vmem_limit_bytes=VMEM_BYTES),
        cost_estimate=pl.CostEstimate(flops=flops, bytes_accessed=1 << 18, transcendentals=0),
    )(*args)


def shards(raw_movie, shifts, footprints, anchors, block_of, init_traces):
    frames, rows, cols = raw_movie.shape
    slabs = lax.axis_size("slab")
    frame_parts = lax.axis_size("frames")
    small = pltpu.VMEM((8, LANES), F32)
    tiles = pltpu.VMEM((TILE * K, LANES), BF16)
    half_tiles = pltpu.VMEM((TILE * K // 2, LANES), BF16)
    image = pltpu.VMEM((frames, rows, LANES), BF16)
    rim = pltpu.VMEM((frames, RIM, LANES), F32)
    extra_rows = K + 8 * frames + 16

    given = (
        raw_movie,
        shifts.transpose(0, 1, 3, 2),
        footprints.transpose(1, 2, 0),
        anchors.T,
        init_traces.T,
        block_of[None],
    )
    pack, pair, raw, line = local_call(
        pack_kernel,
        (pltpu.VMEM((PK_ALL, LANES), BF16), pltpu.VMEM((PK_ALL, LANES), BF16), image, small),
        [pltpu.VMEM(x.shape, x.dtype) for x in given[1:]] + [pltpu.SemaphoreType.DMA((len(given),))],
        10**8,
        given,
        space=pltpu.HBM,
    )
    pairs, middle = neighbour_routes(slabs)
    by_middle = lax.ppermute(pack, "slab", middle)
    by_pair = lax.ppermute(pair, "slab", pairs)

    tile, part, t_own, corr, extra = local_call(
        own_kernel,
        (small, small, tiles, image, pltpu.VMEM((extra_rows, LANES), BF16)),
        [pltpu.VMEM((rows + 32, LANES), F32)],
        10**9,
        (pack, raw),
    )
    gathered, t_up, top = local_call(
        edge_kernel,
        (pltpu.VMEM((16, LANES), F32), tiles, rim),
        [],
        10**9,
        (pack, raw, by_middle, by_pair, line, t_own, tile, part),
    )
    for n, mask in enumerate(gather_masks(slabs)):
        route = [(i, i ^ mask) for i in range(slabs)]
        if n == 0:
            extra, gathered = lax.optimization_barrier((extra, gathered))
        other = lax.ppermute(gathered, "slab", route)
        if n == 0:
            by_cross = lax.ppermute(extra, "slab", [(i, i ^ 3) for i in range(slabs)])
        gathered = jnp.concatenate([gathered, other], axis=0)

    t_low, tail, lines = local_call(
        low_kernel,
        (half_tiles, rim, small),
        [pltpu.VMEM((24, LANES), F32)],
        10**9,
        (pack, raw, by_middle, by_pair, by_cross),
    )
    values, sent = local_call(
        functools.partial(sweep_kernel, frames, slabs),
        (small, small),
        [pltpu.VMEM((4 * LANES, LANES), F32), pltpu.VMEM((8 * 3 * K, LANES), F32)],
        10**9,
        (gathered,),
    )

    moments = values[3 * frames : 3 * frames + 2, :K]
    for hop in range(1, frame_parts):
        route = [
            (f * slabs + s, ((f + hop) % frame_parts) * slabs + (s ^ 1))
            for f in range(frame_parts)
            for s in range(slabs)
        ]
        moments = moments + lax.ppermute(sent, ("frames", "slab"), route)[:2, :K]

    residual = local_call(
        finish_kernel,
        jax.ShapeDtypeStruct((frames, rows, LANES), F32),
        [],
        10**9,
        (pack, by_middle, by_pair, corr, top, tail, lines, t_own, t_up, t_low, values),
    )

    frame_total = frames * frame_parts
    trace_mean = moments[0] / frame_total
    spread = moments[1] / frame_total - trace_mean * trace_mean
    traces_z = (values[:frames, :K] - trace_mean) / jnp.sqrt(spread + EPSILON)
    return traces_z.T, residual


def solution(mesh):
    in_specs = (
        P("frames", "slab", None),
        P(None, "frames", "slab", None),
        P("slab", None, None),
        P("slab", None),
        P("slab"),
        P("slab", "frames"),
    )
    out_specs = (P("slab", "frames"), P("frames", "slab", None))
    return jax.shard_map(shards, mesh=mesh, in_specs=in_specs, out_specs=out_specs, check_vma=False)
```

```python
import functools

import jax
import jax.numpy as jnp
from jax import lax
from jax.experimental import pallas as pl
from jax.experimental.pallas import tpu as pltpu
from jax.sharding import PartitionSpec as P

SHIFT = 3
PATCH_R = 32
BLOCKS = 4
SWEEPS = 3
TILE = 16
RIM = 8
LANES = 128
K = 32
GROUPS = LANES // K
WEIGHT_NEAR = 0.75
WEIGHT_FAR = 0.25
EPSILON = 1e-05
F32 = jnp.float32
BF16 = jnp.bfloat16

PK_RAW = 64
PK_META = 96
PK_ALL = 112
META_ROW = 0
META_COL = 1
META_SHIFT = 2
META_FIRST = 6
VMEM_BYTES = 8 << 20
VMEM_SPEC = pl.BlockSpec(memory_space=pltpu.VMEM)


def iota(shape, axis):
    return lax.broadcasted_iota(jnp.int32, shape, axis)


def lane_pick(values, index):
    return jnp.take_along_axis(values, index, axis=1, mode="promise_in_bounds")


def as_column(line):
    own = iota((K, LANES), 0) == iota((K, LANES), 1)
    return jnp.sum(jnp.where(own, line, 0.0), axis=1, keepdims=True)


def placed_tiles(tiles, col_line):
    col = as_column(col_line).astype(jnp.int32)
    offset = iota((K, LANES), 1) - col
    inside = (offset >= 0) & (offset < TILE)
    base = jnp.clip(offset, 0, TILE - 1)
    out = []
    for i in range(tiles.shape[0] // K * 8):
        half, part = divmod(i, 8)
        tile = tiles[half * K : (half + 1) * K].astype(F32)
        out.append(jnp.where(inside, lane_pick(tile, base + part * TILE), 0.0))
    return jnp.concatenate(out, axis=0).astype(BF16)


def dot_nt(a, b):
    return lax.dot_general(a, b, (((1,), (1,)), ((), ())), preferred_element_type=F32)


def fold_lanes(x):
    return (x + pltpu.roll(x, K, 1)) + (pltpu.roll(x, 2 * K, 1) + pltpu.roll(x, 3 * K, 1))


def masked_sum(block, diff, places):
    total = jnp.zeros((K, LANES), F32)
    for q in places:
        parts = [block(4 * m - q, m) for m in range(4) if 0 <= 4 * m - q < TILE]
        if parts:
            total = total + jnp.where(diff == float(q), functools.reduce(jnp.add, parts), 0.0)
    return fold_lanes(total)


def row_diff(row_a, row_b):
    return row_a - row_b - (iota((K, LANES), 1) // K).astype(F32)


def gram(tiles_a, tiles_b, row_a, row_b):
    full = dot_nt(tiles_a, tiles_b)

    def block(i, m):
        return full[i * K : (i + 1) * K, m * LANES : (m + 1) * LANES]

    return masked_sum(block, row_diff(row_a, row_b), range(-(TILE - 1), TILE))


def gram_above(left, right, row_a, row_b):
    def block(i, m):
        part, first = (left, 1) if m < 2 else (right, 9)
        lane = (m % 2) * LANES
        return part[(i - first) * K : (i - first + 1) * K, lane : lane + LANES]

    return masked_sum(block, row_diff(row_a, row_b), range(-(TILE - 1), 0))


def pick_rows(part, rel):
    total = jnp.zeros(rel.shape, F32)
    for m in range(4):
        total = total + jnp.where(rel == float(4 * m), part[:, m * LANES : (m + 1) * LANES], 0.0)
    return fold_lanes(jnp.sum(total, axis=0, keepdims=True))


def project(corr, tiles, rel):
    return pick_rows(dot_nt(corr, tiles), rel)


def neighbour_routes(slabs):
    pairs = [(i, i ^ 1) for i in range(slabs)]
    ends = [(0, 1), (1, 2), (2, 0), (slabs - 3, slabs - 2), (slabs - 2, slabs - 1), (slabs - 1, slabs - 3)]
    middle = [p for i in range(3, slabs - 4, 2) for p in ((i, i + 1), (i + 1, i))]
    return pairs, ends + middle


def from_above(slab, by_pair, by_middle):
    found = jnp.where(slab % 2 == 1, by_pair.astype(F32), by_middle.astype(F32))
    return jnp.where(slab == 0, 0.0, found)


def below_part(pack, firsts):
    return jnp.concatenate([pack[0:K].astype(F32), *firsts, pack[PK_META:PK_ALL].astype(F32)], axis=0)


def received_below(pack, frames):
    firsts = [pack[PK_RAW + 16 * t : PK_RAW + 16 * t + 16].astype(F32)[0:8] for t in range(frames)]
    return below_part(pack, firsts)


def write_edge_rows(out, raw, to_below):
    frames, rows, _ = raw.shape
    for t in range(frames):
        last, first = raw[t, rows - 16 : rows].astype(F32), raw[t, 0:16].astype(F32)
        out[PK_RAW + 16 * t : PK_RAW + 16 * t + 16] = jnp.where(to_below, last, first).astype(BF16)


def from_below(slab, slabs, by_pair, by_middle, by_cross):
    odd = jnp.where((slab == 1) | (slab == slabs - 3), by_cross, by_middle)
    found = jnp.where(slab % 2 == 0, by_pair, odd)
    return jnp.where(slab == slabs - 1, 0.0, found)


def gather_masks(slabs):
    bits = slabs.bit_length() - 1
    return [(1 << b) | 1 for b in range(bits - 1, 0, -1)] + [1]


def gather_place(diff, slabs):
    bits = slabs.bit_length() - 1
    odd = diff & 1
    place = jnp.zeros_like(diff)
    for r in range(bits - 1):
        bit = (diff >> (bits - 1 - r)) & 1
        place = place + bit * (1 << r)
        odd = odd ^ bit
    return place + odd * (1 << (bits - 1))


def gather_source():
    place = iota((8, LANES), 1)
    return 8 * ((place // 16) % 4) + place % 8, (place // 8) % 2, place < LANES // 2


def pack_kernel(*refs):
    count = 6
    given, (out, pair, raw, line) = refs[:count], refs[count : count + 4]
    held = refs[count + 4 : 2 * count + 3]
    sems = refs[-1]
    tiles, shifts, anchors, init, block_of = held
    copies = [
        pltpu.make_async_copy(source, target, sems.at[n])
        for n, (source, target) in enumerate(zip(given, (raw, *held)))
    ]
    for copy in copies:
        copy.start()
    raw_copy, tiles_copy, *small_copies = copies
    frames, rows, _ = raw.shape
    last = rows // PATCH_R - 1
    slab = lax.axis_index("slab")
    base = slab * rows - RIM
    for copy in small_copies:
        copy.wait()
    places = jnp.concatenate([anchors[...].astype(F32)] * GROUPS, axis=1)
    sub = iota((16, LANES), 0)
    meta = jnp.where(sub == META_COL, places[1:2], 0.0)
    meta = jnp.where(sub == META_ROW, places[0:1] - base.astype(F32), meta)
    for t in range(frames):
        for axis in range(2):
            moves = shifts[axis, t].astype(F32)
            for place, patch in ((META_SHIFT, last), (META_FIRST, 0)):
                meta = jnp.where(sub == place + axis * frames + t, moves[:, patch : patch + 1], meta)
    out[PK_META:PK_ALL] = meta.astype(BF16)
    pair[PK_META:PK_ALL] = meta.astype(BF16)
    source, frame, first_kind = gather_source()
    inits = jnp.concatenate([init[...]] * GROUPS, axis=1)
    blocks = jnp.concatenate([block_of[...].astype(F32)] * GROUPS, axis=1)
    found = jnp.zeros((8, LANES), F32)
    for t in range(frames):
        both = [lane_pick(jnp.broadcast_to(x, (8, LANES)), source) for x in (inits[t : t + 1], blocks)]
        found = jnp.where(frame == t, jnp.where(first_kind, both[0], both[1]), found)
    line[...] = found
    raw_copy.wait()
    write_edge_rows(out, raw, slab % 2 == 1)
    write_edge_rows(pair, raw, slab % 2 == 0)
    tiles_copy.wait()
    for half in range(2):
        part = tiles[8 * half : 8 * half + 8].astype(F32).reshape(LANES, K)
        part = part.T.astype(BF16)
        out[K * half : K * half + K] = part
        pair[K * half : K * half + K] = part


def write_tile(out, first, mat, rows):
    lane = iota((K, LANES), 1)
    own = lane // 8 == iota((K, LANES), 0) % 16
    for lq in range(4):
        part = jnp.where(own, lane_pick(mat, 8 * lq + lane % 8), 0.0)
        for jh in range(2):
            if 2 * lq + jh in rows:
                out[first + 2 * lq + jh : first + 2 * lq + jh + 1] = jnp.sum(
                    part[16 * jh : 16 * jh + 16], axis=0, keepdims=True
                )


def warp(rows_at, count, a_line, c_line):
    both = jnp.zeros((count, LANES), F32)
    for a in range(-SHIFT, SHIFT + 1):
        window = rows_at(a)
        blend = WEIGHT_NEAR * window[0:count] + WEIGHT_FAR * window[1 : count + 1]
        both = jnp.where(a_line == float(a), blend, both)
    place = iota((count, LANES), 1) + c_line.astype(jnp.int32)
    moved = lane_pick(both, jnp.clip(place, 0, LANES - 1))
    return jnp.where((place >= 0) & (place < LANES), moved, 0.0)


def shift_lines(meta, row, frames, t):
    return meta[row + t : row + t + 1], meta[row + frames + t : row + frames + t + 1]


def own_kernel(own, raw, tile, part, t_own, corr, extra, ext):
    frames, rows, _ = raw.shape
    slab = lax.axis_index("slab")
    is_last = slab == lax.axis_size("slab") - 1
    extra[...] = below_part(own[...], [raw[t, 0:16].astype(F32)[0:8] for t in range(frames)]).astype(BF16)
    meta = own[PK_META:PK_ALL].astype(F32)
    row = meta[META_ROW : META_ROW + 1]
    tiles = placed_tiles(own[0 : 2 * K], meta[META_COL : META_COL + 1])
    t_own[...] = tiles
    tile[...] = jnp.zeros((8, LANES), F32)
    part[...] = jnp.zeros((8, LANES), F32)
    write_tile(tile, 0, gram(tiles, tiles, as_column(row), row), (0, 2, 4, 5, 6, 7))
    y = iota((rows, LANES), 0)
    keep = (y >= RIM) & ((y < rows - RIM) | is_last)
    rel = (y + RIM).astype(F32) - row - (iota((rows, LANES), 1) // K).astype(F32)
    for t in range(frames):
        ext[0:16] = jnp.zeros((16, LANES), F32)
        ext[16 : 16 + rows] = raw[t].astype(F32)
        ext[16 + rows : 32 + rows] = jnp.zeros((16, LANES), F32)
        parts = []
        for p, row_of in ((0, META_FIRST), (1, META_SHIFT)):

            def rows_at(a, first=16 + p * PATCH_R):
                return ext[first + a : first + a + PATCH_R + 1]

            parts.append(warp(rows_at, PATCH_R, *shift_lines(meta, row_of, frames, t)))
        image = jnp.concatenate(parts, axis=0)
        corr[t] = image.astype(BF16)
        part[t : t + 1] = project(jnp.where(keep, image, 0.0).astype(BF16), tiles, rel)


def low_kernel(own, raw, by_middle, by_pair, by_cross, tiles, tail, lines, ext):
    frames, rows, _ = raw.shape
    low = from_below(
        lax.axis_index("slab"),
        lax.axis_size("slab"),
        received_below(by_pair[...], frames),
        received_below(by_middle[...], frames),
        by_cross[...].astype(F32),
    )
    meta = own[PK_META:PK_ALL].astype(F32)
    meta_low = low[K + 8 * frames :]
    tiles[...] = placed_tiles(low[0:K], meta_low[META_COL : META_COL + 1])
    lines[...] = jnp.broadcast_to(meta_low[META_ROW : META_ROW + 1], (8, LANES))
    for t in range(frames):
        ext[0:16] = raw[t, rows - 16 : rows].astype(F32)
        ext[16:24] = low[K + 8 * t : K + 8 * t + 8]

        def rows_at(a):
            return ext[8 + a : 17 + a]

        tail[t] = warp(rows_at, RIM, *shift_lines(meta, META_SHIFT, frames, t))


def edge_kernel(own, raw, by_middle, by_pair, line, t_own, tile, part, out, t_up, top):
    frames, rows, _ = raw.shape
    up = from_above(lax.axis_index("slab"), by_pair[...], by_middle[...])
    meta_own = own[PK_META:PK_ALL].astype(F32)
    meta_up = up[PK_META:PK_ALL]
    row_own = meta_own[META_ROW : META_ROW + 1]
    row_up = meta_up[META_ROW : META_ROW + 1] - float(rows)
    tiles_own = t_own[...]
    tiles_up = placed_tiles(up[0 : 2 * K], meta_up[META_COL : META_COL + 1])
    t_up[...] = tiles_up
    out[0:8] = tile[...]
    source, frame, first_kind = gather_source()
    found = jnp.zeros((8, LANES), F32)
    shape = (2 * RIM, LANES)
    rel_own = iota(shape, 0).astype(F32) - row_own - (iota(shape, 1) // K).astype(F32)
    rel_up = iota(shape, 0).astype(F32) - row_up - (iota(shape, 1) // K).astype(F32)
    images = []
    for t in range(frames):
        at = PK_RAW + 16 * t
        near = jnp.concatenate([up[at : at + 16], raw[t, 0:16].astype(F32)], axis=0)
        zone = []
        for start, meta, row in ((8, meta_up, META_SHIFT), (16, meta_own, META_FIRST)):

            def rows_at(a, start=start):
                return near[start + a : start + a + RIM + 1]

            zone.append(warp(rows_at, RIM, *shift_lines(meta, row, frames, t)))
        images.append(jnp.concatenate(zone, axis=0).astype(BF16))
        top[t] = zone[1]
    images = jnp.concatenate(images, axis=0)
    half = TILE * K // 2
    left = dot_nt(jnp.concatenate([tiles_up[K:], images], axis=0), tiles_own[0:half])
    right = dot_nt(jnp.concatenate([tiles_up[9 * K :], images], axis=0), tiles_own[half:])
    write_tile(out, 8, gram_above(left, right, as_column(row_up), row_own), range(8))
    by_own = jnp.concatenate([left[15 * K :], right[7 * K :]], axis=1)
    by_up = dot_nt(images, tiles_up)
    for t in range(frames):
        at = 2 * RIM * t
        sums = (
            pick_rows(by_own[at : at + 2 * RIM], rel_own) + part[t : t + 1],
            pick_rows(by_up[at : at + 2 * RIM], rel_up),
        )
        both = [lane_pick(jnp.broadcast_to(x, (8, LANES)), source) for x in sums]
        found = jnp.where(frame == t, jnp.where(first_kind, both[0], both[1]), found)
    out[1:2] = found[0:1]
    out[3:4] = line[0:1]


def sweep_kernel(frames, slabs, gathered, out, sent, turned, g_ref):
    per = K // slabs
    lane = iota((8, LANES), 1)
    sub = iota((8, LANES), 0)
    quarter = lane // K
    slab = lane % slabs
    frame = (lane % K) // slabs
    me = lax.axis_index("slab")
    later = jnp.minimum(slab + 1, slabs - 1)
    here = gather_place(slab ^ me, slabs)
    there = gather_place(later ^ me, slabs)

    def turn(tile):
        arrays = []
        for n in range(2 // per):
            lines = []
            for lq in range(4):
                for h in range(per):
                    jh = n * per + h
                    lines.append(gathered[pl.ds(8 * tile + 2 * lq + jh, slabs, stride=16), :])
            at = (2 * tile + n) * LANES
            turned[at : at + LANES] = jnp.concatenate(lines, axis=0).T
            arrays.append(at)
        return (arrays * 2)[:2] if per == 2 else arrays

    def half_lane(jh):
        return jh * slabs if per == 2 else 0

    base_g = turn(0)
    base_x = turn(1)

    for jh in range(2):
        index = quarter * K + half_lane(jh) + here
        for j in range(16):
            n = 16 * jh + j
            rows = turned[base_x[jh] + 8 * j : base_x[jh] + 8 * j + 8]
            g_ref[8 * (K + n) : 8 * (K + n) + 8] = lane_pick(rows, index)
            rows = turned[base_g[jh] + 8 * j : base_g[jh] + 8 * j + 8]
            g_ref[8 * n : 8 * n + 8] = lane_pick(rows, index)
    for r in range(8):
        parts = [turned[pl.ds(base_g[0] + 64 * v + r, 8, stride=8), :] for v in range(2)]
        for oq in (2, 3):
            n = 8 * oq + r
            index = oq * K + half_lane(0) + here
            corner = jnp.where(quarter == 0, lane_pick(parts[0], index), lane_pick(parts[1], index))
            at = pl.ds(8 * n, 8)
            g_ref[at, :] = jnp.where(quarter < 2, corner, g_ref[at, :])
    inner = slab < slabs - 1
    for r in range(8):
        parts = [
            [turned[pl.ds(base_x[uh] + 64 * v + r, 8, stride=8), :] for v in range(2)]
            for uh in range(3 - per)
        ]
        for oq in range(4):
            if per == 2:
                index = oq * K + (quarter // 2) * slabs + there
                value = jnp.where(
                    quarter % 2 == 0, lane_pick(parts[0][0], index), lane_pick(parts[0][1], index)
                )
            else:
                index = oq * K + there
                value = lane_pick(parts[0][0], index)
                for uq in range(1, 4):
                    value = jnp.where(quarter == uq, lane_pick(parts[uq // 2][uq % 2], index), value)
            n = 2 * K + 8 * oq + r
            g_ref[8 * n : 8 * n + 8] = jnp.where(inner, value, 0.0)

    lanes_of = half_lane(1)
    states = []
    for nv in range(frames // per):
        found = []
        for line, kind, shifted in ((0, 0, False), (0, 1, True), (1, 0, False), (1, 1, False)):
            index = line * K + lanes_of + (there if shifted else here)
            value = jnp.zeros((8, LANES), F32)
            for lq in range(4):
                for h in range(per):
                    n = 8 * kind + 2 * lq + nv * per + h
                    rows = turned[base_g[1] + 8 * n : base_g[1] + 8 * n + 8]
                    value = jnp.where((quarter == lq) & (frame == h), lane_pick(rows, index), value)
            found.append(jnp.where(inner, value, 0.0) if shifted else value)
        states.append(found)
    norm = jnp.zeros((8, LANES), F32)
    for n in range(K):
        mine = (sub == n % 8) & (quarter == n // 8)
        norm = jnp.where(mine, g_ref[8 * n : 8 * n + 8], norm)
    inverse = 1.0 / norm
    block_of = states[0][3]

    local = lane % K
    before = jnp.where(slab == 0, local, local - 1)
    after = jnp.where(inner, local + 1, local)

    def coupled(change):
        totals = [None] * 6
        for kind, place in enumerate((local, before, after)):
            for q in range(4):
                picked = lane_pick(change, q * K + place)
                for r in range(8):
                    n = kind * K + 8 * q + r
                    term = g_ref[8 * n : 8 * n + 8] * jnp.broadcast_to(picked[r : r + 1], (8, LANES))
                    slot = 2 * kind + r % 2
                    totals[slot] = term if totals[slot] is None else totals[slot] + term
        return (totals[0] + totals[1]) + ((totals[2] + totals[3]) + (totals[4] + totals[5]))

    def step(n, carry):
        p, change, traces = carry
        p = [x - coupled(c) for x, c in zip(p, change)]
        scale = jnp.where(block_of == lax.rem(n, BLOCKS).astype(F32), inverse, 0.0)
        change = [x * scale for x in p]
        return p, change, [x + c for x, c in zip(traces, change)]

    first = [s[2] for s in states]
    start = ([s[0] + s[1] for s in states], first, first)
    _, _, traces = lax.fori_loop(0, SWEEPS * BLOCKS, step, start, unroll=12)

    mine = sub == lane % 8

    def lines_of(other):
        lines = []
        for t in range(frames):
            index = ((lane % K) // 8) * K + (t % per) * slabs + other
            value = jnp.where(mine, lane_pick(traces[t // per], index), 0.0)
            lines.append(jnp.sum(value, axis=0, keepdims=True))
        return lines

    def sums_of(lines):
        return [functools.reduce(jnp.add, lines), functools.reduce(jnp.add, [x * x for x in lines])]

    own = lines_of(me)
    lines = own + lines_of(jnp.maximum(me - 1, 0)) + lines_of(jnp.minimum(me + 1, slabs - 1))
    for n, line in enumerate(lines + sums_of(own)):
        out[n : n + 1] = line
    for n, line in enumerate(sums_of(lines_of(me ^ 1))):
        sent[n : n + 1] = line


def render(rel, values, tiles, groups=range(4)):
    mixed = jnp.concatenate([jnp.where(rel == float(4 * m), values, 0.0) for m in groups], axis=1)
    high = mixed.astype(BF16)
    low = (mixed - high.astype(F32)).astype(BF16)
    return jnp.dot(high, tiles, preferred_element_type=F32) + jnp.dot(
        low, tiles, preferred_element_type=F32
    )


def finish_kernel(own, by_middle, by_pair, corr, top, tail, lines, t_own, t_up, t_low, values, out):
    frames, rows, _ = corr.shape
    slab = lax.axis_index("slab")
    meta_up = from_above(slab, by_pair[PK_META:PK_ALL], by_middle[PK_META:PK_ALL])
    row_own = own[PK_META:PK_ALL].astype(F32)[META_ROW : META_ROW + 1]
    row_up = meta_up[META_ROW : META_ROW + 1] - float(rows)
    row_low = lines[0:1] + float(rows)
    y = (iota((rows, LANES), 0) + RIM).astype(F32)
    group = (iota((rows, LANES), 1) // K).astype(F32)
    rel_own = y - row_own - group
    rel_up = (y - row_up - group)[0:RIM]
    rel_low = (y - row_low - group)[rows - RIM : rows]
    half = t_low.shape[0]
    for t in range(frames):
        image = render(rel_own, values[t : t + 1], t_own[...])
        above = render(rel_up, values[frames + t : frames + t + 1], t_up[half:], (2, 3))
        below = render(rel_low, values[2 * frames + t : 2 * frames + t + 1], t_low[...], (0, 1))
        out[t, 0:RIM] = top[t].astype(BF16).astype(F32) - image[0:RIM] - above
        out[t, RIM : rows - RIM] = corr[t, RIM : rows - RIM].astype(F32) - image[RIM : rows - RIM]
        out[t, rows - RIM : rows] = tail[t].astype(BF16).astype(F32) - image[rows - RIM : rows] - below


def score_kernel(frame_total, values, *rest):
    out = rest[-1]
    frames = out.shape[0]
    sums = values[3 * frames : 3 * frames + 2]
    for other in rest[:-1]:
        sums = sums + other[0:2]
    mean = sums[0:1] / frame_total
    spread = sums[1:2] / frame_total - mean * mean
    out[...] = ((values[0:frames] - mean) / jnp.sqrt(spread + EPSILON))[:, 0:K]


def local_call(kernel, out_shape, scratch_shapes, flops, args, space=pltpu.VMEM):
    args = [pltpu.with_memory_space_constraint(x, space) for x in args]
    return pl.pallas_call(
        kernel,
        out_shape=out_shape,
        in_specs=[pl.BlockSpec(memory_space=space)] * len(args),
        out_specs=jax.tree.map(lambda _: VMEM_SPEC, out_shape),
        scratch_shapes=scratch_shapes,
        compiler_params=pltpu.CompilerParams(vmem_limit_bytes=VMEM_BYTES),
        cost_estimate=pl.CostEstimate(flops=flops, bytes_accessed=1 << 18, transcendentals=0),
    )(*args)


def shards(raw_movie, shifts, footprints, anchors, block_of, init_traces):
    frames, rows, cols = raw_movie.shape
    slabs = lax.axis_size("slab")
    frame_parts = lax.axis_size("frames")
    small = pltpu.VMEM((8, LANES), F32)
    tiles = pltpu.VMEM((TILE * K, LANES), BF16)
    half_tiles = pltpu.VMEM((TILE * K // 2, LANES), BF16)
    image = pltpu.VMEM((frames, rows, LANES), BF16)
    rim = pltpu.VMEM((frames, RIM, LANES), F32)
    extra_rows = K + 8 * frames + 16

    given = (
        raw_movie,
        footprints.transpose(1, 2, 0),
        shifts.transpose(0, 1, 3, 2),
        anchors.T,
        init_traces.T,
        block_of[None],
    )
    pack, pair, raw, line = local_call(
        pack_kernel,
        (pltpu.VMEM((PK_ALL, LANES), BF16), pltpu.VMEM((PK_ALL, LANES), BF16), image, small),
        [pltpu.VMEM(x.shape, x.dtype) for x in given[1:]] + [pltpu.SemaphoreType.DMA((len(given),))],
        10**8,
        given,
        space=pltpu.HBM,
    )
    pairs, middle = neighbour_routes(slabs)
    by_middle = lax.ppermute(pack, "slab", middle)
    by_pair = lax.ppermute(pair, "slab", pairs)

    tile, part, t_own, corr, extra = local_call(
        own_kernel,
        (small, small, tiles, image, pltpu.VMEM((extra_rows, LANES), BF16)),
        [pltpu.VMEM((rows + 32, LANES), F32)],
        10**9,
        (pack, raw),
    )
    gathered, t_up, top = local_call(
        edge_kernel,
        (pltpu.VMEM((16, LANES), F32), tiles, rim),
        [],
        10**9,
        (pack, raw, by_middle, by_pair, line, t_own, tile, part),
    )
    for n, mask in enumerate(gather_masks(slabs)):
        route = [(i, i ^ mask) for i in range(slabs)]
        if n == 0:
            extra, gathered = lax.optimization_barrier((extra, gathered))
        other = lax.ppermute(gathered, "slab", route)
        if n == 0:
            by_cross = lax.ppermute(extra, "slab", [(i, i ^ 3) for i in range(slabs)])
        gathered = jnp.concatenate([gathered, other], axis=0)

    t_low, tail, lines = local_call(
        low_kernel,
        (half_tiles, rim, small),
        [pltpu.VMEM((24, LANES), F32)],
        10**9,
        (pack, raw, by_middle, by_pair, by_cross),
    )
    values, sent = local_call(
        functools.partial(sweep_kernel, frames, slabs),
        (small, small),
        [pltpu.VMEM((4 * LANES, LANES), F32), pltpu.VMEM((8 * 3 * K, LANES), F32)],
        10**9,
        (gathered,),
    )

    others = []
    for hop in range(1, frame_parts):
        route = [
            (f * slabs + s, ((f + hop) % frame_parts) * slabs + (s ^ 1))
            for f in range(frame_parts)
            for s in range(slabs)
        ]
        others.append(lax.ppermute(sent, ("frames", "slab"), route))

    residual = local_call(
        finish_kernel,
        jax.ShapeDtypeStruct((frames, rows, LANES), F32),
        [],
        10**9,
        (pack, by_middle, by_pair, corr, top, tail, lines, t_own, t_up, t_low, values),
    )

    traces_z = local_call(
        functools.partial(score_kernel, frames * frame_parts),
        jax.ShapeDtypeStruct((frames, K), F32),
        [],
        10**4,
        (values, *others),
    )
    return traces_z.T, residual


def solution(mesh):
    in_specs = (
        P("frames", "slab", None),
        P(None, "frames", "slab", None),
        P("slab", None, None),
        P("slab", None),
        P("slab"),
        P("slab", "frames"),
    )
    out_specs = (P("slab", "frames"), P("frames", "slab", None))
    return jax.shard_map(shards, mesh=mesh, in_specs=in_specs, out_specs=out_specs, check_vma=False)
```

```python
import functools

import jax
import jax.numpy as jnp
from jax import lax
from jax.experimental import pallas as pl
from jax.experimental.pallas import tpu as pltpu
from jax.sharding import PartitionSpec as P

SHIFT = 3
PATCH_R = 32
BLOCKS = 4
SWEEPS = 3
TILE = 16
RIM = 8
LANES = 128
K = 32
GROUPS = LANES // K
WEIGHT_NEAR = 0.75
WEIGHT_FAR = 0.25
EPSILON = 1e-05
F32 = jnp.float32
BF16 = jnp.bfloat16

PK_RAW = 64
PK_META = 96
PK_ALL = 112
META_ROW = 0
META_COL = 1
META_SHIFT = 2
META_FIRST = 6
VMEM_BYTES = 8 << 20
VMEM_SPEC = pl.BlockSpec(memory_space=pltpu.VMEM)


def iota(shape, axis):
    return lax.broadcasted_iota(jnp.int32, shape, axis)


def lane_pick(values, index):
    return jnp.take_along_axis(values, index, axis=1, mode="promise_in_bounds")


def as_column(line):
    own = iota((K, LANES), 0) == iota((K, LANES), 1)
    return jnp.sum(jnp.where(own, line, 0.0), axis=1, keepdims=True)


def placed_tiles(tiles, col_line):
    col = as_column(col_line).astype(jnp.int32)
    offset = iota((K, LANES), 1) - col
    inside = (offset >= 0) & (offset < TILE)
    base = jnp.clip(offset, 0, TILE - 1)
    out = []
    for i in range(tiles.shape[0] // K * 8):
        half, part = divmod(i, 8)
        tile = tiles[half * K : (half + 1) * K].astype(F32)
        out.append(jnp.where(inside, lane_pick(tile, base + part * TILE), 0.0))
    return jnp.concatenate(out, axis=0).astype(BF16)


def dot_nt(a, b):
    return lax.dot_general(a, b, (((1,), (1,)), ((), ())), preferred_element_type=F32)


def fold_lanes(x):
    return (x + pltpu.roll(x, K, 1)) + (pltpu.roll(x, 2 * K, 1) + pltpu.roll(x, 3 * K, 1))


def masked_sum(block, diff, places):
    total = jnp.zeros((K, LANES), F32)
    for q in places:
        parts = [block(4 * m - q, m) for m in range(4) if 0 <= 4 * m - q < TILE]
        if parts:
            total = total + jnp.where(diff == float(q), functools.reduce(jnp.add, parts), 0.0)
    return fold_lanes(total)


def row_diff(row_a, row_b):
    return row_a - row_b - (iota((K, LANES), 1) // K).astype(F32)


def gram(tiles_a, tiles_b, row_a, row_b):
    full = dot_nt(tiles_a, tiles_b)

    def block(i, m):
        return full[i * K : (i + 1) * K, m * LANES : (m + 1) * LANES]

    return masked_sum(block, row_diff(row_a, row_b), range(-(TILE - 1), TILE))


def gram_above(left, right, row_a, row_b):
    def block(i, m):
        part, first = (left, 1) if m < 2 else (right, 9)
        lane = (m % 2) * LANES
        return part[(i - first) * K : (i - first + 1) * K, lane : lane + LANES]

    return masked_sum(block, row_diff(row_a, row_b), range(-(TILE - 1), 0))


def pick_rows(part, rel):
    total = jnp.zeros(rel.shape, F32)
    for m in range(4):
        total = total + jnp.where(rel == float(4 * m), part[:, m * LANES : (m + 1) * LANES], 0.0)
    return fold_lanes(jnp.sum(total, axis=0, keepdims=True))


def project(corr, tiles, rel):
    return pick_rows(dot_nt(corr, tiles), rel)


def neighbour_routes(slabs):
    pairs = [(i, i ^ 1) for i in range(slabs)]
    ends = [(0, 1), (1, 2), (2, 0), (slabs - 3, slabs - 2), (slabs - 2, slabs - 1), (slabs - 1, slabs - 3)]
    middle = [p for i in range(3, slabs - 4, 2) for p in ((i, i + 1), (i + 1, i))]
    return pairs, ends + middle


def from_above(slab, by_pair, by_middle):
    found = jnp.where(slab % 2 == 1, by_pair.astype(F32), by_middle.astype(F32))
    return jnp.where(slab == 0, 0.0, found)


def below_part(pack, firsts):
    return jnp.concatenate([pack[0:K].astype(F32), *firsts, pack[PK_META:PK_ALL].astype(F32)], axis=0)


def received_below(pack, frames):
    firsts = [pack[PK_RAW + 16 * t : PK_RAW + 16 * t + 16].astype(F32)[0:8] for t in range(frames)]
    return below_part(pack, firsts)


def write_edge_rows(out, raw, to_below):
    frames, rows, _ = raw.shape
    for t in range(frames):
        last, first = raw[t, rows - 16 : rows].astype(F32), raw[t, 0:16].astype(F32)
        out[PK_RAW + 16 * t : PK_RAW + 16 * t + 16] = jnp.where(to_below, last, first).astype(BF16)


def from_below(slab, slabs, by_pair, by_middle, by_cross):
    odd = jnp.where((slab == 1) | (slab == slabs - 3), by_cross, by_middle)
    found = jnp.where(slab % 2 == 0, by_pair, odd)
    return jnp.where(slab == slabs - 1, 0.0, found)


def gather_masks(slabs):
    bits = slabs.bit_length() - 1
    return [(1 << b) | 1 for b in range(bits - 1, 0, -1)] + [1]


def gather_place(diff, slabs):
    bits = slabs.bit_length() - 1
    odd = diff & 1
    place = jnp.zeros_like(diff)
    for r in range(bits - 1):
        bit = (diff >> (bits - 1 - r)) & 1
        place = place + bit * (1 << r)
        odd = odd ^ bit
    return place + odd * (1 << (bits - 1))


def gather_source():
    place = iota((8, LANES), 1)
    return 8 * ((place // 16) % 4) + place % 8, (place // 8) % 2, place < LANES // 2


def pack_kernel(*refs):
    count = 6
    given, (out, pair, raw, line) = refs[:count], refs[count : count + 4]
    held = refs[count + 4 : 2 * count + 3]
    sems = refs[-1]
    tiles, shifts, anchors, init, block_of = held
    copies = [
        pltpu.make_async_copy(source, target, sems.at[n])
        for n, (source, target) in enumerate(zip(given, (raw, *held)))
    ]
    for copy in copies:
        copy.start()
    raw_copy, tiles_copy, *small_copies = copies
    frames, rows, _ = raw.shape
    last = rows // PATCH_R - 1
    slab = lax.axis_index("slab")
    base = slab * rows - RIM
    for copy in small_copies:
        copy.wait()
    places = jnp.concatenate([anchors[...].astype(F32)] * GROUPS, axis=1)
    sub = iota((16, LANES), 0)
    meta = jnp.where(sub == META_COL, places[1:2], 0.0)
    meta = jnp.where(sub == META_ROW, places[0:1] - base.astype(F32), meta)
    for t in range(frames):
        for axis in range(2):
            moves = shifts[axis, t].astype(F32)
            for place, patch in ((META_SHIFT, last), (META_FIRST, 0)):
                meta = jnp.where(sub == place + axis * frames + t, moves[:, patch : patch + 1], meta)
    out[PK_META:PK_ALL] = meta.astype(BF16)
    pair[PK_META:PK_ALL] = meta.astype(BF16)
    source, frame, first_kind = gather_source()
    inits = jnp.concatenate([init[...]] * GROUPS, axis=1)
    blocks = jnp.concatenate([block_of[...].astype(F32)] * GROUPS, axis=1)
    found = jnp.zeros((8, LANES), F32)
    for t in range(frames):
        both = [lane_pick(jnp.broadcast_to(x, (8, LANES)), source) for x in (inits[t : t + 1], blocks)]
        found = jnp.where(frame == t, jnp.where(first_kind, both[0], both[1]), found)
    line[...] = found
    raw_copy.wait()
    write_edge_rows(out, raw, slab % 2 == 1)
    write_edge_rows(pair, raw, slab % 2 == 0)
    tiles_copy.wait()
    for half in range(2):
        part = tiles[8 * half : 8 * half + 8].astype(F32).reshape(LANES, K)
        part = part.T.astype(BF16)
        out[K * half : K * half + K] = part
        pair[K * half : K * half + K] = part


def write_tile(out, first, mat, rows):
    lane = iota((K, LANES), 1)
    own = lane // 8 == iota((K, LANES), 0) % 16
    for lq in range(4):
        part = jnp.where(own, lane_pick(mat, 8 * lq + lane % 8), 0.0)
        for jh in range(2):
            if 2 * lq + jh in rows:
                out[first + 2 * lq + jh : first + 2 * lq + jh + 1] = jnp.sum(
                    part[16 * jh : 16 * jh + 16], axis=0, keepdims=True
                )


def warp(rows_at, count, a_line, c_line):
    both = jnp.zeros((count, LANES), F32)
    for a in range(-SHIFT, SHIFT + 1):
        window = rows_at(a)
        blend = WEIGHT_NEAR * window[0:count] + WEIGHT_FAR * window[1 : count + 1]
        both = jnp.where(a_line == float(a), blend, both)
    place = iota((count, LANES), 1) + c_line.astype(jnp.int32)
    moved = lane_pick(both, jnp.clip(place, 0, LANES - 1))
    return jnp.where((place >= 0) & (place < LANES), moved, 0.0)


def shift_lines(meta, row, frames, t):
    return meta[row + t : row + t + 1], meta[row + frames + t : row + frames + t + 1]


def own_kernel(own, raw, tile, part, t_own, corr, extra, ext):
    frames, rows, _ = raw.shape
    slab = lax.axis_index("slab")
    is_last = slab == lax.axis_size("slab") - 1
    extra[...] = below_part(own[...], [raw[t, 0:16].astype(F32)[0:8] for t in range(frames)]).astype(BF16)
    meta = own[PK_META:PK_ALL].astype(F32)
    row = meta[META_ROW : META_ROW + 1]
    tiles = placed_tiles(own[0 : 2 * K], meta[META_COL : META_COL + 1])
    t_own[...] = tiles
    tile[...] = jnp.zeros((8, LANES), F32)
    part[...] = jnp.zeros((8, LANES), F32)
    write_tile(tile, 0, gram(tiles, tiles, as_column(row), row), (0, 2, 4, 5, 6, 7))
    y = iota((rows, LANES), 0)
    keep = (y >= RIM) & ((y < rows - RIM) | is_last)
    rel = (y + RIM).astype(F32) - row - (iota((rows, LANES), 1) // K).astype(F32)
    for t in range(frames):
        ext[0:16] = jnp.zeros((16, LANES), F32)
        ext[16 : 16 + rows] = raw[t].astype(F32)
        ext[16 + rows : 32 + rows] = jnp.zeros((16, LANES), F32)
        parts = []
        for p, row_of in ((0, META_FIRST), (1, META_SHIFT)):

            def rows_at(a, first=16 + p * PATCH_R):
                return ext[first + a : first + a + PATCH_R + 1]

            parts.append(warp(rows_at, PATCH_R, *shift_lines(meta, row_of, frames, t)))
        image = jnp.concatenate(parts, axis=0)
        corr[t] = image.astype(BF16)
        part[t : t + 1] = project(jnp.where(keep, image, 0.0).astype(BF16), tiles, rel)


def low_kernel(own, raw, by_middle, by_pair, by_cross, tiles, tail, lines, ext):
    frames, rows, _ = raw.shape
    low = from_below(
        lax.axis_index("slab"),
        lax.axis_size("slab"),
        received_below(by_pair[...], frames),
        received_below(by_middle[...], frames),
        by_cross[...].astype(F32),
    )
    meta = own[PK_META:PK_ALL].astype(F32)
    meta_low = low[K + 8 * frames :]
    tiles[...] = placed_tiles(low[0:K], meta_low[META_COL : META_COL + 1])
    lines[...] = jnp.broadcast_to(meta_low[META_ROW : META_ROW + 1], (8, LANES))
    for t in range(frames):
        ext[0:16] = raw[t, rows - 16 : rows].astype(F32)
        ext[16:24] = low[K + 8 * t : K + 8 * t + 8]

        def rows_at(a):
            return ext[8 + a : 17 + a]

        tail[t] = warp(rows_at, RIM, *shift_lines(meta, META_SHIFT, frames, t))


def edge_kernel(own, raw, by_middle, by_pair, line, t_own, tile, part, out, t_up, top):
    frames, rows, _ = raw.shape
    up = from_above(lax.axis_index("slab"), by_pair[...], by_middle[...])
    meta_own = own[PK_META:PK_ALL].astype(F32)
    meta_up = up[PK_META:PK_ALL]
    row_own = meta_own[META_ROW : META_ROW + 1]
    row_up = meta_up[META_ROW : META_ROW + 1] - float(rows)
    tiles_own = t_own[...]
    tiles_up = placed_tiles(up[0 : 2 * K], meta_up[META_COL : META_COL + 1])
    t_up[...] = tiles_up
    out[0:8] = tile[...]
    source, frame, first_kind = gather_source()
    found = jnp.zeros((8, LANES), F32)
    shape = (2 * RIM, LANES)
    rel_own = iota(shape, 0).astype(F32) - row_own - (iota(shape, 1) // K).astype(F32)
    rel_up = iota(shape, 0).astype(F32) - row_up - (iota(shape, 1) // K).astype(F32)
    images = []
    for t in range(frames):
        at = PK_RAW + 16 * t
        near = jnp.concatenate([up[at : at + 16], raw[t, 0:16].astype(F32)], axis=0)
        zone = []
        for start, meta, row in ((8, meta_up, META_SHIFT), (16, meta_own, META_FIRST)):

            def rows_at(a, start=start):
                return near[start + a : start + a + RIM + 1]

            zone.append(warp(rows_at, RIM, *shift_lines(meta, row, frames, t)))
        images.append(jnp.concatenate(zone, axis=0).astype(BF16))
        top[t] = zone[1]
    images = jnp.concatenate(images, axis=0)
    half = TILE * K // 2
    left = dot_nt(jnp.concatenate([tiles_up[K:], images], axis=0), tiles_own[0:half])
    right = dot_nt(jnp.concatenate([tiles_up[9 * K :], images], axis=0), tiles_own[half:])
    write_tile(out, 8, gram_above(left, right, as_column(row_up), row_own), range(8))
    by_own = jnp.concatenate([left[15 * K :], right[7 * K :]], axis=1)
    by_up = dot_nt(images, tiles_up)
    for t in range(frames):
        at = 2 * RIM * t
        sums = (
            pick_rows(by_own[at : at + 2 * RIM], rel_own) + part[t : t + 1],
            pick_rows(by_up[at : at + 2 * RIM], rel_up),
        )
        both = [lane_pick(jnp.broadcast_to(x, (8, LANES)), source) for x in sums]
        found = jnp.where(frame == t, jnp.where(first_kind, both[0], both[1]), found)
    out[1:2] = found[0:1]
    out[3:4] = line[0:1]


def sweep_kernel(frames, slabs, gathered, out, sent, turned, g_ref):
    per = K // slabs
    lane = iota((8, LANES), 1)
    sub = iota((8, LANES), 0)
    quarter = lane // K
    slab = lane % slabs
    frame = (lane % K) // slabs
    me = lax.axis_index("slab")
    later = jnp.minimum(slab + 1, slabs - 1)
    here = gather_place(slab ^ me, slabs)
    there = gather_place(later ^ me, slabs)

    def turn(tile):
        arrays = []
        for n in range(2 // per):
            lines = []
            for lq in range(4):
                for h in range(per):
                    jh = n * per + h
                    lines.append(gathered[pl.ds(8 * tile + 2 * lq + jh, slabs, stride=16), :])
            at = (2 * tile + n) * LANES
            turned[at : at + LANES] = jnp.concatenate(lines, axis=0).T
            arrays.append(at)
        return (arrays * 2)[:2] if per == 2 else arrays

    def half_lane(jh):
        return jh * slabs if per == 2 else 0

    base_g = turn(0)
    base_x = turn(1)

    for jh in range(2):
        index = quarter * K + half_lane(jh) + here
        for j in range(16):
            n = 16 * jh + j
            rows = turned[base_x[jh] + 8 * j : base_x[jh] + 8 * j + 8]
            g_ref[8 * (K + n) : 8 * (K + n) + 8] = lane_pick(rows, index)
            rows = turned[base_g[jh] + 8 * j : base_g[jh] + 8 * j + 8]
            g_ref[8 * n : 8 * n + 8] = lane_pick(rows, index)
    for r in range(8):
        parts = [turned[pl.ds(base_g[0] + 64 * v + r, 8, stride=8), :] for v in range(2)]
        for oq in (2, 3):
            n = 8 * oq + r
            index = oq * K + half_lane(0) + here
            corner = jnp.where(quarter == 0, lane_pick(parts[0], index), lane_pick(parts[1], index))
            at = pl.ds(8 * n, 8)
            g_ref[at, :] = jnp.where(quarter < 2, corner, g_ref[at, :])
    inner = slab < slabs - 1
    for r in range(8):
        parts = [
            [turned[pl.ds(base_x[uh] + 64 * v + r, 8, stride=8), :] for v in range(2)]
            for uh in range(3 - per)
        ]
        if per == 2:
            even, odd = parts[0]
            merged = (
                jnp.where(quarter % 2 == 0, even, pltpu.roll(odd, K, 1)),
                jnp.where(quarter % 2 == 0, pltpu.roll(even, LANES - K, 1), odd),
            )
        for oq in range(4):
            if per == 2:
                index = (2 * (oq // 2) + quarter % 2) * K + (quarter // 2) * slabs + there
                value = lane_pick(merged[oq % 2], index)
            else:
                index = oq * K + there
                value = lane_pick(parts[0][0], index)
                for uq in range(1, 4):
                    value = jnp.where(quarter == uq, lane_pick(parts[uq // 2][uq % 2], index), value)
            n = 2 * K + 8 * oq + r
            g_ref[8 * n : 8 * n + 8] = jnp.where(inner, value, 0.0)

    lanes_of = half_lane(1)
    states = []
    for nv in range(frames // per):
        found = []
        for line, kind, shifted in ((0, 0, False), (0, 1, True), (1, 0, False), (1, 1, False)):
            index = line * K + lanes_of + (there if shifted else here)
            value = jnp.zeros((8, LANES), F32)
            for lq in range(4):
                for h in range(per):
                    n = 8 * kind + 2 * lq + nv * per + h
                    rows = turned[base_g[1] + 8 * n : base_g[1] + 8 * n + 8]
                    value = jnp.where((quarter == lq) & (frame == h), lane_pick(rows, index), value)
            found.append(jnp.where(inner, value, 0.0) if shifted else value)
        states.append(found)
    norm = jnp.zeros((8, LANES), F32)
    for n in range(K):
        mine = (sub == n % 8) & (quarter == n // 8)
        norm = jnp.where(mine, g_ref[8 * n : 8 * n + 8], norm)
    inverse = 1.0 / norm
    block_of = states[0][3]

    local = lane % K
    before = jnp.where(slab == 0, local, local - 1)
    after = jnp.where(inner, local + 1, local)

    def coupled(change):
        totals = [None] * 8
        picks = [[lane_pick(change, q * K + place) for q in range(4)] for place in (local, before, after)]
        for kind in range(3):
            for q in range(4):
                for r in range(8):
                    n = kind * K + 8 * q + r
                    term = g_ref[8 * n : 8 * n + 8] * jnp.broadcast_to(picks[kind][q][r : r + 1], (8, LANES))
                    totals[r] = term if totals[r] is None else totals[r] + term
        while len(totals) > 1:
            totals = [functools.reduce(jnp.add, totals[i : i + 2]) for i in range(0, len(totals), 2)]
        return totals[0]

    def step(n, carry):
        p, change, traces = carry
        p = [x - coupled(c) for x, c in zip(p, change)]
        scale = jnp.where(block_of == lax.rem(n, BLOCKS).astype(F32), inverse, 0.0)
        change = [x * scale for x in p]
        return p, change, [x + c for x, c in zip(traces, change)]

    first = [s[2] for s in states]
    start = ([s[0] + s[1] for s in states], first, first)
    _, _, traces = lax.fori_loop(0, SWEEPS * BLOCKS, step, start, unroll=12)

    mine = sub == lane % 8

    def lines_of(other):
        lines = []
        for t in range(frames):
            index = ((lane % K) // 8) * K + (t % per) * slabs + other
            value = jnp.where(mine, lane_pick(traces[t // per], index), 0.0)
            lines.append(jnp.sum(value, axis=0, keepdims=True))
        return lines

    def sums_of(lines):
        return [functools.reduce(jnp.add, lines), functools.reduce(jnp.add, [x * x for x in lines])]

    own = lines_of(me)
    lines = own + lines_of(jnp.maximum(me - 1, 0)) + lines_of(jnp.minimum(me + 1, slabs - 1))
    for n, line in enumerate(lines + sums_of(own)):
        out[n : n + 1] = line
    for n, line in enumerate(sums_of(lines_of(me ^ 1))):
        sent[n : n + 1] = line


def render(rel, values, tiles, groups=range(4)):
    mixed = jnp.concatenate([jnp.where(rel == float(4 * m), values, 0.0) for m in groups], axis=1)
    high = mixed.astype(BF16)
    low = (mixed - high.astype(F32)).astype(BF16)
    return jnp.dot(high, tiles, preferred_element_type=F32) + jnp.dot(
        low, tiles, preferred_element_type=F32
    )


def finish_kernel(own, by_middle, by_pair, corr, top, tail, lines, t_own, t_up, t_low, values, out):
    frames, rows, _ = corr.shape
    slab = lax.axis_index("slab")
    meta_up = from_above(slab, by_pair[PK_META:PK_ALL], by_middle[PK_META:PK_ALL])
    row_own = own[PK_META:PK_ALL].astype(F32)[META_ROW : META_ROW + 1]
    row_up = meta_up[META_ROW : META_ROW + 1] - float(rows)
    row_low = lines[0:1] + float(rows)
    y = (iota((rows, LANES), 0) + RIM).astype(F32)
    group = (iota((rows, LANES), 1) // K).astype(F32)
    rel_own = y - row_own - group
    rel_up = (y - row_up - group)[0:RIM]
    rel_low = (y - row_low - group)[rows - RIM : rows]
    half = t_low.shape[0]
    for t in range(frames):
        image = render(rel_own, values[t : t + 1], t_own[...])
        above = render(rel_up, values[frames + t : frames + t + 1], t_up[half:], (2, 3))
        below = render(rel_low, values[2 * frames + t : 2 * frames + t + 1], t_low[...], (0, 1))
        out[t, 0:RIM] = top[t].astype(BF16).astype(F32) - image[0:RIM] - above
        out[t, RIM : rows - RIM] = corr[t].astype(F32)[RIM : rows - RIM] - image[RIM : rows - RIM]
        out[t, rows - RIM : rows] = tail[t].astype(BF16).astype(F32) - image[rows - RIM : rows] - below


def score_kernel(frame_total, values, *rest):
    out = rest[-1]
    frames = out.shape[0]
    sums = values[3 * frames : 3 * frames + 2]
    for other in rest[:-1]:
        sums = sums + other[0:2]
    mean = sums[0:1] / frame_total
    spread = sums[1:2] / frame_total - mean * mean
    out[...] = ((values[0:frames] - mean) / jnp.sqrt(spread + EPSILON))[:, 0:K]


def local_call(kernel, out_shape, scratch_shapes, flops, args, space=pltpu.VMEM):
    args = [pltpu.with_memory_space_constraint(x, space) for x in args]
    return pl.pallas_call(
        kernel,
        out_shape=out_shape,
        in_specs=[pl.BlockSpec(memory_space=space)] * len(args),
        out_specs=jax.tree.map(lambda _: VMEM_SPEC, out_shape),
        scratch_shapes=scratch_shapes,
        compiler_params=pltpu.CompilerParams(vmem_limit_bytes=VMEM_BYTES),
        cost_estimate=pl.CostEstimate(flops=flops, bytes_accessed=1 << 18, transcendentals=0),
    )(*args)


def shards(raw_movie, shifts, footprints, anchors, block_of, init_traces):
    frames, rows, cols = raw_movie.shape
    slabs = lax.axis_size("slab")
    frame_parts = lax.axis_size("frames")
    small = pltpu.VMEM((8, LANES), F32)
    tiles = pltpu.VMEM((TILE * K, LANES), BF16)
    half_tiles = pltpu.VMEM((TILE * K // 2, LANES), BF16)
    image = pltpu.VMEM((frames, rows, LANES), BF16)
    rim = pltpu.VMEM((frames, RIM, LANES), F32)
    extra_rows = K + 8 * frames + 16

    given = (
        raw_movie,
        footprints.transpose(1, 2, 0),
        shifts.transpose(0, 1, 3, 2),
        anchors.T,
        init_traces.T,
        block_of[None],
    )
    pack, pair, raw, line = local_call(
        pack_kernel,
        (pltpu.VMEM((PK_ALL, LANES), BF16), pltpu.VMEM((PK_ALL, LANES), BF16), image, small),
        [pltpu.VMEM(x.shape, x.dtype) for x in given[1:]] + [pltpu.SemaphoreType.DMA((len(given),))],
        10**8,
        given,
        space=pltpu.HBM,
    )
    pairs, middle = neighbour_routes(slabs)
    by_middle = lax.ppermute(pack, "slab", middle)
    by_pair = lax.ppermute(pair, "slab", pairs)

    tile, part, t_own, corr, extra = local_call(
        own_kernel,
        (small, small, tiles, image, pltpu.VMEM((extra_rows, LANES), BF16)),
        [pltpu.VMEM((rows + 32, LANES), F32)],
        10**9,
        (pack, raw),
    )
    gathered, t_up, top = local_call(
        edge_kernel,
        (pltpu.VMEM((16, LANES), F32), tiles, rim),
        [],
        10**9,
        (pack, raw, by_middle, by_pair, line, t_own, tile, part),
    )
    for n, mask in enumerate(gather_masks(slabs)):
        route = [(i, i ^ mask) for i in range(slabs)]
        if n == 0:
            extra, gathered = lax.optimization_barrier((extra, gathered))
        other = lax.ppermute(gathered, "slab", route)
        if n == 0:
            by_cross = lax.ppermute(extra, "slab", [(i, i ^ 3) for i in range(slabs)])
        gathered = jnp.concatenate([gathered, other], axis=0)

    t_low, tail, lines = local_call(
        low_kernel,
        (half_tiles, rim, small),
        [pltpu.VMEM((24, LANES), F32)],
        10**9,
        (pack, raw, by_middle, by_pair, by_cross),
    )
    values, sent = local_call(
        functools.partial(sweep_kernel, frames, slabs),
        (small, small),
        [pltpu.VMEM((4 * LANES, LANES), F32), pltpu.VMEM((8 * 3 * K, LANES), F32)],
        10**9,
        (gathered,),
    )

    others = []
    for hop in range(1, frame_parts):
        route = [
            (f * slabs + s, ((f + hop) % frame_parts) * slabs + (s ^ 1))
            for f in range(frame_parts)
            for s in range(slabs)
        ]
        others.append(lax.ppermute(sent, ("frames", "slab"), route))

    residual = local_call(
        finish_kernel,
        jax.ShapeDtypeStruct((frames, rows, LANES), F32),
        [],
        10**9,
        (pack, by_middle, by_pair, corr, top, tail, lines, t_own, t_up, t_low, values),
    )

    traces_z = local_call(
        functools.partial(score_kernel, frames * frame_parts),
        jax.ShapeDtypeStruct((frames, K), F32),
        [],
        10**4,
        (values, *others),
    )
    return traces_z.T, residual


def solution(mesh):
    in_specs = (
        P("frames", "slab", None),
        P(None, "frames", "slab", None),
        P("slab", None, None),
        P("slab", None),
        P("slab"),
        P("slab", "frames"),
    )
    out_specs = (P("slab", "frames"), P("frames", "slab", None))
    return jax.shard_map(shards, mesh=mesh, in_specs=in_specs, out_specs=out_specs, check_vma=False)
```

```python
import functools

import jax
import jax.numpy as jnp
from jax import lax
from jax.experimental import pallas as pl
from jax.experimental.pallas import tpu as pltpu
from jax.sharding import PartitionSpec as P

SHIFT = 3
PATCH_R = 32
BLOCKS = 4
SWEEPS = 3
TILE = 16
RIM = 8
LANES = 128
K = 32
GROUPS = LANES // K
WEIGHT_NEAR = 0.75
WEIGHT_FAR = 0.25
EPSILON = 1e-05
F32 = jnp.float32
BF16 = jnp.bfloat16

PK_RAW = 64
PK_META = 96
PK_ALL = 112
META_ROW = 0
META_COL = 1
META_SHIFT = 2
META_FIRST = 6
VMEM_BYTES = 8 << 20
VMEM_SPEC = pl.BlockSpec(memory_space=pltpu.VMEM)


def iota(shape, axis):
    return lax.broadcasted_iota(jnp.int32, shape, axis)


def lane_pick(values, index):
    return jnp.take_along_axis(values, index, axis=1, mode="promise_in_bounds")


def as_column(line):
    own = iota((K, LANES), 0) == iota((K, LANES), 1)
    return jnp.sum(jnp.where(own, line, 0.0), axis=1, keepdims=True)


def placed_tiles(tiles, col_line):
    col = as_column(col_line).astype(jnp.int32)
    offset = iota((K, LANES), 1) - col
    inside = (offset >= 0) & (offset < TILE)
    base = jnp.clip(offset, 0, TILE - 1)
    out = []
    for i in range(tiles.shape[0] // K * 8):
        half, part = divmod(i, 8)
        tile = tiles[half * K : (half + 1) * K].astype(F32)
        out.append(jnp.where(inside, lane_pick(tile, base + part * TILE), 0.0))
    return jnp.concatenate(out, axis=0).astype(BF16)


def dot_nt(a, b):
    return lax.dot_general(a, b, (((1,), (1,)), ((), ())), preferred_element_type=F32)


def fold_lanes(x):
    return (x + pltpu.roll(x, K, 1)) + (pltpu.roll(x, 2 * K, 1) + pltpu.roll(x, 3 * K, 1))


def masked_sum(block, diff, places):
    total = jnp.zeros((K, LANES), F32)
    for q in places:
        parts = [block(4 * m - q, m) for m in range(4) if 0 <= 4 * m - q < TILE]
        if parts:
            total = total + jnp.where(diff == float(q), functools.reduce(jnp.add, parts), 0.0)
    return fold_lanes(total)


def row_diff(row_a, row_b):
    return row_a - row_b - (iota((K, LANES), 1) // K).astype(F32)


def gram(tiles_a, tiles_b, row_a, row_b):
    full = dot_nt(tiles_a, tiles_b)

    def block(i, m):
        return full[i * K : (i + 1) * K, m * LANES : (m + 1) * LANES]

    return masked_sum(block, row_diff(row_a, row_b), range(-(TILE - 1), TILE))


def gram_above(left, right, row_a, row_b):
    def block(i, m):
        part, first = (left, 1) if m < 2 else (right, 9)
        lane = (m % 2) * LANES
        return part[(i - first) * K : (i - first + 1) * K, lane : lane + LANES]

    return masked_sum(block, row_diff(row_a, row_b), range(-(TILE - 1), 0))


def pick_rows(part, rel):
    total = jnp.zeros(rel.shape, F32)
    for m in range(4):
        total = total + jnp.where(rel == float(4 * m), part[:, m * LANES : (m + 1) * LANES], 0.0)
    return fold_lanes(jnp.sum(total, axis=0, keepdims=True))


def project(corr, tiles, rel):
    return pick_rows(dot_nt(corr, tiles), rel)


def neighbour_routes(slabs):
    pairs = [(i, i ^ 1) for i in range(slabs)]
    ends = [(0, 1), (1, 2), (2, 0), (slabs - 3, slabs - 2), (slabs - 2, slabs - 1), (slabs - 1, slabs - 3)]
    middle = [p for i in range(3, slabs - 4, 2) for p in ((i, i + 1), (i + 1, i))]
    return pairs, ends + middle


def from_above(slab, by_pair, by_middle):
    found = jnp.where(slab % 2 == 1, by_pair.astype(F32), by_middle.astype(F32))
    return jnp.where(slab == 0, 0.0, found)


def below_part(pack, firsts):
    return jnp.concatenate([pack[0:K].astype(F32), *firsts, pack[PK_META:PK_ALL].astype(F32)], axis=0)


def received_below(pack, frames):
    firsts = [pack[PK_RAW + 16 * t : PK_RAW + 16 * t + 16].astype(F32)[0:8] for t in range(frames)]
    return below_part(pack, firsts)


def write_edge_rows(out, raw, to_below):
    frames, rows, _ = raw.shape
    for t in range(frames):
        last, first = raw[t, rows - 16 : rows].astype(F32), raw[t, 0:16].astype(F32)
        out[PK_RAW + 16 * t : PK_RAW + 16 * t + 16] = jnp.where(to_below, last, first).astype(BF16)


def from_below(slab, slabs, by_pair, by_middle, by_cross):
    odd = jnp.where((slab == 1) | (slab == slabs - 3), by_cross, by_middle)
    found = jnp.where(slab % 2 == 0, by_pair, odd)
    return jnp.where(slab == slabs - 1, 0.0, found)


def gather_masks(slabs):
    bits = slabs.bit_length() - 1
    return [(1 << b) | 1 for b in range(bits - 1, 0, -1)] + [1]


def gather_place(diff, slabs):
    bits = slabs.bit_length() - 1
    odd = diff & 1
    place = jnp.zeros_like(diff)
    for r in range(bits - 1):
        bit = (diff >> (bits - 1 - r)) & 1
        place = place + bit * (1 << r)
        odd = odd ^ bit
    return place + odd * (1 << (bits - 1))


def gather_source():
    place = iota((8, LANES), 1)
    return 8 * ((place // 16) % 4) + place % 8, (place // 8) % 2, place < LANES // 2


def pack_kernel(*refs):
    count = 6
    given, (out, pair, raw, line) = refs[:count], refs[count : count + 4]
    held = refs[count + 4 : 2 * count + 3]
    sems = refs[-1]
    tiles, shifts, anchors, init, block_of = held
    copies = [
        pltpu.make_async_copy(source, target, sems.at[n])
        for n, (source, target) in enumerate(zip(given, (raw, *held)))
    ]
    for copy in copies:
        copy.start()
    raw_copy, tiles_copy, *small_copies = copies
    frames, rows, _ = raw.shape
    last = rows // PATCH_R - 1
    slab = lax.axis_index("slab")
    base = slab * rows - RIM
    for copy in small_copies:
        copy.wait()
    places = jnp.concatenate([anchors[...].astype(F32)] * GROUPS, axis=1)
    sub = iota((16, LANES), 0)
    meta = jnp.where(sub == META_COL, places[1:2], 0.0)
    meta = jnp.where(sub == META_ROW, places[0:1] - base.astype(F32), meta)
    for t in range(frames):
        for axis in range(2):
            moves = shifts[axis, t].astype(F32)
            for place, patch in ((META_SHIFT, last), (META_FIRST, 0)):
                meta = jnp.where(sub == place + axis * frames + t, moves[:, patch : patch + 1], meta)
    out[PK_META:PK_ALL] = meta.astype(BF16)
    pair[PK_META:PK_ALL] = meta.astype(BF16)
    source, frame, first_kind = gather_source()
    inits = jnp.concatenate([init[...]] * GROUPS, axis=1)
    blocks = jnp.concatenate([block_of[...].astype(F32)] * GROUPS, axis=1)
    found = jnp.zeros((8, LANES), F32)
    for t in range(frames):
        both = [lane_pick(jnp.broadcast_to(x, (8, LANES)), source) for x in (inits[t : t + 1], blocks)]
        found = jnp.where(frame == t, jnp.where(first_kind, both[0], both[1]), found)
    line[...] = found
    raw_copy.wait()
    write_edge_rows(out, raw, slab % 2 == 1)
    write_edge_rows(pair, raw, slab % 2 == 0)
    tiles_copy.wait()
    for half in range(2):
        part = tiles[8 * half : 8 * half + 8].astype(F32).reshape(LANES, K)
        part = part.T.astype(BF16)
        out[K * half : K * half + K] = part
        pair[K * half : K * half + K] = part


def write_tile(out, first, mat, rows):
    lane = iota((K, LANES), 1)
    own = lane // 8 == iota((K, LANES), 0) % 16
    for lq in range(4):
        part = jnp.where(own, lane_pick(mat, 8 * lq + lane % 8), 0.0)
        for jh in range(2):
            if 2 * lq + jh in rows:
                out[first + 2 * lq + jh : first + 2 * lq + jh + 1] = jnp.sum(
                    part[16 * jh : 16 * jh + 16], axis=0, keepdims=True
                )


def warp(rows_at, count, a_line, c_line):
    both = jnp.zeros((count, LANES), F32)
    for a in range(-SHIFT, SHIFT + 1):
        window = rows_at(a)
        blend = WEIGHT_NEAR * window[0:count] + WEIGHT_FAR * window[1 : count + 1]
        both = jnp.where(a_line == float(a), blend, both)
    place = iota((count, LANES), 1) + c_line.astype(jnp.int32)
    moved = lane_pick(both, jnp.clip(place, 0, LANES - 1))
    return jnp.where((place >= 0) & (place < LANES), moved, 0.0)


def shift_lines(meta, row, frames, t):
    return meta[row + t : row + t + 1], meta[row + frames + t : row + frames + t + 1]


def own_kernel(own, raw, tile, part, t_own, corr, extra, ext):
    frames, rows, _ = raw.shape
    slab = lax.axis_index("slab")
    is_last = slab == lax.axis_size("slab") - 1
    extra[...] = below_part(own[...], [raw[t, 0:16].astype(F32)[0:8] for t in range(frames)])
    meta = own[PK_META:PK_ALL].astype(F32)
    row = meta[META_ROW : META_ROW + 1]
    tiles = placed_tiles(own[0 : 2 * K], meta[META_COL : META_COL + 1])
    t_own[...] = tiles
    tile[...] = jnp.zeros((8, LANES), F32)
    part[...] = jnp.zeros((8, LANES), F32)
    write_tile(tile, 0, gram(tiles, tiles, as_column(row), row), (0, 2, 4, 5, 6, 7))
    y = iota((rows, LANES), 0)
    keep = (y >= RIM) & ((y < rows - RIM) | is_last)
    rel = (y + RIM).astype(F32) - row - (iota((rows, LANES), 1) // K).astype(F32)
    for t in range(frames):
        ext[0:16] = jnp.zeros((16, LANES), F32)
        ext[16 : 16 + rows] = raw[t].astype(F32)
        ext[16 + rows : 32 + rows] = jnp.zeros((16, LANES), F32)
        parts = []
        for p, row_of in ((0, META_FIRST), (1, META_SHIFT)):

            def rows_at(a, first=16 + p * PATCH_R):
                return ext[first + a : first + a + PATCH_R + 1]

            parts.append(warp(rows_at, PATCH_R, *shift_lines(meta, row_of, frames, t)))
        image = jnp.concatenate(parts, axis=0)
        corr[t] = image.astype(BF16)
        part[t : t + 1] = project(jnp.where(keep, image, 0.0).astype(BF16), tiles, rel)


def low_kernel(own, raw, by_middle, by_pair, by_cross, tiles, tail, lines, ext):
    frames, rows, _ = raw.shape
    low = from_below(
        lax.axis_index("slab"),
        lax.axis_size("slab"),
        received_below(by_pair[...], frames),
        received_below(by_middle[...], frames),
        by_cross[...],
    )
    meta = own[PK_META:PK_ALL].astype(F32)
    meta_low = low[K + 8 * frames :]
    tiles[...] = placed_tiles(low[0:K], meta_low[META_COL : META_COL + 1])
    lines[...] = jnp.broadcast_to(meta_low[META_ROW : META_ROW + 1], (8, LANES))
    for t in range(frames):
        ext[0:16] = raw[t, rows - 16 : rows].astype(F32)
        ext[16:24] = low[K + 8 * t : K + 8 * t + 8]

        def rows_at(a):
            return ext[8 + a : 17 + a]

        tail[t] = warp(rows_at, RIM, *shift_lines(meta, META_SHIFT, frames, t))


def edge_kernel(own, raw, by_middle, by_pair, line, t_own, tile, part, out, t_up, top):
    frames, rows, _ = raw.shape
    up = from_above(lax.axis_index("slab"), by_pair[...], by_middle[...])
    meta_own = own[PK_META:PK_ALL].astype(F32)
    meta_up = up[PK_META:PK_ALL]
    row_own = meta_own[META_ROW : META_ROW + 1]
    row_up = meta_up[META_ROW : META_ROW + 1] - float(rows)
    tiles_own = t_own[...]
    tiles_up = placed_tiles(up[0 : 2 * K], meta_up[META_COL : META_COL + 1])
    t_up[...] = tiles_up
    out[0:8] = tile[...]
    source, frame, first_kind = gather_source()
    found = jnp.zeros((8, LANES), F32)
    shape = (2 * RIM, LANES)
    rel_own = iota(shape, 0).astype(F32) - row_own - (iota(shape, 1) // K).astype(F32)
    rel_up = iota(shape, 0).astype(F32) - row_up - (iota(shape, 1) // K).astype(F32)
    images = []
    for t in range(frames):
        at = PK_RAW + 16 * t
        near = jnp.concatenate([up[at : at + 16], raw[t, 0:16].astype(F32)], axis=0)
        zone = []
        for start, meta, row in ((8, meta_up, META_SHIFT), (16, meta_own, META_FIRST)):

            def rows_at(a, start=start):
                return near[start + a : start + a + RIM + 1]

            zone.append(warp(rows_at, RIM, *shift_lines(meta, row, frames, t)))
        images.append(jnp.concatenate(zone, axis=0).astype(BF16))
        top[t] = zone[1]
    images = jnp.concatenate(images, axis=0)
    half = TILE * K // 2
    left = dot_nt(jnp.concatenate([tiles_up[K:], images], axis=0), tiles_own[0:half])
    right = dot_nt(jnp.concatenate([tiles_up[9 * K :], images], axis=0), tiles_own[half:])
    write_tile(out, 8, gram_above(left, right, as_column(row_up), row_own), range(8))
    by_own = jnp.concatenate([left[15 * K :], right[7 * K :]], axis=1)
    by_up = dot_nt(images, tiles_up)
    for t in range(frames):
        at = 2 * RIM * t
        sums = (
            pick_rows(by_own[at : at + 2 * RIM], rel_own) + part[t : t + 1],
            pick_rows(by_up[at : at + 2 * RIM], rel_up),
        )
        both = [lane_pick(jnp.broadcast_to(x, (8, LANES)), source) for x in sums]
        found = jnp.where(frame == t, jnp.where(first_kind, both[0], both[1]), found)
    out[1:2] = found[0:1]
    out[3:4] = line[0:1]


def sweep_kernel(frames, slabs, gathered, out, sent, turned, g_ref):
    per = K // slabs
    lane = iota((8, LANES), 1)
    sub = iota((8, LANES), 0)
    quarter = lane // K
    slab = lane % slabs
    frame = (lane % K) // slabs
    me = lax.axis_index("slab")
    later = jnp.minimum(slab + 1, slabs - 1)
    here = gather_place(slab ^ me, slabs)
    there = gather_place(later ^ me, slabs)

    def turn(tile):
        arrays = []
        for n in range(2 // per):
            lines = []
            for lq in range(4):
                for h in range(per):
                    jh = n * per + h
                    lines.append(gathered[pl.ds(8 * tile + 2 * lq + jh, slabs, stride=16), :])
            at = (2 * tile + n) * LANES
            turned[at : at + LANES] = jnp.concatenate(lines, axis=0).T
            arrays.append(at)
        return (arrays * 2)[:2] if per == 2 else arrays

    def half_lane(jh):
        return jh * slabs if per == 2 else 0

    base_g = turn(0)
    base_x = turn(1)

    for jh in range(2):
        index = quarter * K + half_lane(jh) + here
        for j in range(16):
            n = 16 * jh + j
            rows = turned[base_x[jh] + 8 * j : base_x[jh] + 8 * j + 8]
            g_ref[8 * (K + n) : 8 * (K + n) + 8] = lane_pick(rows, index)
            rows = turned[base_g[jh] + 8 * j : base_g[jh] + 8 * j + 8]
            g_ref[8 * n : 8 * n + 8] = lane_pick(rows, index)
    for r in range(8):
        parts = [turned[pl.ds(base_g[0] + 64 * v + r, 8, stride=8), :] for v in range(2)]
        for oq in (2, 3):
            n = 8 * oq + r
            index = oq * K + half_lane(0) + here
            corner = jnp.where(quarter == 0, lane_pick(parts[0], index), lane_pick(parts[1], index))
            at = pl.ds(8 * n, 8)
            g_ref[at, :] = jnp.where(quarter < 2, corner, g_ref[at, :])
    inner = slab < slabs - 1
    for r in range(8):
        parts = [
            [turned[pl.ds(base_x[uh] + 64 * v + r, 8, stride=8), :] for v in range(2)]
            for uh in range(3 - per)
        ]
        if per == 2:
            even, odd = parts[0]
            merged = (
                jnp.where(quarter % 2 == 0, even, pltpu.roll(odd, K, 1)),
                jnp.where(quarter % 2 == 0, pltpu.roll(even, LANES - K, 1), odd),
            )
        for oq in range(4):
            if per == 2:
                index = (2 * (oq // 2) + quarter % 2) * K + (quarter // 2) * slabs + there
                value = lane_pick(merged[oq % 2], index)
            else:
                index = oq * K + there
                value = lane_pick(parts[0][0], index)
                for uq in range(1, 4):
                    value = jnp.where(quarter == uq, lane_pick(parts[uq // 2][uq % 2], index), value)
            n = 2 * K + 8 * oq + r
            g_ref[8 * n : 8 * n + 8] = jnp.where(inner, value, 0.0)

    lanes_of = half_lane(1)
    states = []
    for nv in range(frames // per):
        found = []
        for line, kind, shifted in ((0, 0, False), (0, 1, True), (1, 0, False), (1, 1, False)):
            index = line * K + lanes_of + (there if shifted else here)
            value = jnp.zeros((8, LANES), F32)
            for lq in range(4):
                for h in range(per):
                    n = 8 * kind + 2 * lq + nv * per + h
                    rows = turned[base_g[1] + 8 * n : base_g[1] + 8 * n + 8]
                    value = jnp.where((quarter == lq) & (frame == h), lane_pick(rows, index), value)
            found.append(jnp.where(inner, value, 0.0) if shifted else value)
        states.append(found)
    norm = jnp.zeros((8, LANES), F32)
    for n in range(K):
        mine = (sub == n % 8) & (quarter == n // 8)
        norm = jnp.where(mine, g_ref[8 * n : 8 * n + 8], norm)
    inverse = 1.0 / norm
    block_of = states[0][3]

    local = lane % K
    before = jnp.where(slab == 0, local, local - 1)
    after = jnp.where(inner, local + 1, local)

    def coupled(change):
        totals = [None] * 8
        picks = [[lane_pick(change, q * K + place) for q in range(4)] for place in (local, before, after)]
        for kind in range(3):
            for q in range(4):
                for r in range(8):
                    n = kind * K + 8 * q + r
                    term = g_ref[8 * n : 8 * n + 8] * jnp.broadcast_to(picks[kind][q][r : r + 1], (8, LANES))
                    totals[r] = term if totals[r] is None else totals[r] + term
        while len(totals) > 1:
            totals = [functools.reduce(jnp.add, totals[i : i + 2]) for i in range(0, len(totals), 2)]
        return totals[0]

    def step(n, carry):
        p, change, traces = carry
        p = [x - coupled(c) for x, c in zip(p, change)]
        scale = jnp.where(block_of == lax.rem(n, BLOCKS).astype(F32), inverse, 0.0)
        change = [x * scale for x in p]
        return p, change, [x + c for x, c in zip(traces, change)]

    first = [s[2] for s in states]
    start = ([s[0] + s[1] for s in states], first, first)
    _, _, traces = lax.fori_loop(0, SWEEPS * BLOCKS, step, start, unroll=12)

    mine = sub == lane % 8

    def lines_of(other):
        lines = []
        for t in range(frames):
            index = ((lane % K) // 8) * K + (t % per) * slabs + other
            value = jnp.where(mine, lane_pick(traces[t // per], index), 0.0)
            lines.append(jnp.sum(value, axis=0, keepdims=True))
        return lines

    def sums_of(lines):
        return [functools.reduce(jnp.add, lines), functools.reduce(jnp.add, [x * x for x in lines])]

    own = lines_of(me)
    lines = own + lines_of(jnp.maximum(me - 1, 0)) + lines_of(jnp.minimum(me + 1, slabs - 1))
    for n, line in enumerate(lines + sums_of(own)):
        out[n : n + 1] = line
    for n, line in enumerate(sums_of(lines_of(me ^ 1))):
        sent[n : n + 1] = line


def render(rel, values, tiles, groups=range(4)):
    mixed = jnp.concatenate([jnp.where(rel == float(4 * m), values, 0.0) for m in groups], axis=1)
    high = mixed.astype(BF16)
    low = (mixed - high.astype(F32)).astype(BF16)
    return jnp.dot(high, tiles, preferred_element_type=F32) + jnp.dot(
        low, tiles, preferred_element_type=F32
    )


def finish_kernel(own, by_middle, by_pair, corr, top, tail, lines, t_own, t_up, t_low, values, out):
    frames, rows, _ = corr.shape
    slab = lax.axis_index("slab")
    meta_up = from_above(slab, by_pair[PK_META:PK_ALL], by_middle[PK_META:PK_ALL])
    row_own = own[PK_META:PK_ALL].astype(F32)[META_ROW : META_ROW + 1]
    row_up = meta_up[META_ROW : META_ROW + 1] - float(rows)
    row_low = lines[0:1] + float(rows)
    y = (iota((rows, LANES), 0) + RIM).astype(F32)
    group = (iota((rows, LANES), 1) // K).astype(F32)
    rel_own = y - row_own - group
    rel_up = (y - row_up - group)[0:RIM]
    rel_low = (y - row_low - group)[rows - RIM : rows]
    half = t_low.shape[0]
    for t in range(frames):
        image = render(rel_own, values[t : t + 1], t_own[...])
        above = render(rel_up, values[frames + t : frames + t + 1], t_up[half:], (2, 3))
        below = render(rel_low, values[2 * frames + t : 2 * frames + t + 1], t_low[...], (0, 1))
        out[t, 0:RIM] = top[t].astype(BF16).astype(F32) - image[0:RIM] - above
        out[t, RIM : rows - RIM] = corr[t].astype(F32)[RIM : rows - RIM] - image[RIM : rows - RIM]
        out[t, rows - RIM : rows] = tail[t].astype(BF16).astype(F32) - image[rows - RIM : rows] - below


def score_kernel(frame_total, values, *rest):
    out = rest[-1]
    frames = out.shape[0]
    sums = values[3 * frames : 3 * frames + 2]
    for other in rest[:-1]:
        sums = sums + other[0:2]
    mean = sums[0:1] / frame_total
    spread = sums[1:2] / frame_total - mean * mean
    out[...] = ((values[0:frames] - mean) / jnp.sqrt(spread + EPSILON))[:, 0:K]


def local_call(kernel, out_shape, scratch_shapes, flops, args, space=pltpu.VMEM):
    args = [pltpu.with_memory_space_constraint(x, space) for x in args]
    return pl.pallas_call(
        kernel,
        out_shape=out_shape,
        in_specs=[pl.BlockSpec(memory_space=space)] * len(args),
        out_specs=jax.tree.map(lambda _: VMEM_SPEC, out_shape),
        scratch_shapes=scratch_shapes,
        compiler_params=pltpu.CompilerParams(vmem_limit_bytes=VMEM_BYTES),
        cost_estimate=pl.CostEstimate(flops=flops, bytes_accessed=1 << 18, transcendentals=0),
    )(*args)


def shards(raw_movie, shifts, footprints, anchors, block_of, init_traces):
    frames, rows, cols = raw_movie.shape
    slabs = lax.axis_size("slab")
    frame_parts = lax.axis_size("frames")
    small = pltpu.VMEM((8, LANES), F32)
    tiles = pltpu.VMEM((TILE * K, LANES), BF16)
    half_tiles = pltpu.VMEM((TILE * K // 2, LANES), BF16)
    image = pltpu.VMEM((frames, rows, LANES), BF16)
    rim = pltpu.VMEM((frames, RIM, LANES), F32)
    extra_rows = K + 8 * frames + 16

    given = (
        raw_movie,
        footprints.transpose(1, 2, 0),
        shifts.transpose(0, 1, 3, 2),
        anchors.T,
        init_traces.T,
        block_of[None],
    )
    pack, pair, raw, line = local_call(
        pack_kernel,
        (pltpu.VMEM((PK_ALL, LANES), BF16), pltpu.VMEM((PK_ALL, LANES), BF16), image, small),
        [pltpu.VMEM(x.shape, x.dtype) for x in given[1:]] + [pltpu.SemaphoreType.DMA((len(given),))],
        10**8,
        given,
        space=pltpu.HBM,
    )
    pairs, middle = neighbour_routes(slabs)
    by_middle = lax.ppermute(pack, "slab", middle)
    by_pair = lax.ppermute(pair, "slab", pairs)

    tile, part, t_own, corr, extra = local_call(
        own_kernel,
        (small, small, tiles, image, pltpu.VMEM((extra_rows, LANES), F32)),
        [pltpu.VMEM((rows + 32, LANES), F32)],
        10**9,
        (pack, raw),
    )
    gathered, t_up, top = local_call(
        edge_kernel,
        (pltpu.VMEM((16, LANES), F32), tiles, rim),
        [],
        10**9,
        (pack, raw, by_middle, by_pair, line, t_own, tile, part),
    )
    block = gathered.shape[0]
    crossing = [(i, i ^ 3) for i in range(slabs)]
    early = []
    for n, mask in enumerate(gather_masks(slabs)):
        route = [(i, i ^ mask) for i in range(slabs)]
        if mask == 3:
            rest = gathered[block * len(early) :]
            other = jnp.concatenate([*early, lax.ppermute(rest, "slab", route)], axis=0)
        else:
            other = lax.ppermute(gathered, "slab", route)
        if n == 0:
            by_cross = lax.ppermute(jnp.concatenate([extra, gathered], axis=0), "slab", crossing)
            early.append(by_cross[extra_rows:])
            by_cross = by_cross[:extra_rows]
        elif n == 1:
            early.append(lax.ppermute(gathered[block:], "slab", crossing))
        gathered = jnp.concatenate([gathered, other], axis=0)

    t_low, tail, lines = local_call(
        low_kernel,
        (half_tiles, rim, small),
        [pltpu.VMEM((24, LANES), F32)],
        10**9,
        (pack, raw, by_middle, by_pair, by_cross),
    )
    values, sent = local_call(
        functools.partial(sweep_kernel, frames, slabs),
        (small, small),
        [pltpu.VMEM((4 * LANES, LANES), F32), pltpu.VMEM((8 * 3 * K, LANES), F32)],
        10**9,
        (gathered,),
    )

    others = []
    for hop in range(1, frame_parts):
        route = [
            (f * slabs + s, ((f + hop) % frame_parts) * slabs + (s ^ 1))
            for f in range(frame_parts)
            for s in range(slabs)
        ]
        others.append(lax.ppermute(sent, ("frames", "slab"), route))

    residual = local_call(
        finish_kernel,
        jax.ShapeDtypeStruct((frames, rows, LANES), F32),
        [],
        10**9,
        (pack, by_middle, by_pair, corr, top, tail, lines, t_own, t_up, t_low, values),
    )

    traces_z = local_call(
        functools.partial(score_kernel, frames * frame_parts),
        jax.ShapeDtypeStruct((frames, K), F32),
        [],
        10**4,
        (values, *others),
    )
    return traces_z.T, residual


def solution(mesh):
    in_specs = (
        P("frames", "slab", None),
        P(None, "frames", "slab", None),
        P("slab", None, None),
        P("slab", None),
        P("slab"),
        P("slab", "frames"),
    )
    out_specs = (P("slab", "frames"), P("frames", "slab", None))
    return jax.shard_map(shards, mesh=mesh, in_specs=in_specs, out_specs=out_specs, check_vma=False)
```

```python
import functools

import jax
import jax.numpy as jnp
from jax import lax
from jax.experimental import pallas as pl
from jax.experimental.pallas import tpu as pltpu
from jax.sharding import PartitionSpec as P

SHIFT = 3
PATCH_R = 32
BLOCKS = 4
SWEEPS = 3
TILE = 16
RIM = 8
LANES = 128
K = 32
GROUPS = LANES // K
WEIGHT_NEAR = 0.75
WEIGHT_FAR = 0.25
EPSILON = 1e-05
F32 = jnp.float32
BF16 = jnp.bfloat16

PK_RAW = 64
PK_META = 96
PK_ALL = 112
META_ROW = 0
META_COL = 1
META_SHIFT = 2
META_FIRST = 6
VMEM_BYTES = 8 << 20
VMEM_SPEC = pl.BlockSpec(memory_space=pltpu.VMEM)


def iota(shape, axis):
    return lax.broadcasted_iota(jnp.int32, shape, axis)


def lane_pick(values, index):
    return jnp.take_along_axis(values, index, axis=1, mode="promise_in_bounds")


def as_column(line):
    own = iota((K, LANES), 0) == iota((K, LANES), 1)
    return jnp.sum(jnp.where(own, line, 0.0), axis=1, keepdims=True)


def placed_tiles(tiles, col_line):
    col = as_column(col_line).astype(jnp.int32)
    offset = iota((K, LANES), 1) - col
    inside = (offset >= 0) & (offset < TILE)
    base = jnp.clip(offset, 0, TILE - 1)
    out = []
    for i in range(tiles.shape[0] // K * 8):
        half, part = divmod(i, 8)
        tile = tiles[half * K : (half + 1) * K].astype(F32)
        out.append(jnp.where(inside, lane_pick(tile, base + part * TILE), 0.0))
    return jnp.concatenate(out, axis=0).astype(BF16)


def dot_nt(a, b):
    return lax.dot_general(a, b, (((1,), (1,)), ((), ())), preferred_element_type=F32)


def fold_lanes(x):
    return (x + pltpu.roll(x, K, 1)) + (pltpu.roll(x, 2 * K, 1) + pltpu.roll(x, 3 * K, 1))


def masked_sum(block, diff, places):
    total = jnp.zeros((K, LANES), F32)
    for q in places:
        parts = [block(4 * m - q, m) for m in range(4) if 0 <= 4 * m - q < TILE]
        if parts:
            total = total + jnp.where(diff == float(q), functools.reduce(jnp.add, parts), 0.0)
    return fold_lanes(total)


def row_diff(row_a, row_b):
    return row_a - row_b - (iota((K, LANES), 1) // K).astype(F32)


def gram(tiles_a, tiles_b, row_a, row_b):
    full = dot_nt(tiles_a, tiles_b)

    def block(i, m):
        return full[i * K : (i + 1) * K, m * LANES : (m + 1) * LANES]

    return masked_sum(block, row_diff(row_a, row_b), range(-(TILE - 1), TILE))


def gram_above(left, right, row_a, row_b):
    def block(i, m):
        part, first = (left, 1) if m < 2 else (right, 9)
        lane = (m % 2) * LANES
        return part[(i - first) * K : (i - first + 1) * K, lane : lane + LANES]

    return masked_sum(block, row_diff(row_a, row_b), range(-(TILE - 1), 0))


def pick_rows(part, rel):
    total = jnp.zeros(rel.shape, F32)
    for m in range(4):
        total = total + jnp.where(rel == float(4 * m), part[:, m * LANES : (m + 1) * LANES], 0.0)
    return fold_lanes(jnp.sum(total, axis=0, keepdims=True))


def project(corr, tiles, rel):
    return pick_rows(dot_nt(corr, tiles), rel)


def neighbour_routes(slabs):
    pairs = [(i, i ^ 1) for i in range(slabs)]
    runs = [range(0, 3)] + [range(i, i + 4) for i in range(3, slabs - 5, 4)] + [range(slabs - 5, slabs)]
    downwards = [(run[n], run[(n + 1) % len(run)]) for run in runs for n in range(len(run))]
    middle = [p for i in range(3, slabs - 4, 2) for p in ((i, i + 1), (i + 1, i))]
    ends = [(2, 1), (1, 0), (0, 2), (slabs - 2, slabs - 3), (slabs - 3, slabs - 1), (slabs - 1, slabs - 2)]
    return pairs, downwards, ends + middle


def from_above(slab, by_pair, by_middle):
    found = jnp.where(slab % 2 == 1, by_pair.astype(F32), by_middle.astype(F32))
    return jnp.where(slab == 0, 0.0, found)


def below_part(pack, firsts):
    return jnp.concatenate([pack[0:K].astype(F32), *firsts, pack[PK_META:PK_ALL].astype(F32)], axis=0)


def received_below(pack, frames):
    firsts = [pack[PK_RAW + 16 * t : PK_RAW + 16 * t + 16].astype(F32)[0:8] for t in range(frames)]
    return below_part(pack, firsts)


def write_edge_rows(out, raw, to_below):
    frames, rows, _ = raw.shape
    for t in range(frames):
        last, first = raw[t, rows - 16 : rows].astype(F32), raw[t, 0:16].astype(F32)
        out[PK_RAW + 16 * t : PK_RAW + 16 * t + 16] = jnp.where(to_below, last, first).astype(BF16)


def from_below(slab, slabs, by_pair, by_low):
    found = jnp.where(slab % 2 == 0, by_pair, by_low)
    return jnp.where(slab == slabs - 1, 0.0, found)


def gather_masks(slabs):
    bits = slabs.bit_length() - 1
    return [(1 << b) | 1 for b in range(bits - 1, 0, -1)] + [1]


def gather_place(diff, slabs):
    bits = slabs.bit_length() - 1
    odd = diff & 1
    place = jnp.zeros_like(diff)
    for r in range(bits - 1):
        bit = (diff >> (bits - 1 - r)) & 1
        place = place + bit * (1 << r)
        odd = odd ^ bit
    return place + odd * (1 << (bits - 1))


def gather_source():
    place = iota((8, LANES), 1)
    return 8 * ((place // 16) % 4) + place % 8, (place // 8) % 2, place < LANES // 2


def meta_lines(shifts, anchors, frames, last, base):
    places = jnp.concatenate([anchors[...].astype(F32)] * GROUPS, axis=1)
    sub = iota((16, LANES), 0)
    meta = jnp.where(sub == META_COL, places[1:2], 0.0)
    meta = jnp.where(sub == META_ROW, places[0:1] - base.astype(F32), meta)
    for t in range(frames):
        for axis in range(2):
            moves = shifts[axis, t].astype(F32)
            for place, patch in ((META_SHIFT, last), (META_FIRST, 0)):
                meta = jnp.where(sub == place + axis * frames + t, moves[:, patch : patch + 1], meta)
    return meta.astype(BF16)


def turned_tiles(tiles, half):
    return tiles[8 * half : 8 * half + 8].astype(F32).reshape(LANES, K).T.astype(BF16)


def send_kernel(raw_in, tiles_in, shifts_in, anchors_in, out, raw, tiles, shifts, anchors, sems):
    frames, rows, _ = raw.shape
    slab = lax.axis_index("slab")

    @pl.when(slab % 2 == 0)
    def _():
        out[...] = jnp.zeros((PK_ALL, LANES), BF16)

    @pl.when(slab % 2 == 1)
    def _():
        pairs = ((raw_in, raw), (tiles_in, tiles), (shifts_in, shifts), (anchors_in, anchors))
        copies = [pltpu.make_async_copy(*pair, sems.at[n]) for n, pair in enumerate(pairs)]
        for copy in copies:
            copy.start()
        copies[2].wait()
        copies[3].wait()
        out[PK_META:PK_ALL] = meta_lines(shifts, anchors, frames, rows // PATCH_R - 1, slab * rows - RIM)
        copies[0].wait()
        write_edge_rows(out, raw, True)
        copies[1].wait()
        for half in range(2):
            out[K * half : K * half + K] = turned_tiles(tiles, half)


def pack_kernel(*refs):
    count = 6
    given, (out, pair, raw, line) = refs[:count], refs[count + 1 : count + 5]
    held = refs[count + 5 : 2 * count + 4]
    sems = refs[-1]
    tiles, shifts, anchors, init, block_of = held
    copies = [
        pltpu.make_async_copy(source, target, sems.at[n])
        for n, (source, target) in enumerate(zip(given, (raw, *held)))
    ]
    for copy in copies:
        copy.start()
    raw_copy, tiles_copy, *small_copies = copies
    frames, rows, _ = raw.shape
    slab = lax.axis_index("slab")
    for copy in small_copies:
        copy.wait()
    meta = meta_lines(shifts, anchors, frames, rows // PATCH_R - 1, slab * rows - RIM)
    out[PK_META:PK_ALL] = meta
    pair[PK_META:PK_ALL] = meta
    source, frame, first_kind = gather_source()
    inits = jnp.concatenate([init[...]] * GROUPS, axis=1)
    blocks = jnp.concatenate([block_of[...].astype(F32)] * GROUPS, axis=1)
    found = jnp.zeros((8, LANES), F32)
    for t in range(frames):
        both = [lane_pick(jnp.broadcast_to(x, (8, LANES)), source) for x in (inits[t : t + 1], blocks)]
        found = jnp.where(frame == t, jnp.where(first_kind, both[0], both[1]), found)
    line[...] = found
    raw_copy.wait()
    write_edge_rows(out, raw, slab % 2 == 1)
    write_edge_rows(pair, raw, slab % 2 == 0)
    tiles_copy.wait()
    for half in range(2):
        part = turned_tiles(tiles, half)
        out[K * half : K * half + K] = part
        pair[K * half : K * half + K] = part


def write_tile(out, first, mat, rows):
    lane = iota((K, LANES), 1)
    own = lane // 8 == iota((K, LANES), 0) % 16
    for lq in range(4):
        part = jnp.where(own, lane_pick(mat, 8 * lq + lane % 8), 0.0)
        for jh in range(2):
            if 2 * lq + jh in rows:
                out[first + 2 * lq + jh : first + 2 * lq + jh + 1] = jnp.sum(
                    part[16 * jh : 16 * jh + 16], axis=0, keepdims=True
                )


def warp(rows_at, count, a_line, c_line):
    both = jnp.zeros((count, LANES), F32)
    for a in range(-SHIFT, SHIFT + 1):
        window = rows_at(a)
        blend = WEIGHT_NEAR * window[0:count] + WEIGHT_FAR * window[1 : count + 1]
        both = jnp.where(a_line == float(a), blend, both)
    place = iota((count, LANES), 1) + c_line.astype(jnp.int32)
    moved = lane_pick(both, jnp.clip(place, 0, LANES - 1))
    return jnp.where((place >= 0) & (place < LANES), moved, 0.0)


def shift_lines(meta, row, frames, t):
    return meta[row + t : row + t + 1], meta[row + frames + t : row + frames + t + 1]


def own_kernel(own, raw, tile, part, t_own, corr, extra, ext):
    frames, rows, _ = raw.shape
    slab = lax.axis_index("slab")
    is_last = slab == lax.axis_size("slab") - 1
    extra[...] = below_part(own[...], [raw[t, 0:16].astype(F32)[0:8] for t in range(frames)]).astype(BF16)
    meta = own[PK_META:PK_ALL].astype(F32)
    row = meta[META_ROW : META_ROW + 1]
    tiles = placed_tiles(own[0 : 2 * K], meta[META_COL : META_COL + 1])
    t_own[...] = tiles
    tile[...] = jnp.zeros((8, LANES), F32)
    part[...] = jnp.zeros((8, LANES), F32)
    write_tile(tile, 0, gram(tiles, tiles, as_column(row), row), (0, 2, 4, 5, 6, 7))
    y = iota((rows, LANES), 0)
    keep = (y >= RIM) & ((y < rows - RIM) | is_last)
    rel = (y + RIM).astype(F32) - row - (iota((rows, LANES), 1) // K).astype(F32)
    for t in range(frames):
        ext[0:16] = jnp.zeros((16, LANES), F32)
        ext[16 : 16 + rows] = raw[t].astype(F32)
        ext[16 + rows : 32 + rows] = jnp.zeros((16, LANES), F32)
        parts = []
        for p, row_of in ((0, META_FIRST), (1, META_SHIFT)):

            def rows_at(a, first=16 + p * PATCH_R):
                return ext[first + a : first + a + PATCH_R + 1]

            parts.append(warp(rows_at, PATCH_R, *shift_lines(meta, row_of, frames, t)))
        image = jnp.concatenate(parts, axis=0)
        corr[t] = image.astype(BF16)
        part[t : t + 1] = project(jnp.where(keep, image, 0.0).astype(BF16), tiles, rel)


def low_kernel(own, raw, by_pair, by_low, tiles, tail, lines, ext):
    frames, rows, _ = raw.shape
    low = from_below(
        lax.axis_index("slab"),
        lax.axis_size("slab"),
        received_below(by_pair[...], frames),
        by_low[...].astype(F32),
    )
    meta = own[PK_META:PK_ALL].astype(F32)
    meta_low = low[K + 8 * frames :]
    tiles[...] = placed_tiles(low[0:K], meta_low[META_COL : META_COL + 1])
    lines[...] = jnp.broadcast_to(meta_low[META_ROW : META_ROW + 1], (8, LANES))
    for t in range(frames):
        ext[0:16] = raw[t, rows - 16 : rows].astype(F32)
        ext[16:24] = low[K + 8 * t : K + 8 * t + 8]

        def rows_at(a):
            return ext[8 + a : 17 + a]

        tail[t] = warp(rows_at, RIM, *shift_lines(meta, META_SHIFT, frames, t))


def edge_kernel(own, raw, by_middle, by_pair, line, t_own, tile, part, out, t_up, top):
    frames, rows, _ = raw.shape
    up = from_above(lax.axis_index("slab"), by_pair[...], by_middle[...])
    meta_own = own[PK_META:PK_ALL].astype(F32)
    meta_up = up[PK_META:PK_ALL]
    row_own = meta_own[META_ROW : META_ROW + 1]
    row_up = meta_up[META_ROW : META_ROW + 1] - float(rows)
    tiles_own = t_own[...]
    tiles_up = placed_tiles(up[0 : 2 * K], meta_up[META_COL : META_COL + 1])
    t_up[...] = tiles_up
    out[0:8] = tile[...]
    source, frame, first_kind = gather_source()
    found = jnp.zeros((8, LANES), F32)
    shape = (2 * RIM, LANES)
    rel_own = iota(shape, 0).astype(F32) - row_own - (iota(shape, 1) // K).astype(F32)
    rel_up = iota(shape, 0).astype(F32) - row_up - (iota(shape, 1) // K).astype(F32)
    images = []
    for t in range(frames):
        at = PK_RAW + 16 * t
        near = jnp.concatenate([up[at : at + 16], raw[t, 0:16].astype(F32)], axis=0)
        zone = []
        for start, meta, row in ((8, meta_up, META_SHIFT), (16, meta_own, META_FIRST)):

            def rows_at(a, start=start):
                return near[start + a : start + a + RIM + 1]

            zone.append(warp(rows_at, RIM, *shift_lines(meta, row, frames, t)))
        images.append(jnp.concatenate(zone, axis=0).astype(BF16))
        top[t] = zone[1]
    images = jnp.concatenate(images, axis=0)
    half = TILE * K // 2
    left = dot_nt(jnp.concatenate([tiles_up[K:], images], axis=0), tiles_own[0:half])
    right = dot_nt(jnp.concatenate([tiles_up[9 * K :], images], axis=0), tiles_own[half:])
    write_tile(out, 8, gram_above(left, right, as_column(row_up), row_own), range(8))
    by_own = jnp.concatenate([left[15 * K :], right[7 * K :]], axis=1)
    by_up = dot_nt(images, tiles_up)
    for t in range(frames):
        at = 2 * RIM * t
        sums = (
            pick_rows(by_own[at : at + 2 * RIM], rel_own) + part[t : t + 1],
            pick_rows(by_up[at : at + 2 * RIM], rel_up),
        )
        both = [lane_pick(jnp.broadcast_to(x, (8, LANES)), source) for x in sums]
        found = jnp.where(frame == t, jnp.where(first_kind, both[0], both[1]), found)
    out[1:2] = found[0:1]
    out[3:4] = line[0:1]


def sweep_kernel(frames, slabs, gathered, out, sent, turned, g_ref):
    per = K // slabs
    lane = iota((8, LANES), 1)
    sub = iota((8, LANES), 0)
    quarter = lane // K
    slab = lane % slabs
    frame = (lane % K) // slabs
    me = lax.axis_index("slab")
    later = jnp.minimum(slab + 1, slabs - 1)
    here = gather_place(slab ^ me, slabs)
    there = gather_place(later ^ me, slabs)

    def turn(tile):
        arrays = []
        for n in range(2 // per):
            lines = []
            for lq in range(4):
                for h in range(per):
                    jh = n * per + h
                    lines.append(gathered[pl.ds(8 * tile + 2 * lq + jh, slabs, stride=16), :])
            at = (2 * tile + n) * LANES
            turned[at : at + LANES] = jnp.concatenate(lines, axis=0).T
            arrays.append(at)
        return (arrays * 2)[:2] if per == 2 else arrays

    def half_lane(jh):
        return jh * slabs if per == 2 else 0

    base_g = turn(0)
    base_x = turn(1)

    for jh in range(2):
        index = quarter * K + half_lane(jh) + here
        for j in range(16):
            n = 16 * jh + j
            rows = turned[base_x[jh] + 8 * j : base_x[jh] + 8 * j + 8]
            g_ref[8 * (K + n) : 8 * (K + n) + 8] = lane_pick(rows, index)
            rows = turned[base_g[jh] + 8 * j : base_g[jh] + 8 * j + 8]
            g_ref[8 * n : 8 * n + 8] = lane_pick(rows, index)
    for r in range(8):
        parts = [turned[pl.ds(base_g[0] + 64 * v + r, 8, stride=8), :] for v in range(2)]
        for oq in (2, 3):
            n = 8 * oq + r
            index = oq * K + half_lane(0) + here
            corner = jnp.where(quarter == 0, lane_pick(parts[0], index), lane_pick(parts[1], index))
            at = pl.ds(8 * n, 8)
            g_ref[at, :] = jnp.where(quarter < 2, corner, g_ref[at, :])
    inner = slab < slabs - 1
    for r in range(8):
        parts = [
            [turned[pl.ds(base_x[uh] + 64 * v + r, 8, stride=8), :] for v in range(2)]
            for uh in range(3 - per)
        ]
        if per == 2:
            even, odd = parts[0]
            merged = (
                jnp.where(quarter % 2 == 0, even, pltpu.roll(odd, K, 1)),
                jnp.where(quarter % 2 == 0, pltpu.roll(even, LANES - K, 1), odd),
            )
        for oq in range(4):
            if per == 2:
                index = (2 * (oq // 2) + quarter % 2) * K + (quarter // 2) * slabs + there
                value = lane_pick(merged[oq % 2], index)
            else:
                index = oq * K + there
                value = lane_pick(parts[0][0], index)
                for uq in range(1, 4):
                    value = jnp.where(quarter == uq, lane_pick(parts[uq // 2][uq % 2], index), value)
            n = 2 * K + 8 * oq + r
            g_ref[8 * n : 8 * n + 8] = jnp.where(inner, value, 0.0)

    lanes_of = half_lane(1)
    states = []
    for nv in range(frames // per):
        found = []
        for line, kind, shifted in ((0, 0, False), (0, 1, True), (1, 0, False), (1, 1, False)):
            index = line * K + lanes_of + (there if shifted else here)
            value = jnp.zeros((8, LANES), F32)
            for lq in range(4):
                for h in range(per):
                    n = 8 * kind + 2 * lq + nv * per + h
                    rows = turned[base_g[1] + 8 * n : base_g[1] + 8 * n + 8]
                    value = jnp.where((quarter == lq) & (frame == h), lane_pick(rows, index), value)
            found.append(jnp.where(inner, value, 0.0) if shifted else value)
        states.append(found)
    norm = jnp.zeros((8, LANES), F32)
    for n in range(K):
        mine = (sub == n % 8) & (quarter == n // 8)
        norm = jnp.where(mine, g_ref[8 * n : 8 * n + 8], norm)
    inverse = 1.0 / norm
    block_of = states[0][3]

    local = lane % K
    before = jnp.where(slab == 0, local, local - 1)
    after = jnp.where(inner, local + 1, local)

    def coupled(change):
        totals = [None] * 8
        picks = [[lane_pick(change, q * K + place) for q in range(4)] for place in (local, before, after)]
        for kind in range(3):
            for q in range(4):
                for r in range(8):
                    n = kind * K + 8 * q + r
                    term = g_ref[8 * n : 8 * n + 8] * jnp.broadcast_to(picks[kind][q][r : r + 1], (8, LANES))
                    totals[r] = term if totals[r] is None else totals[r] + term
        while len(totals) > 1:
            totals = [functools.reduce(jnp.add, totals[i : i + 2]) for i in range(0, len(totals), 2)]
        return totals[0]

    def step(n, carry):
        p, change, traces = carry
        p = [x - coupled(c) for x, c in zip(p, change)]
        scale = jnp.where(block_of == lax.rem(n, BLOCKS).astype(F32), inverse, 0.0)
        change = [x * scale for x in p]
        return p, change, [x + c for x, c in zip(traces, change)]

    first = [s[2] for s in states]
    start = ([s[0] + s[1] for s in states], first, first)
    _, _, traces = lax.fori_loop(0, SWEEPS * BLOCKS, step, start, unroll=12)

    mine = sub == lane % 8

    def lines_of(other):
        lines = []
        for t in range(frames):
            index = ((lane % K) // 8) * K + (t % per) * slabs + other
            value = jnp.where(mine, lane_pick(traces[t // per], index), 0.0)
            lines.append(jnp.sum(value, axis=0, keepdims=True))
        return lines

    def sums_of(lines):
        return [functools.reduce(jnp.add, lines), functools.reduce(jnp.add, [x * x for x in lines])]

    own = lines_of(me)
    lines = own + lines_of(jnp.maximum(me - 1, 0)) + lines_of(jnp.minimum(me + 1, slabs - 1))
    for n, line in enumerate(lines + sums_of(own)):
        out[n : n + 1] = line
    for n, line in enumerate(sums_of(lines_of(me ^ 1))):
        sent[n : n + 1] = line


def render(rel, values, tiles, groups=range(4)):
    mixed = jnp.concatenate([jnp.where(rel == float(4 * m), values, 0.0) for m in groups], axis=1)
    high = mixed.astype(BF16)
    low = (mixed - high.astype(F32)).astype(BF16)
    return jnp.dot(high, tiles, preferred_element_type=F32) + jnp.dot(
        low, tiles, preferred_element_type=F32
    )


def finish_kernel(own, by_middle, by_pair, corr, top, tail, lines, t_own, t_up, t_low, values, out):
    frames, rows, _ = corr.shape
    slab = lax.axis_index("slab")
    meta_up = from_above(slab, by_pair[PK_META:PK_ALL], by_middle[PK_META:PK_ALL])
    row_own = own[PK_META:PK_ALL].astype(F32)[META_ROW : META_ROW + 1]
    row_up = meta_up[META_ROW : META_ROW + 1] - float(rows)
    row_low = lines[0:1] + float(rows)
    y = (iota((rows, LANES), 0) + RIM).astype(F32)
    group = (iota((rows, LANES), 1) // K).astype(F32)
    rel_own = y - row_own - group
    rel_up = (y - row_up - group)[0:RIM]
    rel_low = (y - row_low - group)[rows - RIM : rows]
    half = t_low.shape[0]
    for t in range(frames):
        image = render(rel_own, values[t : t + 1], t_own[...])
        above = render(rel_up, values[frames + t : frames + t + 1], t_up[half:], (2, 3))
        below = render(rel_low, values[2 * frames + t : 2 * frames + t + 1], t_low[...], (0, 1))
        out[t, 0:RIM] = top[t].astype(BF16).astype(F32) - image[0:RIM] - above
        out[t, RIM : rows - RIM] = corr[t].astype(F32)[RIM : rows - RIM] - image[RIM : rows - RIM]
        out[t, rows - RIM : rows] = tail[t].astype(BF16).astype(F32) - image[rows - RIM : rows] - below


def score_kernel(frame_total, values, *rest):
    out = rest[-1]
    frames = out.shape[0]
    sums = values[3 * frames : 3 * frames + 2]
    for other in rest[:-1]:
        sums = sums + other[0:2]
    mean = sums[0:1] / frame_total
    spread = sums[1:2] / frame_total - mean * mean
    out[...] = ((values[0:frames] - mean) / jnp.sqrt(spread + EPSILON))[:, 0:K]


def local_call(kernel, out_shape, scratch_shapes, flops, args, space=pltpu.VMEM):
    args = [pltpu.with_memory_space_constraint(x, space) for x in args]
    return pl.pallas_call(
        kernel,
        out_shape=out_shape,
        in_specs=[pl.BlockSpec(memory_space=space)] * len(args),
        out_specs=jax.tree.map(lambda _: VMEM_SPEC, out_shape),
        scratch_shapes=scratch_shapes,
        compiler_params=pltpu.CompilerParams(vmem_limit_bytes=VMEM_BYTES),
        cost_estimate=pl.CostEstimate(flops=flops, bytes_accessed=1 << 18, transcendentals=0),
    )(*args)


def shards(raw_movie, shifts, footprints, anchors, block_of, init_traces):
    frames, rows, cols = raw_movie.shape
    slabs = lax.axis_size("slab")
    frame_parts = lax.axis_size("frames")
    small = pltpu.VMEM((8, LANES), F32)
    tiles = pltpu.VMEM((TILE * K, LANES), BF16)
    half_tiles = pltpu.VMEM((TILE * K // 2, LANES), BF16)
    image = pltpu.VMEM((frames, rows, LANES), BF16)
    rim = pltpu.VMEM((frames, RIM, LANES), F32)
    extra_rows = K + 8 * frames + 16

    given = (
        raw_movie,
        footprints.transpose(1, 2, 0),
        shifts.transpose(0, 1, 3, 2),
        anchors.T,
        init_traces.T,
        block_of[None],
    )
    pairs, downwards, upwards = neighbour_routes(slabs)
    sent_down = local_call(
        send_kernel,
        pltpu.VMEM((PK_ALL, LANES), BF16),
        [pltpu.VMEM(x.shape, x.dtype) for x in given[:4]] + [pltpu.SemaphoreType.DMA((4,))],
        10**8,
        given[:4],
        space=pltpu.HBM,
    )
    by_middle = lax.ppermute(sent_down, "slab", downwards)

    pack, pair, raw, line = local_call(
        pack_kernel,
        (pltpu.VMEM((PK_ALL, LANES), BF16), pltpu.VMEM((PK_ALL, LANES), BF16), image, small),
        [pltpu.VMEM(x.shape, x.dtype) for x in given[1:]] + [pltpu.SemaphoreType.DMA((len(given),))],
        10**8,
        given + (sent_down,),
        space=pltpu.HBM,
    )
    by_pair = lax.ppermute(pair, "slab", pairs)

    tile, part, t_own, corr, extra = local_call(
        own_kernel,
        (small, small, tiles, image, pltpu.VMEM((extra_rows, LANES), BF16)),
        [pltpu.VMEM((rows + 32, LANES), F32)],
        10**9,
        (pack, raw),
    )
    gathered, t_up, top = local_call(
        edge_kernel,
        (pltpu.VMEM((16, LANES), F32), tiles, rim),
        [],
        10**9,
        (pack, raw, by_middle, by_pair, line, t_own, tile, part),
    )
    block = gathered.shape[0]
    crossing = [(i, i ^ 3) for i in range(slabs)]
    early = []
    for n, mask in enumerate(gather_masks(slabs)):
        route = [(i, i ^ mask) for i in range(slabs)]
        if n == 0:
            extra, gathered = lax.optimization_barrier((extra, gathered))
        if mask == 3:
            rest = gathered[2 * block :]
            other = jnp.concatenate([*early, lax.ppermute(rest, "slab", route)], axis=0)
        else:
            other = lax.ppermute(gathered, "slab", route)
        if n == 0:
            by_low = lax.ppermute(extra, "slab", upwards)
        elif n == 1:
            early.append(lax.ppermute(gathered, "slab", crossing))
        gathered = jnp.concatenate([gathered, other], axis=0)

    t_low, tail, lines = local_call(
        low_kernel,
        (half_tiles, rim, small),
        [pltpu.VMEM((24, LANES), F32)],
        10**9,
        (pack, raw, by_pair, by_low),
    )
    values, sent = local_call(
        functools.partial(sweep_kernel, frames, slabs),
        (small, small),
        [pltpu.VMEM((4 * LANES, LANES), F32), pltpu.VMEM((8 * 3 * K, LANES), F32)],
        10**9,
        (gathered,),
    )

    others = []
    for hop in range(1, frame_parts):
        route = [
            (f * slabs + s, ((f + hop) % frame_parts) * slabs + (s ^ 1))
            for f in range(frame_parts)
            for s in range(slabs)
        ]
        others.append(lax.ppermute(sent, ("frames", "slab"), route))

    residual = local_call(
        finish_kernel,
        jax.ShapeDtypeStruct((frames, rows, LANES), F32),
        [],
        10**9,
        (pack, by_middle, by_pair, corr, top, tail, lines, t_own, t_up, t_low, values),
    )

    traces_z = local_call(
        functools.partial(score_kernel, frames * frame_parts),
        jax.ShapeDtypeStruct((frames, K), F32),
        [],
        10**4,
        (values, *others),
    )
    return traces_z.T, residual


def solution(mesh):
    in_specs = (
        P("frames", "slab", None),
        P(None, "frames", "slab", None),
        P("slab", None, None),
        P("slab", None),
        P("slab"),
        P("slab", "frames"),
    )
    out_specs = (P("slab", "frames"), P("frames", "slab", None))
    return jax.shard_map(shards, mesh=mesh, in_specs=in_specs, out_specs=out_specs, check_vma=False)
```

```python
import functools

import jax
import jax.numpy as jnp
from jax import lax
from jax.experimental import pallas as pl
from jax.experimental.pallas import tpu as pltpu
from jax.sharding import PartitionSpec as P

SHIFT = 3
PATCH_R = 32
BLOCKS = 4
SWEEPS = 3
TILE = 16
RIM = 8
LANES = 128
K = 32
GROUPS = LANES // K
WEIGHT_NEAR = 0.75
WEIGHT_FAR = 0.25
EPSILON = 1e-05
F32 = jnp.float32
BF16 = jnp.bfloat16

PK_RAW = 64
PK_META = 96
PK_ALL = 112
META_ROW = 0
META_COL = 1
META_SHIFT = 2
META_FIRST = 6
VMEM_BYTES = 8 << 20
VMEM_SPEC = pl.BlockSpec(memory_space=pltpu.VMEM)


def iota(shape, axis):
    return lax.broadcasted_iota(jnp.int32, shape, axis)


def lane_pick(values, index):
    return jnp.take_along_axis(values, index, axis=1, mode="promise_in_bounds")


def as_column(line):
    own = iota((K, LANES), 0) == iota((K, LANES), 1)
    return jnp.sum(jnp.where(own, line, 0.0), axis=1, keepdims=True)


def placed_tiles(tiles, col_line):
    col = as_column(col_line).astype(jnp.int32)
    offset = iota((K, LANES), 1) - col
    inside = (offset >= 0) & (offset < TILE)
    base = jnp.clip(offset, 0, TILE - 1)
    out = []
    for i in range(tiles.shape[0] // K * 8):
        half, part = divmod(i, 8)
        tile = tiles[half * K : (half + 1) * K].astype(F32)
        out.append(jnp.where(inside, lane_pick(tile, base + part * TILE), 0.0))
    return jnp.concatenate(out, axis=0).astype(BF16)


def dot_nt(a, b):
    return lax.dot_general(a, b, (((1,), (1,)), ((), ())), preferred_element_type=F32)


def fold_lanes(x):
    return (x + pltpu.roll(x, K, 1)) + (pltpu.roll(x, 2 * K, 1) + pltpu.roll(x, 3 * K, 1))


def masked_sum(block, diff, places):
    total = jnp.zeros((K, LANES), F32)
    for q in places:
        parts = [block(4 * m - q, m) for m in range(4) if 0 <= 4 * m - q < TILE]
        if parts:
            total = total + jnp.where(diff == float(q), functools.reduce(jnp.add, parts), 0.0)
    return fold_lanes(total)


def row_diff(row_a, row_b):
    return row_a - row_b - (iota((K, LANES), 1) // K).astype(F32)


def gram(tiles_a, tiles_b, row_a, row_b):
    full = dot_nt(tiles_a, tiles_b)

    def block(i, m):
        return full[i * K : (i + 1) * K, m * LANES : (m + 1) * LANES]

    return masked_sum(block, row_diff(row_a, row_b), range(-(TILE - 1), TILE))


def gram_above(left, right, row_a, row_b):
    def block(i, m):
        part, first = (left, 1) if m < 2 else (right, 9)
        lane = (m % 2) * LANES
        return part[(i - first) * K : (i - first + 1) * K, lane : lane + LANES]

    return masked_sum(block, row_diff(row_a, row_b), range(-(TILE - 1), 0))


def pick_rows(part, rel):
    total = jnp.zeros(rel.shape, F32)
    for m in range(4):
        total = total + jnp.where(rel == float(4 * m), part[:, m * LANES : (m + 1) * LANES], 0.0)
    return fold_lanes(jnp.sum(total, axis=0, keepdims=True))


def project(corr, tiles, rel):
    return pick_rows(dot_nt(corr, tiles), rel)


def neighbour_routes(slabs):
    pairs = [(i, i ^ 1) for i in range(slabs)]
    runs = [range(0, 3)] + [range(i, i + 4) for i in range(3, slabs - 5, 4)] + [range(slabs - 5, slabs)]
    downwards = [(run[n], run[(n + 1) % len(run)]) for run in runs for n in range(len(run))]
    middle = [p for i in range(3, slabs - 4, 2) for p in ((i, i + 1), (i + 1, i))]
    ends = [(2, 1), (1, 0), (0, 2), (slabs - 2, slabs - 3), (slabs - 3, slabs - 1), (slabs - 1, slabs - 2)]
    return pairs, downwards, ends + middle


def from_above(slab, by_pair, by_middle):
    found = jnp.where(slab % 2 == 1, by_pair.astype(F32), by_middle.astype(F32))
    return jnp.where(slab == 0, 0.0, found)


def below_part(pack, firsts):
    return jnp.concatenate([pack[0:K].astype(F32), *firsts, pack[PK_META:PK_ALL].astype(F32)], axis=0)


def received_below(pack, frames):
    firsts = [pack[PK_RAW + 16 * t : PK_RAW + 16 * t + 16].astype(F32)[0:8] for t in range(frames)]
    return below_part(pack, firsts)


def write_edge_rows(out, raw, to_below):
    frames, rows, _ = raw.shape
    for t in range(frames):
        last, first = raw[t, rows - 16 : rows].astype(F32), raw[t, 0:16].astype(F32)
        out[PK_RAW + 16 * t : PK_RAW + 16 * t + 16] = jnp.where(to_below, last, first).astype(BF16)


def from_below(slab, slabs, by_pair, by_low):
    found = jnp.where(slab % 2 == 0, by_pair, by_low)
    return jnp.where(slab == slabs - 1, 0.0, found)


def gather_masks(slabs):
    bits = slabs.bit_length() - 1
    return [(1 << b) | 1 for b in range(bits - 1, 0, -1)] + [1]


def gather_place(diff, slabs):
    bits = slabs.bit_length() - 1
    odd = diff & 1
    place = jnp.zeros_like(diff)
    for r in range(bits - 1):
        bit = (diff >> (bits - 1 - r)) & 1
        place = place + bit * (1 << r)
        odd = odd ^ bit
    return place + odd * (1 << (bits - 1))


def gather_source():
    place = iota((8, LANES), 1)
    return 8 * ((place // 16) % 4) + place % 8, (place // 8) % 2, place < LANES // 2


def meta_lines(shifts, anchors, frames, last, base):
    places = jnp.concatenate([anchors[...].astype(F32)] * GROUPS, axis=1)
    sub = iota((16, LANES), 0)
    meta = jnp.where(sub == META_COL, places[1:2], 0.0)
    meta = jnp.where(sub == META_ROW, places[0:1] - base.astype(F32), meta)
    for t in range(frames):
        for axis in range(2):
            moves = shifts[axis, t].astype(F32)
            for place, patch in ((META_SHIFT, last), (META_FIRST, 0)):
                meta = jnp.where(sub == place + axis * frames + t, moves[:, patch : patch + 1], meta)
    return meta.astype(BF16)


def turned_tiles(tiles, half):
    return tiles[8 * half : 8 * half + 8].astype(F32).reshape(LANES, K).T.astype(BF16)


def send_kernel(raw_in, tiles_in, shifts_in, anchors_in, out, raw, tiles, shifts, anchors, sems):
    frames, rows, _ = raw.shape
    slab = lax.axis_index("slab")

    @pl.when(slab % 2 == 0)
    def _():
        out[...] = jnp.zeros((PK_ALL, LANES), BF16)

    @pl.when(slab % 2 == 1)
    def _():
        pairs = ((raw_in, raw), (tiles_in, tiles), (shifts_in, shifts), (anchors_in, anchors))
        copies = [pltpu.make_async_copy(*pair, sems.at[n]) for n, pair in enumerate(pairs)]
        for copy in copies:
            copy.start()
        copies[2].wait()
        copies[3].wait()
        out[PK_META:PK_ALL] = meta_lines(shifts, anchors, frames, rows // PATCH_R - 1, slab * rows - RIM)
        copies[0].wait()
        write_edge_rows(out, raw, True)
        copies[1].wait()
        for half in range(2):
            out[K * half : K * half + K] = turned_tiles(tiles, half)


def pack_kernel(*refs):
    count = 6
    given, (out, pair, raw, line) = refs[:count], refs[count + 1 : count + 5]
    held = refs[count + 5 : 2 * count + 4]
    sems = refs[-1]
    tiles, shifts, anchors, init, block_of = held
    copies = [
        pltpu.make_async_copy(source, target, sems.at[n])
        for n, (source, target) in enumerate(zip(given, (raw, *held)))
    ]
    for copy in copies:
        copy.start()
    raw_copy, tiles_copy, *small_copies = copies
    frames, rows, _ = raw.shape
    slab = lax.axis_index("slab")
    for copy in small_copies:
        copy.wait()
    meta = meta_lines(shifts, anchors, frames, rows // PATCH_R - 1, slab * rows - RIM)
    out[PK_META:PK_ALL] = meta
    pair[PK_META:PK_ALL] = meta
    source, frame, first_kind = gather_source()
    inits = jnp.concatenate([init[...]] * GROUPS, axis=1)
    blocks = jnp.concatenate([block_of[...].astype(F32)] * GROUPS, axis=1)
    found = jnp.zeros((8, LANES), F32)
    for t in range(frames):
        both = [lane_pick(jnp.broadcast_to(x, (8, LANES)), source) for x in (inits[t : t + 1], blocks)]
        found = jnp.where(frame == t, jnp.where(first_kind, both[0], both[1]), found)
    line[...] = found
    raw_copy.wait()
    write_edge_rows(out, raw, slab % 2 == 1)
    write_edge_rows(pair, raw, slab % 2 == 0)
    tiles_copy.wait()
    for half in range(2):
        part = turned_tiles(tiles, half)
        out[K * half : K * half + K] = part
        pair[K * half : K * half + K] = part


def write_tile(out, first, mat, rows):
    lane = iota((K, LANES), 1)
    own = lane // 8 == iota((K, LANES), 0) % 16
    for lq in range(4):
        part = jnp.where(own, lane_pick(mat, 8 * lq + lane % 8), 0.0)
        for jh in range(2):
            if 2 * lq + jh in rows:
                out[first + 2 * lq + jh : first + 2 * lq + jh + 1] = jnp.sum(
                    part[16 * jh : 16 * jh + 16], axis=0, keepdims=True
                )


def warp(rows_at, count, a_line, c_line):
    both = jnp.zeros((count, LANES), F32)
    for a in range(-SHIFT, SHIFT + 1):
        window = rows_at(a)
        blend = WEIGHT_NEAR * window[0:count] + WEIGHT_FAR * window[1 : count + 1]
        both = jnp.where(a_line == float(a), blend, both)
    place = iota((count, LANES), 1) + c_line.astype(jnp.int32)
    moved = lane_pick(both, jnp.clip(place, 0, LANES - 1))
    return jnp.where((place >= 0) & (place < LANES), moved, 0.0)


def shift_lines(meta, row, frames, t):
    return meta[row + t : row + t + 1], meta[row + frames + t : row + frames + t + 1]


def own_kernel(own, raw, tile, part, t_own, corr, extra, ext):
    frames, rows, _ = raw.shape
    slab = lax.axis_index("slab")
    is_last = slab == lax.axis_size("slab") - 1
    extra[...] = below_part(own[...], [raw[t, 0:16].astype(F32)[0:8] for t in range(frames)]).astype(BF16)
    meta = own[PK_META:PK_ALL].astype(F32)
    row = meta[META_ROW : META_ROW + 1]
    tiles = placed_tiles(own[0 : 2 * K], meta[META_COL : META_COL + 1])
    t_own[...] = tiles
    tile[...] = jnp.zeros((8, LANES), F32)
    part[...] = jnp.zeros((8, LANES), F32)
    write_tile(tile, 0, gram(tiles, tiles, as_column(row), row), (0, 2, 4, 5, 6, 7))
    y = iota((rows, LANES), 0)
    keep = (y >= RIM) & ((y < rows - RIM) | is_last)
    rel = (y + RIM).astype(F32) - row - (iota((rows, LANES), 1) // K).astype(F32)
    for t in range(frames):
        ext[0:16] = jnp.zeros((16, LANES), F32)
        ext[16 : 16 + rows] = raw[t].astype(F32)
        ext[16 + rows : 32 + rows] = jnp.zeros((16, LANES), F32)
        parts = []
        for p, row_of in ((0, META_FIRST), (1, META_SHIFT)):

            def rows_at(a, first=16 + p * PATCH_R):
                return ext[first + a : first + a + PATCH_R + 1]

            parts.append(warp(rows_at, PATCH_R, *shift_lines(meta, row_of, frames, t)))
        image = jnp.concatenate(parts, axis=0)
        corr[t] = image.astype(BF16)
        part[t : t + 1] = project(jnp.where(keep, image, 0.0).astype(BF16), tiles, rel)


def low_kernel(own, raw, by_pair, by_low, tiles, tail, lines, ext):
    frames, rows, _ = raw.shape
    low = from_below(
        lax.axis_index("slab"),
        lax.axis_size("slab"),
        received_below(by_pair[...], frames),
        by_low[...].astype(F32),
    )
    meta = own[PK_META:PK_ALL].astype(F32)
    meta_low = low[K + 8 * frames :]
    tiles[...] = placed_tiles(low[0:K], meta_low[META_COL : META_COL + 1])
    lines[...] = jnp.broadcast_to(meta_low[META_ROW : META_ROW + 1], (8, LANES))
    for t in range(frames):
        ext[0:16] = raw[t, rows - 16 : rows].astype(F32)
        ext[16:24] = low[K + 8 * t : K + 8 * t + 8]

        def rows_at(a):
            return ext[8 + a : 17 + a]

        tail[t] = warp(rows_at, RIM, *shift_lines(meta, META_SHIFT, frames, t))


def edge_kernel(own, raw, by_middle, by_pair, line, t_own, tile, part, out, t_up, top):
    frames, rows, _ = raw.shape
    up = from_above(lax.axis_index("slab"), by_pair[...], by_middle[...])
    meta_own = own[PK_META:PK_ALL].astype(F32)
    meta_up = up[PK_META:PK_ALL]
    row_own = meta_own[META_ROW : META_ROW + 1]
    row_up = meta_up[META_ROW : META_ROW + 1] - float(rows)
    tiles_own = t_own[...]
    tiles_up = placed_tiles(up[0 : 2 * K], meta_up[META_COL : META_COL + 1])
    t_up[...] = tiles_up
    out[0:8] = tile[...]
    source, frame, first_kind = gather_source()
    found = jnp.zeros((8, LANES), F32)
    shape = (2 * RIM, LANES)
    rel_own = iota(shape, 0).astype(F32) - row_own - (iota(shape, 1) // K).astype(F32)
    rel_up = iota(shape, 0).astype(F32) - row_up - (iota(shape, 1) // K).astype(F32)
    images = []
    for t in range(frames):
        at = PK_RAW + 16 * t
        near = jnp.concatenate([up[at : at + 16], raw[t, 0:16].astype(F32)], axis=0)
        zone = []
        for start, meta, row in ((8, meta_up, META_SHIFT), (16, meta_own, META_FIRST)):

            def rows_at(a, start=start):
                return near[start + a : start + a + RIM + 1]

            zone.append(warp(rows_at, RIM, *shift_lines(meta, row, frames, t)))
        images.append(jnp.concatenate(zone, axis=0).astype(BF16))
        top[t] = zone[1]
    images = jnp.concatenate(images, axis=0)
    half = TILE * K // 2
    left = dot_nt(jnp.concatenate([tiles_up[K:], images], axis=0), tiles_own[0:half])
    right = dot_nt(jnp.concatenate([tiles_up[9 * K :], images], axis=0), tiles_own[half:])
    write_tile(out, 8, gram_above(left, right, as_column(row_up), row_own), range(8))
    by_own = jnp.concatenate([left[15 * K :], right[7 * K :]], axis=1)
    by_up = dot_nt(images, tiles_up)
    for t in range(frames):
        at = 2 * RIM * t
        sums = (
            pick_rows(by_own[at : at + 2 * RIM], rel_own) + part[t : t + 1],
            pick_rows(by_up[at : at + 2 * RIM], rel_up),
        )
        both = [lane_pick(jnp.broadcast_to(x, (8, LANES)), source) for x in sums]
        found = jnp.where(frame == t, jnp.where(first_kind, both[0], both[1]), found)
    out[1:2] = found[0:1]
    out[3:4] = line[0:1]


def sweep_kernel(frames, slabs, gathered, out, sent, turned, g_ref):
    per = K // slabs
    lane = iota((8, LANES), 1)
    sub = iota((8, LANES), 0)
    quarter = lane // K
    slab = lane % slabs
    frame = (lane % K) // slabs
    me = lax.axis_index("slab")
    later = jnp.minimum(slab + 1, slabs - 1)
    here = gather_place(slab ^ me, slabs)
    there = gather_place(later ^ me, slabs)

    def turn(tile):
        arrays = []
        for n in range(2 // per):
            lines = []
            for lq in range(4):
                for h in range(per):
                    jh = n * per + h
                    lines.append(gathered[pl.ds(8 * tile + 2 * lq + jh, slabs, stride=16), :])
            at = (2 * tile + n) * LANES
            turned[at : at + LANES] = jnp.concatenate(lines, axis=0).T
            arrays.append(at)
        return (arrays * 2)[:2] if per == 2 else arrays

    def half_lane(jh):
        return jh * slabs if per == 2 else 0

    base_g = turn(0)
    base_x = turn(1)

    for jh in range(2):
        index = quarter * K + half_lane(jh) + here
        for j in range(16):
            n = 16 * jh + j
            rows = turned[base_x[jh] + 8 * j : base_x[jh] + 8 * j + 8]
            g_ref[8 * (K + n) : 8 * (K + n) + 8] = lane_pick(rows, index)
            rows = turned[base_g[jh] + 8 * j : base_g[jh] + 8 * j + 8]
            g_ref[8 * n : 8 * n + 8] = lane_pick(rows, index)
    for r in range(8):
        parts = [turned[pl.ds(base_g[0] + 64 * v + r, 8, stride=8), :] for v in range(2)]
        for oq in (2, 3):
            n = 8 * oq + r
            index = oq * K + half_lane(0) + here
            corner = jnp.where(quarter == 0, lane_pick(parts[0], index), lane_pick(parts[1], index))
            at = pl.ds(8 * n, 8)
            g_ref[at, :] = jnp.where(quarter < 2, corner, g_ref[at, :])
    inner = slab < slabs - 1
    for r in range(8):
        parts = [
            [turned[pl.ds(base_x[uh] + 64 * v + r, 8, stride=8), :] for v in range(2)]
            for uh in range(3 - per)
        ]
        if per == 2:
            even, odd = parts[0]
            merged = (
                jnp.where(quarter % 2 == 0, even, pltpu.roll(odd, K, 1)),
                jnp.where(quarter % 2 == 0, pltpu.roll(even, LANES - K, 1), odd),
            )
        for oq in range(4):
            if per == 2:
                index = (2 * (oq // 2) + quarter % 2) * K + (quarter // 2) * slabs + there
                value = lane_pick(merged[oq % 2], index)
            else:
                index = oq * K + there
                value = lane_pick(parts[0][0], index)
                for uq in range(1, 4):
                    value = jnp.where(quarter == uq, lane_pick(parts[uq // 2][uq % 2], index), value)
            n = 2 * K + 8 * oq + r
            g_ref[8 * n : 8 * n + 8] = jnp.where(inner, value, 0.0)

    lanes_of = half_lane(1)
    states = []
    for nv in range(frames // per):
        found = []
        for line, kind, shifted in ((0, 0, False), (0, 1, True), (1, 0, False), (1, 1, False)):
            index = line * K + lanes_of + (there if shifted else here)
            value = jnp.zeros((8, LANES), F32)
            for lq in range(4):
                for h in range(per):
                    n = 8 * kind + 2 * lq + nv * per + h
                    rows = turned[base_g[1] + 8 * n : base_g[1] + 8 * n + 8]
                    value = jnp.where((quarter == lq) & (frame == h), lane_pick(rows, index), value)
            found.append(jnp.where(inner, value, 0.0) if shifted else value)
        states.append(found)
    norm = jnp.zeros((8, LANES), F32)
    for n in range(K):
        mine = (sub == n % 8) & (quarter == n // 8)
        norm = jnp.where(mine, g_ref[8 * n : 8 * n + 8], norm)
    inverse = 1.0 / norm
    block_of = states[0][3]

    local = lane % K
    before = jnp.where(slab == 0, local, local - 1)
    after = jnp.where(inner, local + 1, local)

    def coupled(change):
        totals = [None] * 8
        picks = [[lane_pick(change, q * K + place) for q in range(4)] for place in (local, before, after)]
        for kind in range(3):
            for q in range(4):
                for r in range(8):
                    n = kind * K + 8 * q + r
                    term = g_ref[8 * n : 8 * n + 8] * jnp.broadcast_to(picks[kind][q][r : r + 1], (8, LANES))
                    totals[r] = term if totals[r] is None else totals[r] + term
        while len(totals) > 1:
            totals = [functools.reduce(jnp.add, totals[i : i + 2]) for i in range(0, len(totals), 2)]
        return totals[0]

    def step(n, carry):
        p, change, traces = carry
        p = [x - coupled(c) for x, c in zip(p, change)]
        scale = jnp.where(block_of == lax.rem(n, BLOCKS).astype(F32), inverse, 0.0)
        change = [x * scale for x in p]
        return p, change, [x + c for x, c in zip(traces, change)]

    first = [s[2] for s in states]
    start = ([s[0] + s[1] for s in states], first, first)
    _, _, traces = lax.fori_loop(0, SWEEPS * BLOCKS, step, start, unroll=12)

    mine = sub == lane % 8

    def lines_of(other):
        lines = []
        for t in range(frames):
            index = ((lane % K) // 8) * K + (t % per) * slabs + other
            value = jnp.where(mine, lane_pick(traces[t // per], index), 0.0)
            lines.append(jnp.sum(value, axis=0, keepdims=True))
        return lines

    def sums_of(lines):
        return [functools.reduce(jnp.add, lines), functools.reduce(jnp.add, [x * x for x in lines])]

    own = lines_of(me)
    lines = own + lines_of(jnp.maximum(me - 1, 0)) + lines_of(jnp.minimum(me + 1, slabs - 1))
    for n, line in enumerate(lines + sums_of(own)):
        out[n : n + 1] = line
    for n, line in enumerate(sums_of(lines_of(me ^ 1))):
        sent[n : n + 1] = line


def render(rel, values, tiles, groups=range(4)):
    mixed = jnp.concatenate([jnp.where(rel == float(4 * m), values, 0.0) for m in groups], axis=1)
    high = mixed.astype(BF16)
    low = (mixed - high.astype(F32)).astype(BF16)
    return jnp.dot(high, tiles, preferred_element_type=F32) + jnp.dot(
        low, tiles, preferred_element_type=F32
    )


def finish_kernel(own, by_middle, by_pair, corr, top, tail, lines, t_own, t_up, t_low, values, out):
    frames, rows, _ = corr.shape
    slab = lax.axis_index("slab")
    meta_up = from_above(slab, by_pair[PK_META:PK_ALL], by_middle[PK_META:PK_ALL])
    row_own = own[PK_META:PK_ALL].astype(F32)[META_ROW : META_ROW + 1]
    row_up = meta_up[META_ROW : META_ROW + 1] - float(rows)
    row_low = lines[0:1] + float(rows)
    y = (iota((rows, LANES), 0) + RIM).astype(F32)
    group = (iota((rows, LANES), 1) // K).astype(F32)
    rel_own = y - row_own - group
    rel_up = (y - row_up - group)[0:RIM]
    rel_low = (y - row_low - group)[rows - RIM : rows]
    half = t_low.shape[0]
    for t in range(frames):
        image = render(rel_own, values[t : t + 1], t_own[...])
        above = render(rel_up, values[frames + t : frames + t + 1], t_up[half:], (2, 3))
        below = render(rel_low, values[2 * frames + t : 2 * frames + t + 1], t_low[...], (0, 1))
        out[t, 0:RIM] = top[t].astype(BF16).astype(F32) - image[0:RIM] - above
        out[t, RIM : rows - RIM] = corr[t].astype(F32)[RIM : rows - RIM] - image[RIM : rows - RIM]
        out[t, rows - RIM : rows] = tail[t].astype(BF16).astype(F32) - image[rows - RIM : rows] - below


def score_kernel(frame_total, values, *rest):
    out = rest[-1]
    frames = out.shape[0]
    sums = values[3 * frames : 3 * frames + 2]
    for other in rest[:-1]:
        sums = sums + other[0:2]
    mean = sums[0:1] / frame_total
    spread = sums[1:2] / frame_total - mean * mean
    out[...] = ((values[0:frames] - mean) / jnp.sqrt(spread + EPSILON))[:, 0:K]


def local_call(kernel, out_shape, scratch_shapes, flops, args, space=pltpu.VMEM):
    args = [pltpu.with_memory_space_constraint(x, space) for x in args]
    return pl.pallas_call(
        kernel,
        out_shape=out_shape,
        in_specs=[pl.BlockSpec(memory_space=space)] * len(args),
        out_specs=jax.tree.map(lambda _: VMEM_SPEC, out_shape),
        scratch_shapes=scratch_shapes,
        compiler_params=pltpu.CompilerParams(vmem_limit_bytes=VMEM_BYTES),
        cost_estimate=pl.CostEstimate(flops=flops, bytes_accessed=1 << 18, transcendentals=0),
    )(*args)


def shards(raw_movie, shifts, footprints, anchors, block_of, init_traces):
    frames, rows, cols = raw_movie.shape
    slabs = lax.axis_size("slab")
    frame_parts = lax.axis_size("frames")
    small = pltpu.VMEM((8, LANES), F32)
    tiles = pltpu.VMEM((TILE * K, LANES), BF16)
    half_tiles = pltpu.VMEM((TILE * K // 2, LANES), BF16)
    image = pltpu.VMEM((frames, rows, LANES), BF16)
    rim = pltpu.VMEM((frames, RIM, LANES), F32)
    extra_rows = K + 8 * frames + 16

    given = (
        raw_movie,
        footprints.transpose(1, 2, 0),
        shifts.transpose(0, 1, 3, 2),
        anchors.T,
        init_traces.T,
        block_of[None],
    )
    pairs, downwards, upwards = neighbour_routes(slabs)
    sent_down = local_call(
        send_kernel,
        pltpu.VMEM((PK_ALL, LANES), BF16),
        [pltpu.VMEM(x.shape, x.dtype) for x in given[:4]] + [pltpu.SemaphoreType.DMA((4,))],
        10**8,
        given[:4],
        space=pltpu.HBM,
    )
    by_middle = lax.ppermute(sent_down, "slab", downwards)

    pack, pair, raw, line = local_call(
        pack_kernel,
        (pltpu.VMEM((PK_ALL, LANES), BF16), pltpu.VMEM((PK_ALL, LANES), BF16), image, small),
        [pltpu.VMEM(x.shape, x.dtype) for x in given[1:]] + [pltpu.SemaphoreType.DMA((len(given),))],
        10**8,
        given + (sent_down,),
        space=pltpu.HBM,
    )
    by_pair = lax.ppermute(pair, "slab", pairs)

    tile, part, t_own, corr, extra = local_call(
        own_kernel,
        (small, small, tiles, image, pltpu.VMEM((extra_rows, LANES), BF16)),
        [pltpu.VMEM((rows + 32, LANES), F32)],
        10**9,
        (pack, raw),
    )
    gathered, t_up, top = local_call(
        edge_kernel,
        (pltpu.VMEM((16, LANES), F32), tiles, rim),
        [],
        10**9,
        (pack, raw, by_middle, by_pair, line, t_own, tile, part),
    )
    extra, gathered = lax.optimization_barrier((extra, gathered))
    for n, mask in enumerate(gather_masks(slabs)):
        other = lax.ppermute(gathered, "slab", [(i, i ^ mask) for i in range(slabs)])
        if n == 0:
            by_low = lax.ppermute(extra, "slab", upwards)
        gathered = jnp.concatenate([gathered, other], axis=0)

    t_low, tail, lines = local_call(
        low_kernel,
        (half_tiles, rim, small),
        [pltpu.VMEM((24, LANES), F32)],
        10**9,
        (pack, raw, by_pair, by_low),
    )
    values, sent = local_call(
        functools.partial(sweep_kernel, frames, slabs),
        (small, small),
        [pltpu.VMEM((4 * LANES, LANES), F32), pltpu.VMEM((8 * 3 * K, LANES), F32)],
        10**9,
        (gathered,),
    )

    others = []
    for hop in range(1, frame_parts):
        route = [
            (f * slabs + s, ((f + hop) % frame_parts) * slabs + (s ^ 1))
            for f in range(frame_parts)
            for s in range(slabs)
        ]
        others.append(lax.ppermute(sent, ("frames", "slab"), route))

    residual = local_call(
        finish_kernel,
        jax.ShapeDtypeStruct((frames, rows, LANES), F32),
        [],
        10**9,
        (pack, by_middle, by_pair, corr, top, tail, lines, t_own, t_up, t_low, values),
    )

    traces_z = local_call(
        functools.partial(score_kernel, frames * frame_parts),
        jax.ShapeDtypeStruct((frames, K), F32),
        [],
        10**4,
        (values, *others),
    )
    return traces_z.T, residual


def solution(mesh):
    in_specs = (
        P("frames", "slab", None),
        P(None, "frames", "slab", None),
        P("slab", None, None),
        P("slab", None),
        P("slab"),
        P("slab", "frames"),
    )
    out_specs = (P("slab", "frames"), P("frames", "slab", None))
    return jax.shard_map(shards, mesh=mesh, in_specs=in_specs, out_specs=out_specs, check_vma=False)
```
